32 devices in a mesh: dp: 8 (over z, y), expert: 4 (over x, core).
Axes of the slice: x: 2, y: 2, z: 4, core: 2. Of those that a mesh axis runs over, the one named last changes fastest.
Arguments:
- tokens: bfloat16 [1024, 7168], P('dp', 'expert'), may hold values from -6 to 6
- cotangent: bfloat16 [1024, 7168], P('dp', 'expert'), may hold values from -6 to 6
- gates: bfloat16 [1024, 2], P('dp'), may hold values from 0.19921875 to 2.5
- expert_ids: int32 [1024, 2], P('dp'), may hold values from 0 to 8, as said below
- w_gate: bfloat16 [8, 7168, 2048], P('dp', None, 'expert'), may hold values from -0.0625 to 0.0625
- w_up: bfloat16 [8, 7168, 2048], P('dp', None, 'expert'), may hold values from -0.0625 to 0.0625
- w_down: bfloat16 [8, 2048, 7168], P('dp', 'expert'), may hold values from -0.125 to 0.125
Outputs:
- grad_tokens: bfloat16 [1024, 7168], P('dp', 'expert')
- gate_grads: float32 [1024, 2], P('dp')
- grad_gate: bfloat16 [8, 7168, 2048], P('dp', None, 'expert')
- grad_up: bfloat16 [8, 7168, 2048], P('dp', None, 'expert')
- grad_down: bfloat16 [8, 2048, 7168], P('dp', 'expert')
The draws below stay inside these ranges and needn't reach their ends.
Inputs may be any that keep to these rules, and one draw needn't show every extreme that they name: `expert_ids`: column 0 names one of the experts 0 to half of 8 minus 1 and column 1 one of the others, or the value 8 for a choice outside this window. The 128 tokens of one index of dp route at most 8 tokens to one expert; in each column one expert, the same for every index of dp, receives exactly 8 tokens from every index of dp.
All inputs are finite; a program needn't handle non-finite values.
Results may differ from the reference program's by a relative error of at most 0.024.
Values may be sent and summed in bfloat16 or wider, within the bound.
No kernel may reach another device: no remote copies, remote signals or barrier semaphores. Data moves between devices by JAX's collectives and lax.ppermute only.
A program may use at most 128 MiB of HBM per device.

```python
import jax
import jax.numpy as jnp
from jax import lax

D = 7168
H = 2048
TOK_DEV = 128
ROUTES = 2
HID_DEV = 512
CAP = 8
EXPERTS = 8
TOKENS = 1024
N_DP = 8


def draw_expert_ids(key, part):
    key = jax.random.fold_in(key, 11)
    half = EXPERTS // 2
    blocks = TOKENS // TOK_DEV
    hot_key, count_key, perm_key = jax.random.split(key, 3)
    hot = jax.random.randint(hot_key, (2,), 0, half)
    counts = jax.random.randint(count_key, (blocks, 2, half), 0, 2 * CAP // 3 + 1)
    local = jnp.arange(half, dtype=jnp.int32)
    counts = jnp.where(local[None, None, :] == hot[None, :, None], CAP, counts)
    ends = jnp.cumsum(counts, axis=2)
    perm_keys = jax.random.split(perm_key, blocks * 2)
    orders = jax.vmap(lambda single: jax.random.permutation(single, TOK_DEV))(perm_keys)
    ranks = jnp.argsort(orders, axis=1, stable=True).reshape(blocks, 2, TOK_DEV)
    label = jnp.sum((ranks[:, :, :, None] >= ends[:, :, None, :]).astype(jnp.int32), axis=3)
    column = jnp.arange(2, dtype=jnp.int32)[None, :, None]
    ids = jnp.where(label < half, label + column * half, EXPERTS)
    return jnp.transpose(ids, (0, 2, 1)).reshape(TOKENS, 2).astype(jnp.int32)


def block_scale(stream_key, shape, cuts, low, largest):
    loudness = 1.0
    for position, shards_of in cuts:
        steps = jax.random.uniform(jax.random.fold_in(jax.random.fold_in(stream_key, 6), position), (shards_of,), jnp.float32, low / len(cuts), largest / len(cuts))
        loudness = loudness * jnp.repeat(jnp.exp(steps), shape[position] // shards_of).reshape((-1,) + (1,) * (len(shape) - 1 - position))
    return loudness


def gaussian(key, extent, spread, limit, shards=(), kind=jnp.bfloat16):
    entries = spread * jax.random.normal(key, extent, jnp.float32)
    if shards:
        entries = entries * block_scale(key, extent, shards, -0.22, 0.18)
    return jnp.clip(entries, -limit, limit).astype(kind)


def setup_inputs(seed: int = 0) -> dict:
    arg_keys = jax.random.split(jax.random.key(seed), 8)
    tokens = gaussian(arg_keys[0], (TOKENS, D), 1.0, 6.0, ((0, 8), (1, 4)))
    cotangent = gaussian(arg_keys[1], (TOKENS, D), 1.0, 6.0, ((0, 8), (1, 4)))
    gates = jnp.clip(0.19921875 + 2.3007812 * jax.random.uniform(arg_keys[2], (TOKENS, ROUTES), jnp.float32) ** block_scale(arg_keys[2], (TOKENS, ROUTES), ((0, 8),), -0.2, 0.2), 0.19921875, 2.5).astype(jnp.bfloat16)
    expert_ids = draw_expert_ids(jax.random.fold_in(arg_keys[7], 71), 0)
    w_gate = gaussian(arg_keys[4], (EXPERTS, D, H), D ** -0.5, 0.0625, ((0, 8), (2, 4)))
    w_up = gaussian(arg_keys[5], (EXPERTS, D, H), D ** -0.5, 0.0625, ((0, 8), (2, 4)))
    w_down = gaussian(arg_keys[6], (EXPERTS, H, D), H ** -0.5, 0.125, ((0, 8), (1, 4)))
    return dict(tokens=tokens, cotangent=cotangent, gates=gates, expert_ids=expert_ids, w_gate=w_gate, w_up=w_up, w_down=w_down)


def slot_grads(x_rows, d_rows, g_rows, gate_m, up_m, down_m):
    pre_gate = jnp.dot(x_rows, gate_m, preferred_element_type=jnp.float32)
    pre_up = jnp.dot(x_rows, up_m, preferred_element_type=jnp.float32)
    sig = jax.nn.sigmoid(pre_gate)
    act = pre_gate * sig
    hidden = (act * pre_up).astype(jnp.bfloat16)
    back = lax.dot_general(d_rows, down_m, (((1,), (1,)), ((), ())), preferred_element_type=jnp.float32)
    gate_terms = jnp.sum(back * hidden.astype(jnp.float32), axis=1)
    dhid = g_rows[:, None] * back
    scaled = (g_rows[:, None] * d_rows.astype(jnp.float32)).astype(jnp.bfloat16)
    grad_down = lax.dot_general(hidden, scaled, (((0,), (0,)), ((), ())), preferred_element_type=jnp.float32).astype(jnp.bfloat16)
    d_gate = (dhid * pre_up * sig * (1.0 + pre_gate * (1.0 - sig))).astype(jnp.bfloat16)
    d_up = (dhid * act).astype(jnp.bfloat16)
    grad_gate = lax.dot_general(x_rows, d_gate, (((0,), (0,)), ((), ())), preferred_element_type=jnp.float32).astype(jnp.bfloat16)
    grad_up = lax.dot_general(x_rows, d_up, (((0,), (0,)), ((), ())), preferred_element_type=jnp.float32).astype(jnp.bfloat16)
    blocks = H // HID_DEV
    rows = x_rows.shape[0]
    dg_blocks = d_gate.astype(jnp.float32).reshape(rows, blocks, HID_DEV)
    du_blocks = d_up.astype(jnp.float32).reshape(rows, blocks, HID_DEV)
    gm_blocks = gate_m.astype(jnp.float32).reshape(gate_m.shape[0], blocks, HID_DEV)
    um_blocks = up_m.astype(jnp.float32).reshape(up_m.shape[0], blocks, HID_DEV)
    partial_rows = jnp.einsum("sbh,dbh->bsd", dg_blocks, gm_blocks) + jnp.einsum("sbh,dbh->bsd", du_blocks, um_blocks)
    row_grads = jnp.sum(partial_rows.astype(jnp.bfloat16).astype(jnp.float32), axis=0)
    return grad_gate, grad_up, grad_down, row_grads, gate_terms


def reference(tokens, cotangent, gates, expert_ids, w_gate, w_up, w_down):
    most = N_DP * CAP
    gate_f = gates.astype(jnp.float32)

    def one(carry, inputs):
        grad_x, gate_acc = carry
        label, gate_m, up_m, down_m = inputs
        hit = expert_ids == label
        member = jnp.any(hit, axis=1)
        route = jnp.sum(jnp.where(hit, gate_f, jnp.float32(0.0)), axis=1)
        where = jnp.nonzero(member, size=most, fill_value=0)[0].astype(jnp.int32)
        valid = jnp.arange(most, dtype=jnp.int32) < jnp.sum(member.astype(jnp.int32))
        x_rows = jnp.where(valid[:, None], tokens[where], jnp.zeros((), tokens.dtype))
        d_rows = jnp.where(valid[:, None], cotangent[where], jnp.zeros((), cotangent.dtype))
        g_rows = jnp.where(valid, route[where], jnp.float32(0.0))
        grad_gate, grad_up, grad_down, row_grads, gate_terms = slot_grads(x_rows, d_rows, g_rows, gate_m, up_m, down_m)
        grad_x = grad_x.at[where].add(jnp.where(valid[:, None], row_grads, jnp.float32(0.0)))
        gate_vec = jnp.zeros((tokens.shape[0],), jnp.float32).at[where].add(jnp.where(valid, gate_terms, jnp.float32(0.0)))
        gate_acc = gate_acc + jnp.where(hit, gate_vec[:, None], jnp.float32(0.0))
        return (grad_x, gate_acc), (grad_gate, grad_up, grad_down)

    start = (jnp.zeros(tokens.shape, jnp.float32), jnp.zeros(expert_ids.shape, jnp.float32))
    labels = jnp.arange(EXPERTS, dtype=jnp.int32)
    (grad_x, gate_acc), (grad_gate, grad_up, grad_down) = lax.scan(one, start, (labels, w_gate, w_up, w_down))
    return grad_x.astype(jnp.bfloat16), gate_acc, grad_gate, grad_up, grad_down
```

```python
import functools

import jax
import jax.numpy as jnp
from jax import lax
from jax.experimental import pallas as pl
from jax.experimental.pallas import tpu as pltpu
from jax.sharding import PartitionSpec as P

CAP = 8
LANES = 128
F32 = jnp.float32
BF16 = jnp.bfloat16
VMEM = pl.BlockSpec(memory_space=pltpu.VMEM)
SMEM = pl.BlockSpec(memory_space=pltpu.SMEM)


def keep(array):
    return pltpu.with_memory_space_constraint(array, pltpu.VMEM)


def swap(value, axis, mask):
    size = lax.axis_size(axis)
    return lax.ppermute(value, axis, [(i, i ^ mask) for i in range(size)])


def reorder(shards, me):
    size = len(shards)
    mask = 1
    while mask < size:
        flip = (me & mask) != 0
        shards = [jnp.where(flip, shards[i ^ mask], shards[i]) for i in range(size)]
        mask *= 2
    return shards


def gather_far(own, axis):
    size = lax.axis_size(axis)
    held = {0: own}
    mask = size // 2
    while mask > 1:
        for rel in list(held):
            held[rel ^ mask] = swap(held[rel], axis, mask)
        mask //= 2
    return held


def gather_near(held, axis):
    size = lax.axis_size(axis)
    if size > 1:
        held = {**held, **{rel ^ 1: swap(held[rel], axis, 1) for rel in held}}
    return [held[i] for i in range(size)]


def gather_shards(own, axis):
    return gather_near(gather_far(own, axis), axis)


def add(held, arrived):
    return (held.astype(F32) + arrived.astype(F32)).astype(BF16)


def sum_far(held, axis):
    size = lax.axis_size(axis)
    total = None
    mask = 2
    while mask < size:
        arrived = {rel ^ mask: swap(held.pop(rel), axis, mask) for rel in list(held) if rel & mask}
        for rel, value in arrived.items():
            if rel:
                held[rel] = add(held[rel], value)
            else:
                total = value if total is None else add(total, value)
        mask *= 2
    return total


def sum_all(value, axis):
    size = lax.axis_size(axis)
    arrived = jnp.zeros_like(value)
    mask = 1
    while mask < size:
        if mask > 1:
            value = add(value, arrived)
        arrived = swap(value, axis, mask)
        mask *= 2
    return value, arrived


def one_hot(ids, gates, expert, experts):
    rows, tokens = expert.shape
    row = lax.broadcasted_iota(jnp.int32, (rows, tokens), 0)
    low = expert < experts // 2
    member = jnp.where(low, ids[0:1, :], ids[1:2, :]) == expert
    gate = jnp.where(low, gates[0:1, :], gates[1:2, :])
    earlier = lax.broadcasted_iota(jnp.int32, (tokens, tokens), 0) < lax.broadcasted_iota(
        jnp.int32, (tokens, tokens), 1
    )
    before = jnp.dot(
        member.astype(F32).astype(BF16), earlier.astype(F32).astype(BF16), preferred_element_type=F32
    )
    pick = jnp.logical_and(member, before == (row & (CAP - 1)).astype(F32))
    return jnp.where(pick, 1.0, 0.0), jnp.where(pick, gate, 0.0)


def row_blocks(experts, tokens):
    return lax.broadcasted_iota(jnp.int32, (experts * CAP, tokens), 0) // CAP


def pack_kernel(experts, ids_ref, gates_ref, x_ref, d_ref, slot_out, pick_out, gates_out):
    ids = ids_ref[...]
    gates = gates_ref[...].astype(F32)
    pick, pick_gate = one_hot(ids, gates, row_blocks(experts, ids.shape[1]), experts)
    pick_out[...] = pick.astype(BF16)
    gates_out[...] = gates
    slot_x = jnp.dot(pick.astype(BF16), x_ref[...], preferred_element_type=F32)
    slot_d = jnp.dot(pick_gate.astype(BF16), d_ref[...], preferred_element_type=F32)
    for i in range(experts):
        slot_out[i] = jnp.concatenate(
            [slot_x[i * CAP:(i + 1) * CAP], slot_d[i * CAP:(i + 1) * CAP]], axis=0
        ).astype(BF16)


def pack(ids, gates, tokens, cotangent, experts):
    count, feat = tokens.shape
    return pl.pallas_call(
        functools.partial(pack_kernel, experts),
        out_shape=[
            jax.ShapeDtypeStruct((experts, 2 * CAP, feat), BF16),
            jax.ShapeDtypeStruct((experts * CAP, count), BF16),
            jax.ShapeDtypeStruct((2, count), F32),
        ],
        in_specs=[VMEM] * 4,
        out_specs=[VMEM] * 3,
        cost_estimate=pl.CostEstimate(flops=10**8, bytes_accessed=2 * 10**6, transcendentals=0),
        name="pack",
    )(*[pltpu.with_memory_space_constraint(a, pltpu.HBM) for a in (ids, gates, tokens, cotangent)])


def load_kernel(count, *refs):
    sems = refs[-1]
    copies = [
        pltpu.make_async_copy(refs[i], refs[count + 1 + i], sems.at[i]) for i in range(count)
    ]
    for copy in copies:
        copy.start()
    for copy in copies:
        copy.wait()


def load(after, *arrays):
    count = len(arrays)
    total = sum(a.size * a.dtype.itemsize for a in arrays)
    return pl.pallas_call(
        functools.partial(load_kernel, count),
        out_shape=[pltpu.VMEM(a.shape, a.dtype) for a in arrays],
        in_specs=[pl.BlockSpec(memory_space=pltpu.HBM)] * count + [pl.BlockSpec(memory_space=pl.ANY)],
        out_specs=[VMEM] * count,
        scratch_shapes=[pltpu.SemaphoreType.DMA((count,))],
        cost_estimate=pl.CostEstimate(flops=0, bytes_accessed=total, transcendentals=0),
        compiler_params=pltpu.CompilerParams(vmem_limit_bytes=2**22),
        name="load",
    )(*[pltpu.with_memory_space_constraint(a, pltpu.HBM) for a in arrays], after)


def shard_at(me_ref, rel, feat):
    return pl.ds(pl.multiple_of((me_ref[0] ^ rel) * feat, feat), feat)


def products(rels, me_ref, x_refs, d_refs, gate_ref, up_ref, down_ref):
    feat = x_refs[0].shape[1]
    totals = None
    for rel, x_ref, d_ref in zip(rels, x_refs, d_refs):
        at = shard_at(me_ref, rel, feat)
        parts = (
            jnp.dot(x_ref[...], gate_ref[at, :], preferred_element_type=F32),
            jnp.dot(x_ref[...], up_ref[at, :], preferred_element_type=F32),
            lax.dot_general(
                d_ref[...], down_ref[:, at], (((1,), (1,)), ((), ())), preferred_element_type=F32
            ),
        )
        totals = parts if totals is None else tuple(a + b for a, b in zip(totals, parts))
    return totals


def early_kernel(rels, me_ref, *refs):
    count = len(rels)
    x_refs, d_refs, (gate_ref, up_ref, down_ref) = refs[:count], refs[count:2 * count], refs[2 * count:-3]
    totals = products(rels, me_ref, x_refs, d_refs, gate_ref, up_ref, down_ref)
    for out, value in zip(refs[-3:], totals):
        out[...] = value


def early(rels, me, x, d, weights):
    rows, units = x[0].shape[0], weights[0].shape[1]
    work = 6 * rows * units * x[0].shape[1] * len(rels)
    return pl.pallas_call(
        functools.partial(early_kernel, rels),
        out_shape=[jax.ShapeDtypeStruct((rows, units), F32)] * 3,
        in_specs=[SMEM] + [VMEM] * (2 * len(rels) + 3),
        out_specs=[VMEM] * 3,
        cost_estimate=pl.CostEstimate(flops=work, bytes_accessed=work // rows, transcendentals=0),
        compiler_params=pltpu.CompilerParams(vmem_limit_bytes=2**24),
        name="early",
    )(me, *[keep(a) for a in (*x, *d, *weights)])


def partial_x_kernel(rels, me_ref, after_ref, gate_ref, up_ref, down_ref, *refs):
    x_refs, outs = refs[:-2], refs[-2:]
    feat = x_refs[0].shape[1]
    for weight_ref, out in zip((gate_ref, up_ref), outs):
        total = None
        for rel, x_ref in zip(rels, x_refs):
            part = jnp.dot(
                x_ref[...], weight_ref[shard_at(me_ref, rel, feat), :], preferred_element_type=F32
            )
            total = part if total is None else total + part
        out[...] = total


def partial_d_kernel(rels, me_ref, after_ref, gate_ref, up_ref, down_ref, *refs):
    d_refs, out = refs[:-1], refs[-1]
    feat = d_refs[0].shape[1]
    total = None
    for rel, d_ref in zip(rels, d_refs):
        part = lax.dot_general(
            d_ref[...],
            down_ref[:, shard_at(me_ref, rel, feat)],
            (((1,), (1,)), ((), ())),
            preferred_element_type=F32,
        )
        total = part if total is None else total + part
    out[...] = total


def partial(kernel, count, rels, me, after, arrays, weights):
    rows, units = arrays[0].shape[0], weights[0].shape[1]
    work = 2 * count * rows * units * arrays[0].shape[1] * len(rels)
    return pl.pallas_call(
        functools.partial(kernel, rels),
        out_shape=[jax.ShapeDtypeStruct((rows, units), F32)] * count,
        in_specs=[SMEM, pl.BlockSpec(memory_space=pl.ANY)] + [VMEM] * (3 + len(rels)),
        out_specs=[VMEM] * count,
        cost_estimate=pl.CostEstimate(flops=work, bytes_accessed=work // rows, transcendentals=0),
        compiler_params=pltpu.CompilerParams(vmem_limit_bytes=2**24),
        name="partial",
    )(me, keep(after), *[keep(a) for a in (*weights, *arrays)])


def flip(index, rel):
    mask = 1
    while mask <= rel:
        if rel & mask:
            index = index + mask * (1 - 2 * ((index // mask) % 2))
        mask *= 2
    return index


def load_early_kernel(near, far, x0, d0, x1, d1, gate_in, up_in, down_in, gate, up, down, *refs):
    sums, sems = refs[:3], refs[3]
    feat = x0.shape[1]
    me = lax.axis_index("expert")

    def copies(rel):
        at = pl.ds(pl.multiple_of(flip(me, rel) * feat, feat), feat)
        return [
            pltpu.make_async_copy(src.at[place], dst.at[place], sems.at[i, rel])
            for i, (src, dst, place) in enumerate(
                ((gate_in, gate, at), (up_in, up, at), (down_in, down, (slice(None), at)))
            )
        ]

    first = [copies(rel) for rel in near]
    rest = [copies(rel) for rel in far]
    for i in range(3):
        for group in first:
            group[i].start()
    for i in range(3):
        for group in first:
            group[i].wait()
        if i == 0:
            for group in rest:
                for copy in group:
                    copy.start()
        total = None
        for rel, x_ref, d_ref in zip(near, (x0, x1), (d0, d1)):
            at = pl.ds(pl.multiple_of(flip(me, rel) * feat, feat), feat)
            if i < 2:
                part = jnp.dot(x_ref[...], (gate, up)[i][at, :], preferred_element_type=F32)
            else:
                part = lax.dot_general(
                    d_ref[...], down[:, at], (((1,), (1,)), ((), ())), preferred_element_type=F32
                )
            total = part if total is None else total + part
        sums[i][...] = total
    for group in rest:
        for copy in group:
            copy.wait()


def load_early(x, d, weights, after):
    shards = lax.axis_size("expert")
    rows = x[0].shape[0]
    units = weights[0].shape[1]
    near, far = list(range(2)), list(range(2, shards))
    kernel = functools.partial(load_early_kernel, near, far)
    out = pl.pallas_call(
        lambda after_ref, *refs: kernel(*refs),
        out_shape=[pltpu.VMEM(a.shape, a.dtype) for a in weights]
        + [jax.ShapeDtypeStruct((rows, units), F32)] * 3,
        in_specs=[pl.BlockSpec(memory_space=pl.ANY)]
        + [VMEM] * 4
        + [pl.BlockSpec(memory_space=pltpu.HBM)] * 3,
        out_specs=[VMEM] * 6,
        scratch_shapes=[pltpu.SemaphoreType.DMA((3, shards))],
        cost_estimate=pl.CostEstimate(
            flops=6 * rows * units * x[0].shape[1],
            bytes_accessed=sum(a.size * 2 for a in weights),
            transcendentals=0,
        ),
        compiler_params=pltpu.CompilerParams(vmem_limit_bytes=2**23),
        name="load_early",
    )(
        after,
        *[keep(a) for a in (x[0], d[0], x[1], d[1])],
        *[pltpu.with_memory_space_constraint(a, pltpu.HBM) for a in weights],
    )
    return out[:3], out[3:]


def late_kernel(rels, me_ref, *refs):
    count = len(rels)
    x_refs, d_refs, refs = refs[:count], refs[count:2 * count], refs[2 * count:]
    gate_ref, up_ref, down_ref, sum_refs = refs[0], refs[1], refs[2], refs[3:-4]
    hidden_out, d_gate_out, d_up_out, cols_out = refs[-4:]
    totals = [ref[...] for ref in sum_refs[:3]]
    for i, ref in enumerate(sum_refs[3:]):
        totals[i % 3] += ref[...]
    if rels:
        parts = products(rels, me_ref, x_refs, d_refs, gate_ref, up_ref, down_ref)
        totals = [a + b for a, b in zip(totals, parts)]
    pre_gate, pre_up, dhid = totals
    sig = 1.0 / (1.0 + jnp.exp(-pre_gate))
    act = pre_gate * sig
    hidden = (act * pre_up).astype(BF16)
    hidden_out[...] = hidden
    d_gate_out[...] = (dhid * pre_up * sig * (1.0 + pre_gate * (1.0 - sig))).astype(BF16)
    d_up_out[...] = (dhid * act).astype(BF16)
    total = jnp.sum(dhid * hidden.astype(F32), axis=1, keepdims=True)
    cols_out[...] = jnp.broadcast_to(total, cols_out.shape).astype(BF16)


def late(rels, me, x, d, weights, sums):
    rows, units = sums[0].shape
    work = 6 * rows * units * max(1, sum(a.shape[1] for a in x))
    return pl.pallas_call(
        functools.partial(late_kernel, rels),
        out_shape=[jax.ShapeDtypeStruct((rows, units), BF16)] * 3
        + [jax.ShapeDtypeStruct((rows, LANES), BF16)],
        in_specs=[SMEM] + [VMEM] * (2 * len(rels) + 3 + len(sums)),
        out_specs=[VMEM] * 4,
        cost_estimate=pl.CostEstimate(
            flops=work, bytes_accessed=work // rows, transcendentals=rows * units
        ),
        compiler_params=pltpu.CompilerParams(vmem_limit_bytes=2**24),
        name="late",
    )(me, *[keep(a) for a in (*x, *d, *weights, *sums)])


def term_kernel(rels, me_ref, after_ref, last_ref, d_gate_ref, d_up_ref, gate_ref, up_ref, *outs):
    feat = outs[0].shape[1]
    dims = (((1,), (1,)), ((), ()))
    for rel, out in zip(rels, outs):
        at = shard_at(me_ref, rel, feat)
        term = lax.dot_general(d_gate_ref[...], gate_ref[at, :], dims, preferred_element_type=F32)
        term += lax.dot_general(d_up_ref[...], up_ref[at, :], dims, preferred_element_type=F32)
        out[...] = term.astype(BF16)


def terms(rels, me, after, d_gate, d_up, gate_m, up_m, feat):
    rows, units = d_gate.shape
    return pl.pallas_call(
        functools.partial(term_kernel, rels),
        out_shape=[jax.ShapeDtypeStruct((rows, feat), BF16)] * len(rels),
        in_specs=[SMEM] + [pl.BlockSpec(memory_space=pl.ANY)] * 2 + [VMEM] * 4,
        out_specs=[VMEM] * len(rels),
        cost_estimate=pl.CostEstimate(flops=10**6, bytes_accessed=10**6, transcendentals=0),
        compiler_params=pltpu.CompilerParams(vmem_limit_bytes=2**24),
        name="terms",
    )(me, *after, *[keep(a) for a in (d_gate, d_up, gate_m, up_m)])


SLOTS = 4


def stream(steps, fill, copies):
    for step in range(steps + SLOTS):
        if step >= SLOTS:
            for copy in copies(step - SLOTS, step % SLOTS):
                copy.wait()
        if step < steps:
            fill(step, step % SLOTS)
            for copy in copies(step, step % SLOTS):
                copy.start()


def places(feat, shards, block):
    me = lax.axis_index("expert") if shards > 1 else 0

    def place(step):
        rel, part = divmod(step, feat // block)
        start = flip(me, rel) * feat + part * block
        return pl.ds(pl.multiple_of(start, block) if shards > 1 else start, block)

    def source(step):
        rel, part = divmod(step, feat // block)
        return rel, slice(part * block, (part + 1) * block)

    return shards * feat // block, source, place


def outer_rows_kernel(block, shards, after_ref, *refs):
    stage, sems = refs[-2:]
    lefts, refs = refs[:shards], refs[shards:-2]
    half = len(refs) // 2
    rights, outs = refs[:half], refs[half:]
    steps, source, place = places(lefts[0].shape[1], shards, block)

    def fill(step, slot):
        rel, at = source(step)
        left = lefts[rel][:, at].astype(F32).T.astype(BF16)
        for i, right in enumerate(rights):
            stage[slot, i] = jnp.dot(left, right[...], preferred_element_type=F32).astype(BF16)

    def copies(step, slot):
        return [
            pltpu.make_async_copy(stage.at[slot, i], out.at[place(step)], sems.at[slot, i])
            for i, out in enumerate(outs)
        ]

    stream(steps, fill, copies)


def outer_rows(lefts, rights, after, block):
    rows, feat = lefts[0].shape
    tall = feat * len(lefts)
    narrow = rights[0].shape[1]
    count = len(rights)
    return pl.pallas_call(
        functools.partial(outer_rows_kernel, block, len(lefts)),
        out_shape=[jax.ShapeDtypeStruct((tall, narrow), BF16)] * count,
        in_specs=[pl.BlockSpec(memory_space=pl.ANY)] + [VMEM] * (len(lefts) + count),
        out_specs=[pl.BlockSpec(memory_space=pltpu.HBM)] * count,
        scratch_shapes=[
            pltpu.VMEM((SLOTS, count, block, narrow), BF16),
            pltpu.SemaphoreType.DMA((SLOTS, count)),
        ],
        cost_estimate=pl.CostEstimate(
            flops=2 * rows * tall * narrow * count,
            bytes_accessed=2 * tall * narrow * count,
            transcendentals=0,
        ),
        compiler_params=pltpu.CompilerParams(vmem_limit_bytes=2**24),
        name="outer_rows",
    )(pltpu.with_memory_space_constraint(after, pltpu.HBM), *[keep(a) for a in (*lefts, *rights)])


def outer_columns_kernel(block, shards, after_ref, left_ref, *refs):
    rights, (out_ref, turned, stage, sems) = refs[:shards], refs[shards:]
    turned[...] = left_ref[...].astype(F32).T.astype(BF16)
    steps, source, place = places(rights[0].shape[1], shards, block)

    def fill(step, slot):
        rel, at = source(step)
        stage[slot] = jnp.dot(turned[...], rights[rel][:, at], preferred_element_type=F32).astype(BF16)

    def copies(step, slot):
        return [pltpu.make_async_copy(stage.at[slot], out_ref.at[:, place(step)], sems.at[slot])]

    stream(steps, fill, copies)


def outer_columns(left, rights, after, block):
    rows, feat = rights[0].shape
    wide = feat * len(rights)
    tall = left.shape[1]
    return pl.pallas_call(
        functools.partial(outer_columns_kernel, block, len(rights)),
        out_shape=jax.ShapeDtypeStruct((tall, wide), BF16),
        in_specs=[pl.BlockSpec(memory_space=pl.ANY)] + [VMEM] * (1 + len(rights)),
        out_specs=pl.BlockSpec(memory_space=pltpu.HBM),
        scratch_shapes=[
            pltpu.VMEM((tall, rows), BF16),
            pltpu.VMEM((SLOTS, tall, block), BF16),
            pltpu.SemaphoreType.DMA((SLOTS,)),
        ],
        cost_estimate=pl.CostEstimate(flops=10**6, bytes_accessed=10**6, transcendentals=0),
        compiler_params=pltpu.CompilerParams(vmem_limit_bytes=2**24),
        name="outer_columns",
    )(keep(after), keep(left), *[keep(a) for a in rights])


def settle_kernel(held_ref, arrived_ref, cols_ref, more_ref, after_ref, out_ref):
    feat = held_ref.shape[1]
    total = held_ref[...].astype(F32) + arrived_ref[...].astype(F32)
    cols = cols_ref[...].astype(F32) + more_ref[...].astype(F32)
    for i in range(out_ref.shape[0]):
        out_ref[i, :, :feat] = total[i * CAP:(i + 1) * CAP].astype(BF16)
        out_ref[i, :, feat:] = cols[i * CAP:(i + 1) * CAP].astype(BF16)


def settle(own, cols, after):
    rows, feat = own[0].shape
    return pl.pallas_call(
        settle_kernel,
        out_shape=jax.ShapeDtypeStruct((rows // CAP, CAP, feat + LANES), BF16),
        in_specs=[VMEM] * 4 + [pl.BlockSpec(memory_space=pl.ANY)],
        out_specs=VMEM,
        cost_estimate=pl.CostEstimate(flops=0, bytes_accessed=10**6, transcendentals=0),
        name="settle",
    )(*[keep(a) for a in (*own, *cols)], pltpu.with_memory_space_constraint(after, pltpu.HBM))


def combine_kernel(pick_ref, gates_ref, rows_ref, grad_ref, gate_ref):
    feat = grad_ref.shape[1]
    half = pick_ref.shape[0] // 2
    pick = pick_ref[...]
    rows = rows_ref[...]
    grad_ref[...] = lax.dot_general(
        pick, rows[:, :feat], (((0,), (0,)), ((), ())), preferred_element_type=F32
    ).astype(BF16)
    terms = pick.astype(F32) * rows[:, feat:].astype(F32)
    gate_ref[0:1, :] = jnp.sum(terms[:half], axis=0, keepdims=True) / gates_ref[0:1, :]
    gate_ref[1:2, :] = jnp.sum(terms[half:], axis=0, keepdims=True) / gates_ref[1:2, :]


def combine(pick, gates, rows, feat):
    count = pick.shape[1]
    return pl.pallas_call(
        combine_kernel,
        out_shape=[
            jax.ShapeDtypeStruct((count, feat), BF16),
            jax.ShapeDtypeStruct((2, count), F32),
        ],
        in_specs=[VMEM] * 3,
        out_specs=[VMEM] * 2,
        cost_estimate=pl.CostEstimate(flops=10**8, bytes_accessed=10**6, transcendentals=0),
        name="combine",
    )(pick, gates, pltpu.with_memory_space_constraint(rows, pltpu.VMEM))


def per_device(tokens, cotangent, gates, expert_ids, w_gate, w_up, w_down):
    experts = lax.axis_size("dp")
    shards = lax.axis_size("expert")
    me = lax.axis_index("expert")
    rows = experts * CAP
    feat = tokens.shape[1]
    ids_t = expert_ids.T
    gates_t = gates.T
    me_ref = me.reshape(1)
    slots, pick, gates_f = pack(ids_t, gates_t, tokens, cotangent, experts)
    slots = lax.all_to_all(slots, "dp", split_axis=0, concat_axis=0, tiled=True)
    x = gather_far(slots[:, :CAP].reshape(rows, feat), "expert")
    d = gather_far(slots[:, CAP:].reshape(rows, feat), "expert")
    weights = [w_gate[0], w_up[0], w_down[0]]
    if feat % LANES or shards < 4:
        x, d = gather_near(x, "expert"), gather_near(d, "expert")
        x = [jnp.concatenate(reorder(x, me), axis=1)]
        d = [jnp.concatenate(reorder(d, me), axis=1)]
        weights = load(slots, *weights)
        sums = early([0], me_ref * 0, x, d, weights)
        odd = []
    else:
        x[1], d[1] = swap(x[0], "expert", 1), swap(d[0], "expert", 1)
        weights, sums = load_early(x, d, weights, slots)
        even = list(range(2, shards, 2))
        odd = list(range(3, shards, 2))
        rest, sums = lax.optimization_barrier(([x[i] for i in even], sums))
        for i, x_i in zip(even, rest):
            x[i], x[i + 1] = x_i, swap(x_i, "expert", 1)
        more = partial(partial_x_kernel, 2, even, me_ref, sums[0], rest, weights)
        rest, more = lax.optimization_barrier(([d[i] for i in even], more))
        for i, d_i in zip(even, rest):
            d[i], d[i + 1] = d_i, swap(d_i, "expert", 1)
        more = [*more, *partial(partial_d_kernel, 1, even, me_ref, more[0], rest, weights)]
        x, d = [x[i] for i in range(shards)], [d[i] for i in range(shards)]
        sums = [*sums, *more]
    hidden, d_gate, d_up, cols = late(odd, me_ref, [x[i] for i in odd], [d[i] for i in odd], weights, sums)

    def term(rels, after):
        got = terms(rels, me_ref, after, d_gate, d_up, *weights[:2], feat) if rels else []
        return dict(zip(rels, got))

    start = (keep(cols), keep(cols))
    sent = term(list(range(3, shards, 2)), start)
    arrived = {rel ^ 1: swap(part, "expert", 1) for rel, part in sent.items()}
    kept = term(list(range(2, shards, 2)), start)
    held = {rel: add(part, arrived[rel]) for rel, part in kept.items()}
    last = held[max(held)] if held else cols
    wide = feat * shards
    grad_down = outer_columns(hidden, d, last, wide // 8)
    other = sum_far(held, "expert")
    if other is None:
        other = jnp.zeros((rows, feat), BF16)
    start = (keep(other), pltpu.with_memory_space_constraint(grad_down, pltpu.HBM))
    sent = term([1] if shards > 1 else [], start)
    own = term([0], start)[0]
    for part in sent.values():
        own = add(own, swap(part, "expert", 1))
    total = settle((own, other), sum_all(cols, "expert"), grad_down)
    got = lax.all_to_all(total, "dp", split_axis=0, concat_axis=0, tiled=True)
    got = got.reshape(rows, feat + LANES)
    grad_gate, grad_up = outer_rows(x, (d_gate, d_up), total, wide // 16)
    grad_tokens, gate_grads = combine(pick, gates_f, got, feat)
    return (grad_tokens, gate_grads.T, grad_gate[None], grad_up[None], grad_down[None])


def solution(mesh):
    in_specs = (
        P("dp", "expert"),
        P("dp", "expert"),
        P("dp", None),
        P("dp", None),
        P("dp", None, "expert"),
        P("dp", None, "expert"),
        P("dp", "expert", None),
    )
    out_specs = (
        P("dp", "expert"),
        P("dp", None),
        P("dp", None, "expert"),
        P("dp", None, "expert"),
        P("dp", "expert", None),
    )
    return jax.shard_map(
        per_device, mesh=mesh, in_specs=in_specs, out_specs=out_specs, check_vma=False
    )
```

```python
import functools
import math

import jax
import jax.numpy as jnp
from jax import lax
from jax.experimental import pallas as pl
from jax.experimental.pallas import tpu as pltpu
from jax.sharding import PartitionSpec as P

CAP = 8
LANES = 128
F32 = jnp.float32
BF16 = jnp.bfloat16
VMEM = pl.BlockSpec(memory_space=pltpu.VMEM)
SMEM = pl.BlockSpec(memory_space=pltpu.SMEM)


def keep(array):
    return pltpu.with_memory_space_constraint(array, pltpu.VMEM)


def swap(value, axis, mask):
    size = lax.axis_size(axis)
    return lax.ppermute(value, axis, [(i, i ^ mask) for i in range(size)])


def reorder(shards, me):
    size = len(shards)
    mask = 1
    while mask < size:
        flip = (me & mask) != 0
        shards = [jnp.where(flip, shards[i ^ mask], shards[i]) for i in range(size)]
        mask *= 2
    return shards


def gather_far(own, axis):
    size = lax.axis_size(axis)
    held = {0: own}
    mask = size // 2
    while mask > 1:
        for rel in list(held):
            held[rel ^ mask] = swap(held[rel], axis, mask)
        mask //= 2
    return held


def gather_near(held, axis):
    size = lax.axis_size(axis)
    if size > 1:
        held = {**held, **{rel ^ 1: swap(held[rel], axis, 1) for rel in held}}
    return [held[i] for i in range(size)]


def gather_shards(own, axis):
    return gather_near(gather_far(own, axis), axis)


def add(held, arrived):
    return (held.astype(F32) + arrived.astype(F32)).astype(BF16)


def sum_far(held, axis):
    size = lax.axis_size(axis)
    total = None
    mask = 2
    while mask < size:
        arrived = {rel ^ mask: swap(held.pop(rel), axis, mask) for rel in list(held) if rel & mask}
        for rel, value in arrived.items():
            if rel:
                held[rel] = add(held[rel], value)
            else:
                total = value if total is None else add(total, value)
        mask *= 2
    return total


def one_hot(ids, gates, expert, experts):
    rows, tokens = expert.shape
    row = lax.broadcasted_iota(jnp.int32, (rows, tokens), 0)
    low = expert < experts // 2
    member = jnp.where(low, ids[0:1, :], ids[1:2, :]) == expert
    gate = jnp.where(low, gates[0:1, :], gates[1:2, :])
    earlier = lax.broadcasted_iota(jnp.int32, (tokens, tokens), 0) < lax.broadcasted_iota(
        jnp.int32, (tokens, tokens), 1
    )
    before = jnp.dot(
        member.astype(F32).astype(BF16), earlier.astype(F32).astype(BF16), preferred_element_type=F32
    )
    pick = jnp.logical_and(member, before == (row & (CAP - 1)).astype(F32))
    return jnp.where(pick, 1.0, 0.0), jnp.where(pick, gate, 0.0)


def row_blocks(experts, tokens):
    return lax.broadcasted_iota(jnp.int32, (experts * CAP, tokens), 0) // CAP


def column_block(feat):
    return feat // 2 if feat % (2 * LANES) == 0 else feat


def pack_kernel(
    experts, block, ids_hbm, gates_hbm, x_hbm, d_hbm, slot_hbm, pick_out, gates_out, ids, gates_low, x_ref, d_ref, slots, sems
):
    feat = x_ref.shape[1]
    steps = feat // block

    def columns(step):
        return slice(step * block, (step + 1) * block)

    small = [
        pltpu.make_async_copy(ids_hbm, ids, sems.at[3, 0]),
        pltpu.make_async_copy(gates_hbm, gates_low, sems.at[4, 0]),
    ]
    loads = [
        [
            pltpu.make_async_copy(src.at[:, columns(step)], dst.at[:, columns(step)], sems.at[i, step])
            for i, (src, dst) in enumerate(((x_hbm, x_ref), (d_hbm, d_ref)))
        ]
        for step in range(steps)
    ]
    stores = [
        pltpu.make_async_copy(
            slots.at[:, :, columns(step)], slot_hbm.at[:, :, columns(step)], sems.at[2, step]
        )
        for step in range(steps)
    ]
    for copy in small + [copy for pair in loads for copy in pair]:
        copy.start()
    for copy in small:
        copy.wait()
    gates = gates_low[...].astype(F32)
    pick, pick_gate = one_hot(ids[...], gates, row_blocks(experts, ids.shape[1]), experts)
    pick, pick_gate = pick.astype(BF16), pick_gate.astype(BF16)
    for step in range(steps):
        for copy in loads[step]:
            copy.wait()
        slot_x = jnp.dot(pick, x_ref[:, columns(step)], preferred_element_type=F32)
        slot_d = jnp.dot(pick_gate, d_ref[:, columns(step)], preferred_element_type=F32)
        for i in range(experts):
            slots[i, :, columns(step)] = jnp.concatenate(
                [slot_x[i * CAP:(i + 1) * CAP], slot_d[i * CAP:(i + 1) * CAP]], axis=0
            ).astype(BF16)
        stores[step].start()
    pick_out[...] = pick
    gates_out[...] = gates
    for copy in stores:
        copy.wait()


def pack(ids, gates, tokens, cotangent, experts):
    count, feat = tokens.shape
    block = column_block(feat)
    steps = feat // block
    rows = experts * CAP
    hbm = pl.BlockSpec(memory_space=pltpu.HBM)
    return pl.pallas_call(
        functools.partial(pack_kernel, experts, block),
        out_shape=[
            jax.ShapeDtypeStruct((experts, 2 * CAP, feat), BF16),
            jax.ShapeDtypeStruct((rows, count), BF16),
            jax.ShapeDtypeStruct((2, count), F32),
        ],
        in_specs=[hbm] * 4,
        out_specs=[hbm, VMEM, VMEM],
        scratch_shapes=[
            pltpu.VMEM((2, count), jnp.int32),
            pltpu.VMEM((2, count), BF16),
            pltpu.VMEM((count, feat), BF16),
            pltpu.VMEM((count, feat), BF16),
            pltpu.VMEM((experts, 2 * CAP, feat), BF16),
            pltpu.SemaphoreType.DMA((5, steps)),
        ],
        cost_estimate=pl.CostEstimate(flops=10**8, bytes_accessed=2 * 10**6, transcendentals=0),
        compiler_params=pltpu.CompilerParams(vmem_limit_bytes=2**23),
        name="pack",
    )(*[pltpu.with_memory_space_constraint(a, pltpu.HBM) for a in (ids, gates, tokens, cotangent)])


def load_kernel(count, *refs):
    sems = refs[-1]
    copies = [
        pltpu.make_async_copy(refs[i], refs[count + 1 + i], sems.at[i]) for i in range(count)
    ]
    for copy in copies:
        copy.start()
    for copy in copies:
        copy.wait()


def load(after, *arrays):
    count = len(arrays)
    total = sum(a.size * a.dtype.itemsize for a in arrays)
    return pl.pallas_call(
        functools.partial(load_kernel, count),
        out_shape=[pltpu.VMEM(a.shape, a.dtype) for a in arrays],
        in_specs=[pl.BlockSpec(memory_space=pltpu.HBM)] * count + [pl.BlockSpec(memory_space=pl.ANY)],
        out_specs=[VMEM] * count,
        scratch_shapes=[pltpu.SemaphoreType.DMA((count,))],
        cost_estimate=pl.CostEstimate(flops=0, bytes_accessed=total, transcendentals=0),
        compiler_params=pltpu.CompilerParams(vmem_limit_bytes=2**22),
        name="load",
    )(*[pltpu.with_memory_space_constraint(a, pltpu.HBM) for a in arrays], after)


def shard_at(me_ref, rel, feat):
    return pl.ds(pl.multiple_of((me_ref[0] ^ rel) * feat, feat), feat)


def products(rels, me_ref, x_refs, d_refs, gate_ref, up_ref, down_ref):
    feat = x_refs[0].shape[1]
    totals = None
    for rel, x_ref, d_ref in zip(rels, x_refs, d_refs):
        at = shard_at(me_ref, rel, feat)
        parts = (
            jnp.dot(x_ref[...], gate_ref[at, :], preferred_element_type=F32),
            jnp.dot(x_ref[...], up_ref[at, :], preferred_element_type=F32),
            lax.dot_general(
                d_ref[...], down_ref[:, at], (((1,), (1,)), ((), ())), preferred_element_type=F32
            ),
        )
        totals = parts if totals is None else tuple(a + b for a, b in zip(totals, parts))
    return totals


def early_kernel(rels, me_ref, *refs):
    count = len(rels)
    x_refs, d_refs, (gate_ref, up_ref, down_ref) = refs[:count], refs[count:2 * count], refs[2 * count:-3]
    totals = products(rels, me_ref, x_refs, d_refs, gate_ref, up_ref, down_ref)
    for out, value in zip(refs[-3:], totals):
        out[...] = value


def early(rels, me, x, d, weights):
    rows, units = x[0].shape[0], weights[0].shape[1]
    work = 6 * rows * units * x[0].shape[1] * len(rels)
    return pl.pallas_call(
        functools.partial(early_kernel, rels),
        out_shape=[jax.ShapeDtypeStruct((rows, units), F32)] * 3,
        in_specs=[SMEM] + [VMEM] * (2 * len(rels) + 3),
        out_specs=[VMEM] * 3,
        cost_estimate=pl.CostEstimate(flops=work, bytes_accessed=work // rows, transcendentals=0),
        compiler_params=pltpu.CompilerParams(vmem_limit_bytes=2**24),
        name="early",
    )(me, *[keep(a) for a in (*x, *d, *weights)])


def partial_x_kernel(rels, me_ref, after_ref, gate_ref, up_ref, down_ref, *refs):
    x_refs, outs = refs[:-2], refs[-2:]
    feat = x_refs[0].shape[1]
    for weight_ref, out in zip((gate_ref, up_ref), outs):
        total = None
        for rel, x_ref in zip(rels, x_refs):
            part = jnp.dot(
                x_ref[...], weight_ref[shard_at(me_ref, rel, feat), :], preferred_element_type=F32
            )
            total = part if total is None else total + part
        out[...] = total


def partial_d_kernel(rels, me_ref, after_ref, gate_ref, up_ref, down_ref, *refs):
    d_refs, out = refs[:-1], refs[-1]
    feat = d_refs[0].shape[1]
    total = None
    for rel, d_ref in zip(rels, d_refs):
        part = lax.dot_general(
            d_ref[...],
            down_ref[:, shard_at(me_ref, rel, feat)],
            (((1,), (1,)), ((), ())),
            preferred_element_type=F32,
        )
        total = part if total is None else total + part
    out[...] = total


def partial(kernel, count, rels, me, after, arrays, weights):
    rows, units = arrays[0].shape[0], weights[0].shape[1]
    work = 2 * count * rows * units * arrays[0].shape[1] * len(rels)
    return pl.pallas_call(
        functools.partial(kernel, rels),
        out_shape=[jax.ShapeDtypeStruct((rows, units), F32)] * count,
        in_specs=[SMEM, pl.BlockSpec(memory_space=pl.ANY)] + [VMEM] * (3 + len(rels)),
        out_specs=[VMEM] * count,
        cost_estimate=pl.CostEstimate(flops=work, bytes_accessed=work // rows, transcendentals=0),
        compiler_params=pltpu.CompilerParams(vmem_limit_bytes=2**24),
        name="partial",
    )(me, keep(after), *[keep(a) for a in (*weights, *arrays)])


def flip(index, rel):
    mask = 1
    while mask <= rel:
        if rel & mask:
            index = index + mask * (1 - 2 * ((index // mask) % 2))
        mask *= 2
    return index


def load_early_kernel(x0, d0, gate_in, up_in, down_in, gate, up, down, *refs):
    sums, sems = refs[:3], refs[3]
    feat = x0.shape[1]
    me = lax.axis_index("expert")
    shards = gate.shape[0] // feat

    def place(rel):
        return pl.ds(pl.multiple_of(flip(me, rel) * feat, feat), feat)

    def copies(rel):
        at = place(rel)
        return [
            pltpu.make_async_copy(src.at[where], dst.at[where], sems.at[i, rel])
            for i, (src, dst, where) in enumerate(
                ((gate_in, gate, at), (up_in, up, at), (down_in, down, (slice(None), at)))
            )
        ]

    first, *rest = [copies(rel) for rel in range(shards)]
    for copy in first:
        copy.start()
    for group in rest:
        for copy in group:
            copy.start()
    at = place(0)
    for i in range(3):
        first[i].wait()
        if i < 2:
            sums[i][...] = jnp.dot(x0[...], (gate, up)[i][at, :], preferred_element_type=F32)
        else:
            sums[i][...] = lax.dot_general(
                d0[...], down[:, at], (((1,), (1,)), ((), ())), preferred_element_type=F32
            )
    for group in rest:
        for copy in group:
            copy.wait()


def load_early(x, d, weights, after):
    rows = x.shape[0]
    units = weights[0].shape[1]
    shards = lax.axis_size("expert")
    out = pl.pallas_call(
        lambda after_ref, *refs: load_early_kernel(*refs),
        out_shape=[pltpu.VMEM(a.shape, a.dtype) for a in weights]
        + [jax.ShapeDtypeStruct((rows, units), F32)] * 3,
        in_specs=[pl.BlockSpec(memory_space=pl.ANY)]
        + [VMEM] * 2
        + [pl.BlockSpec(memory_space=pltpu.HBM)] * 3,
        out_specs=[VMEM] * 6,
        scratch_shapes=[pltpu.SemaphoreType.DMA((3, shards))],
        cost_estimate=pl.CostEstimate(
            flops=6 * rows * units * x.shape[1],
            bytes_accessed=sum(a.size * 2 for a in weights),
            transcendentals=0,
        ),
        compiler_params=pltpu.CompilerParams(vmem_limit_bytes=2**23),
        name="load_early",
    )(
        keep(after),
        keep(x),
        keep(d),
        *[pltpu.with_memory_space_constraint(a, pltpu.HBM) for a in weights],
    )
    return out[:3], out[3:]


def late_kernel(rels, feat, me_ref, *refs):
    count = len(rels)
    x_refs, d_refs, refs = refs[:count], refs[count:2 * count], refs[2 * count:]
    refs, outs = refs[:-4 - count], refs[-4 - count:]
    (gate_ref, up_ref, down_ref), sum_refs = refs[:3], refs[3:]
    hidden_out, d_gate_out, d_up_out, cols_out = outs[:4]
    totals = [ref[...] for ref in sum_refs[:3]]
    for i, ref in enumerate(sum_refs[3:]):
        totals[i % 3] += ref[...]
    if rels:
        parts = products(rels, me_ref, x_refs, d_refs, gate_ref, up_ref, down_ref)
        totals = [a + b for a, b in zip(totals, parts)]
    pre_gate, pre_up, dhid = totals
    sig = 1.0 / (1.0 + jnp.exp(-pre_gate))
    act = pre_gate * sig
    hidden = (act * pre_up).astype(BF16)
    d_gate = (dhid * pre_up * sig * (1.0 + pre_gate * (1.0 - sig))).astype(BF16)
    d_up = (dhid * act).astype(BF16)
    total = jnp.sum(dhid * hidden.astype(F32), axis=1, keepdims=True)
    cols = jnp.broadcast_to(total, cols_out.shape).astype(BF16)
    for rel, out in zip(rels, outs[4:]):
        out[:, :feat] = term_piece(me_ref, rel, 0, feat, feat, d_gate, d_up, gate_ref, up_ref)
        out[:, feat:] = cols
    hidden_out[...] = hidden
    d_gate_out[...] = d_gate
    d_up_out[...] = d_up
    cols_out[...] = cols


def late(rels, me, x, d, weights, sums, feat):
    rows, units = sums[0].shape
    work = 10 * rows * units * feat * max(1, len(rels))
    return pl.pallas_call(
        functools.partial(late_kernel, rels, feat),
        out_shape=[jax.ShapeDtypeStruct((rows, units), BF16)] * 3
        + [jax.ShapeDtypeStruct((rows, LANES), BF16)]
        + [jax.ShapeDtypeStruct((rows, feat + LANES), BF16)] * len(rels),
        in_specs=[SMEM] + [VMEM] * (2 * len(rels) + 3 + len(sums)),
        out_specs=[VMEM] * (4 + len(rels)),
        cost_estimate=pl.CostEstimate(
            flops=work, bytes_accessed=work // rows, transcendentals=rows * units
        ),
        compiler_params=pltpu.CompilerParams(vmem_limit_bytes=2**24),
        name="late",
    )(me, *[keep(a) for a in (*x, *d, *weights, *sums)])


def term_piece(me_ref, rel, low, high, feat, d_gate, d_up, gate_ref, up_ref):
    dims = (((1,), (1,)), ((), ()))
    start = (me_ref[0] ^ rel) * feat + low
    at = pl.ds(pl.multiple_of(start, math.gcd(feat, low)), high - low)
    term = lax.dot_general(d_gate, gate_ref[at, :], dims, preferred_element_type=F32)
    term += lax.dot_general(d_up, up_ref[at, :], dims, preferred_element_type=F32)
    return term.astype(BF16)


def term_kernel(pieces, feat, me_ref, after_ref, last_ref, d_gate_ref, d_up_ref, cols_ref, gate_ref, up_ref, *outs):
    for (rel, low, high), out in zip(pieces, outs):
        out[:, :high - low] = term_piece(
            me_ref, rel, low, high, feat, d_gate_ref[...], d_up_ref[...], gate_ref, up_ref
        )
        if high == feat:
            out[:, high - low:] = cols_ref[...]


def terms(pieces, me, after, d_gate, d_up, cols, gate_m, up_m, feat):
    rows = d_gate.shape[0]
    return pl.pallas_call(
        functools.partial(term_kernel, pieces, feat),
        out_shape=[
            jax.ShapeDtypeStruct((rows, high - low + (LANES if high == feat else 0)), BF16)
            for rel, low, high in pieces
        ],
        in_specs=[SMEM] + [pl.BlockSpec(memory_space=pl.ANY)] * 2 + [VMEM] * 5,
        out_specs=[VMEM] * len(pieces),
        cost_estimate=pl.CostEstimate(flops=1, bytes_accessed=1, transcendentals=0),
        compiler_params=pltpu.CompilerParams(vmem_limit_bytes=2**24),
        name="terms",
    )(me, *after, *[keep(a) for a in (d_gate, d_up, cols, gate_m, up_m)])


SLOTS = 4


def stream(steps, fill, copies, beside=()):
    beside = list(beside)
    for step in range(steps + SLOTS):
        if step >= SLOTS:
            for copy in copies(step - SLOTS, step % SLOTS):
                copy.wait()
        if step < steps:
            fill(step, step % SLOTS)
            for copy in copies(step, step % SLOTS):
                copy.start()
            if steps - step <= len(beside):
                beside[step - steps]()


def places(feat, shards, block):
    me = lax.axis_index("expert") if shards > 1 else 0

    def place(step):
        rel, part = divmod(step, feat // block)
        start = flip(me, rel) * feat + part * block
        return pl.ds(pl.multiple_of(start, block) if shards > 1 else start, block)

    def source(step):
        rel, part = divmod(step, feat // block)
        return rel, slice(part * block, (part + 1) * block)

    return shards * feat // block, source, place


def outer_rows_kernel(block, shards, after_ref, *refs):
    stage, sems = refs[-2:]
    lefts, refs = refs[:shards], refs[shards:-2]
    half = len(refs) // 2
    rights, outs = refs[:half], refs[half:]
    steps, source, place = places(lefts[0].shape[1], shards, block)

    def fill(step, slot):
        rel, at = source(step)
        left = lefts[rel][:, at].astype(F32).T.astype(BF16)
        for i, right in enumerate(rights):
            stage[slot, i] = jnp.dot(left, right[...], preferred_element_type=F32).astype(BF16)

    def copies(step, slot):
        return [
            pltpu.make_async_copy(stage.at[slot, i], out.at[place(step)], sems.at[slot, i])
            for i, out in enumerate(outs)
        ]

    stream(steps, fill, copies)


def outer_rows(lefts, rights, after, block):
    rows, feat = lefts[0].shape
    tall = feat * len(lefts)
    narrow = rights[0].shape[1]
    count = len(rights)
    return pl.pallas_call(
        functools.partial(outer_rows_kernel, block, len(lefts)),
        out_shape=[jax.ShapeDtypeStruct((tall, narrow), BF16)] * count,
        in_specs=[pl.BlockSpec(memory_space=pl.ANY)] + [VMEM] * (len(lefts) + count),
        out_specs=[pl.BlockSpec(memory_space=pltpu.HBM)] * count,
        scratch_shapes=[
            pltpu.VMEM((SLOTS, count, block, narrow), BF16),
            pltpu.SemaphoreType.DMA((SLOTS, count)),
        ],
        cost_estimate=pl.CostEstimate(
            flops=2 * rows * tall * narrow * count,
            bytes_accessed=2 * tall * narrow * count,
            transcendentals=0,
        ),
        compiler_params=pltpu.CompilerParams(vmem_limit_bytes=2**24),
        name="outer_rows",
    )(pltpu.with_memory_space_constraint(after, pltpu.HBM), *[keep(a) for a in (*lefts, *rights)])


def middle_kernel(
    block, pieces, feat, me_ref, after_ref, left_ref, d_gate_ref, d_up_ref, cols_ref, gate_ref, up_ref, *refs
):
    outs, (turned, stage, sems) = refs[-4 - len(pieces):-3], refs[-3:]
    rights, out_ref, outs = refs[:-4 - len(pieces)], outs[0], outs[1:]
    turned[...] = left_ref[...].astype(F32).T.astype(BF16)
    steps, source, place = places(rights[0].shape[1], len(rights), block)

    def fill(step, slot):
        rel, at = source(step)
        stage[slot] = jnp.dot(turned[...], rights[rel][:, at], preferred_element_type=F32).astype(BF16)

    def copies(step, slot):
        return [pltpu.make_async_copy(stage.at[slot], out_ref.at[:, place(step)], sems.at[slot])]

    def term(piece, out):
        rel, low, high = piece
        out[:, :high - low] = term_piece(
            me_ref, rel, low, high, feat, d_gate_ref[...], d_up_ref[...], gate_ref, up_ref
        )
        if high == feat:
            out[:, high - low:] = cols_ref[...]

    stream(steps, fill, copies, [functools.partial(term, *pair) for pair in zip(pieces, outs)])


def middle(left, rights, after, block, pieces, me, d_gate, d_up, cols, gate_m, up_m, feat):
    rows = left.shape[0]
    wide = rights[0].shape[1] * len(rights)
    tall = left.shape[1]
    return pl.pallas_call(
        functools.partial(middle_kernel, block, pieces, feat),
        out_shape=[jax.ShapeDtypeStruct((tall, wide), BF16)]
        + [
            jax.ShapeDtypeStruct((rows, high - low + (LANES if high == feat else 0)), BF16)
            for rel, low, high in pieces
        ],
        in_specs=[SMEM, pl.BlockSpec(memory_space=pl.ANY)] + [VMEM] * (6 + len(rights)),
        out_specs=[pl.BlockSpec(memory_space=pltpu.HBM)] + [VMEM] * len(pieces),
        scratch_shapes=[
            pltpu.VMEM((tall, rows), BF16),
            pltpu.VMEM((SLOTS, tall, block), BF16),
            pltpu.SemaphoreType.DMA((SLOTS,)),
        ],
        cost_estimate=pl.CostEstimate(
            flops=4 * rows * wide * tall, bytes_accessed=2 * wide * tall, transcendentals=0
        ),
        compiler_params=pltpu.CompilerParams(vmem_limit_bytes=2**24),
        name="middle",
    )(me, keep(after), *[keep(a) for a in (left, d_gate, d_up, cols, gate_m, up_m, *rights)])


def settle_kernel(count, *refs):
    pieces, parts, out_ref = refs[:count], refs[count:-2], refs[-1]
    low = 0
    for piece in pieces:
        at = slice(low, low + piece.shape[1])
        total = piece[...].astype(F32)
        for ref in parts:
            total += ref[:, at].astype(F32)
        for i in range(out_ref.shape[0]):
            out_ref[i, :, at] = total[i * CAP:(i + 1) * CAP].astype(BF16)
        low += piece.shape[1]


def settle(pieces, parts, after):
    rows = pieces[0].shape[0]
    wide = sum(a.shape[1] for a in pieces)
    return pl.pallas_call(
        functools.partial(settle_kernel, len(pieces)),
        out_shape=jax.ShapeDtypeStruct((rows // CAP, CAP, wide), BF16),
        in_specs=[VMEM] * (len(pieces) + len(parts)) + [pl.BlockSpec(memory_space=pl.ANY)],
        out_specs=VMEM,
        cost_estimate=pl.CostEstimate(flops=0, bytes_accessed=10**6, transcendentals=0),
        name="settle",
    )(*[keep(a) for a in (*pieces, *parts)], pltpu.with_memory_space_constraint(after, pltpu.HBM))


def combine_kernel(feat, block, pick_ref, gates_ref, rows_ref, grad_ref, gate_ref):
    pick = pick_ref[...]
    at = pl.ds(pl.multiple_of(pl.program_id(0) * block, block), block) if block < feat else slice(0, feat)
    grad_ref[...] = lax.dot_general(
        pick, rows_ref[:, at], (((0,), (0,)), ((), ())), preferred_element_type=F32
    ).astype(BF16)

    @pl.when(pl.program_id(0) == 0)
    def _():
        half = pick.shape[0] // 2
        terms = pick.astype(F32) * rows_ref[:, feat:].astype(F32)
        gate_ref[0:1, :] = jnp.sum(terms[:half], axis=0, keepdims=True) / gates_ref[0:1, :]
        gate_ref[1:2, :] = jnp.sum(terms[half:], axis=0, keepdims=True) / gates_ref[1:2, :]


def combine(pick, gates, rows, feat):
    count = pick.shape[1]
    block = column_block(feat)
    return pl.pallas_call(
        functools.partial(combine_kernel, feat, block),
        grid=(feat // block,),
        out_shape=[
            jax.ShapeDtypeStruct((count, feat), BF16),
            jax.ShapeDtypeStruct((2, count), F32),
        ],
        in_specs=[VMEM] * 3,
        out_specs=[
            pl.BlockSpec((count, block), lambda i: (0, i)),
            pl.BlockSpec((2, count), lambda i: (0, 0)),
        ],
        cost_estimate=pl.CostEstimate(flops=10**8, bytes_accessed=10**6, transcendentals=0),
        name="combine",
    )(*[keep(a) for a in (pick, gates, rows)])


def per_device(tokens, cotangent, gates, expert_ids, w_gate, w_up, w_down):
    experts = lax.axis_size("dp")
    shards = lax.axis_size("expert")
    me = lax.axis_index("expert")
    rows = experts * CAP
    feat = tokens.shape[1]
    ids_t = expert_ids.T
    gates_t = gates.T
    me_ref = me.reshape(1)
    slots, pick, gates_f = pack(ids_t, gates_t, tokens, cotangent, experts)
    slots = lax.all_to_all(slots, "dp", split_axis=0, concat_axis=0, tiled=True)
    x = gather_far(slots[:, :CAP].reshape(rows, feat), "expert")
    d = gather_far(slots[:, CAP:].reshape(rows, feat), "expert")
    weights = [w_gate[0], w_up[0], w_down[0]]
    if feat % LANES or shards < 4:
        x, d = gather_near(x, "expert"), gather_near(d, "expert")
        x = [jnp.concatenate(reorder(x, me), axis=1)]
        d = [jnp.concatenate(reorder(d, me), axis=1)]
        weights = load(slots, *weights)
        sums = early([0], me_ref * 0, x, d, weights)
        odd = []
    else:
        x[1], d[1] = swap(x[0], "expert", 1), swap(d[0], "expert", 1)
        weights, sums = load_early(x[0], d[0], weights, slots)
        even = list(range(2, shards, 2))
        odd = list(range(3, shards, 2))
        rest, sums = lax.optimization_barrier(([x[i] for i in even], sums))
        for i, x_i in zip(even, rest):
            x[i], x[i + 1] = x_i, swap(x_i, "expert", 1)
        rels = [1] + even
        more = partial(partial_x_kernel, 2, rels, me_ref, sums[0], [x[1]] + rest, weights)
        rest, more = lax.optimization_barrier(([d[i] for i in even], more))
        for i, d_i in zip(even, rest):
            d[i], d[i + 1] = d_i, swap(d_i, "expert", 1)
        more = [*more, *partial(partial_d_kernel, 1, rels, me_ref, more[0], [d[1]] + rest, weights)]
        x, d = [x[i] for i in range(shards)], [d[i] for i in range(shards)]
        sums = [*sums, *more]
    hidden, d_gate, d_up, cols, *sent = late(
        odd, me_ref, [x[i] for i in odd], [d[i] for i in odd], weights, sums, feat
    )

    def term(pieces, after):
        return terms(pieces, me_ref, after, d_gate, d_up, cols, *weights[:2], feat) if pieces else []

    start = (keep(cols), keep(cols))
    if not odd:
        sent = term([(rel, 0, feat) for rel in range(3, shards, 2)], start)
    arrived = [swap(part, "expert", 1) for part in sent]
    even = list(range(2, shards, 2))
    kept = term([(rel, 0, feat) for rel in even], start)
    held = {rel: add(part, more) for rel, part, more in zip(even, kept, arrived)}
    last = held[max(held)] if held else cols
    wide = feat * shards
    other = sum_far(held, "expert")
    half = feat // (2 * LANES) * LANES
    pieces = ([(1, 0, feat)] if shards > 1 else []) + [(0, 0, half)]
    grad_down, *sent, first = middle(
        hidden, d, last, wide // 8, pieces, me_ref, d_gate, d_up, cols, *weights[:2], feat
    )
    down_done = pltpu.with_memory_space_constraint(grad_down, pltpu.HBM)
    parts = [swap(part, "expert", 1) for part in sent]
    parts += [] if other is None else [other]
    second, = term([(0, half, feat)], (keep(parts[-1] if parts else cols), down_done))
    total = settle([first, second], parts, grad_down)
    got = lax.all_to_all(total, "dp", split_axis=0, concat_axis=0, tiled=True)
    got = got.reshape(rows, feat + LANES)
    grad_gate, grad_up = outer_rows(x, (d_gate, d_up), total, wide // 16)
    grad_tokens, gate_grads = combine(pick, gates_f, got, feat)
    return (grad_tokens, gate_grads.T, grad_gate[None], grad_up[None], grad_down[None])


def solution(mesh):
    in_specs = (
        P("dp", "expert"),
        P("dp", "expert"),
        P("dp", None),
        P("dp", None),
        P("dp", None, "expert"),
        P("dp", None, "expert"),
        P("dp", "expert", None),
    )
    out_specs = (
        P("dp", "expert"),
        P("dp", None),
        P("dp", None, "expert"),
        P("dp", None, "expert"),
        P("dp", "expert", None),
    )
    return jax.shard_map(
        per_device, mesh=mesh, in_specs=in_specs, out_specs=out_specs, check_vma=False
    )
```

```python
import functools
import math

import jax
import jax.numpy as jnp
from jax import lax
from jax.experimental import pallas as pl
from jax.experimental.pallas import tpu as pltpu
from jax.sharding import PartitionSpec as P

CAP = 8
LANES = 128
F32 = jnp.float32
BF16 = jnp.bfloat16
VMEM = pl.BlockSpec(memory_space=pltpu.VMEM)
SMEM = pl.BlockSpec(memory_space=pltpu.SMEM)


def keep(array):
    return pltpu.with_memory_space_constraint(array, pltpu.VMEM)


def swap(value, axis, mask):
    size = lax.axis_size(axis)
    return lax.ppermute(value, axis, [(i, i ^ mask) for i in range(size)])


def reorder(shards, me):
    size = len(shards)
    mask = 1
    while mask < size:
        flip = (me & mask) != 0
        shards = [jnp.where(flip, shards[i ^ mask], shards[i]) for i in range(size)]
        mask *= 2
    return shards


def gather_far(own, axis):
    size = lax.axis_size(axis)
    held = {0: own}
    mask = size // 2
    while mask > 1:
        for rel in list(held):
            held[rel ^ mask] = swap(held[rel], axis, mask)
        mask //= 2
    return held


def gather_near(held, axis):
    size = lax.axis_size(axis)
    if size > 1:
        held = {**held, **{rel ^ 1: swap(held[rel], axis, 1) for rel in held}}
    return [held[i] for i in range(size)]


def gather_shards(own, axis):
    return gather_near(gather_far(own, axis), axis)


def add(held, arrived):
    return (held.astype(F32) + arrived.astype(F32)).astype(BF16)


def sum_far(held, axis):
    size = lax.axis_size(axis)
    total = None
    mask = 2
    while mask < size:
        arrived = {rel ^ mask: swap(held.pop(rel), axis, mask) for rel in list(held) if rel & mask}
        for rel, value in arrived.items():
            if rel:
                held[rel] = add(held[rel], value)
            else:
                total = value if total is None else add(total, value)
        mask *= 2
    return total


def one_hot(ids, gates, expert, experts):
    rows, tokens = expert.shape
    row = lax.broadcasted_iota(jnp.int32, (rows, tokens), 0)
    low = expert < experts // 2
    member = jnp.where(low, ids[0:1, :], ids[1:2, :]) == expert
    gate = jnp.where(low, gates[0:1, :], gates[1:2, :])
    earlier = lax.broadcasted_iota(jnp.int32, (tokens, tokens), 0) < lax.broadcasted_iota(
        jnp.int32, (tokens, tokens), 1
    )
    before = jnp.dot(
        member.astype(F32).astype(BF16), earlier.astype(F32).astype(BF16), preferred_element_type=F32
    )
    pick = jnp.logical_and(member, before == (row & (CAP - 1)).astype(F32))
    return jnp.where(pick, 1.0, 0.0), jnp.where(pick, gate, 0.0)


def row_blocks(experts, tokens):
    return lax.broadcasted_iota(jnp.int32, (experts * CAP, tokens), 0) // CAP


def column_block(feat):
    return feat // 2 if feat % (2 * LANES) == 0 else feat


def pack_kernel(
    experts, block, ids_hbm, gates_hbm, x_hbm, d_hbm, slot_hbm, pick_out, gates_out, ids, gates_low, x_ref, d_ref, slots, sems
):
    feat = x_ref.shape[1]
    steps = feat // block

    def columns(step):
        return slice(step * block, (step + 1) * block)

    small = [
        pltpu.make_async_copy(ids_hbm, ids, sems.at[3, 0]),
        pltpu.make_async_copy(gates_hbm, gates_low, sems.at[4, 0]),
    ]
    loads = [
        [
            pltpu.make_async_copy(src.at[:, columns(step)], dst.at[:, columns(step)], sems.at[i, step])
            for i, (src, dst) in enumerate(((x_hbm, x_ref), (d_hbm, d_ref)))
        ]
        for step in range(steps)
    ]
    stores = [
        pltpu.make_async_copy(
            slots.at[:, :, columns(step)], slot_hbm.at[:, :, columns(step)], sems.at[2, step]
        )
        for step in range(steps)
    ]
    for copy in small + [copy for pair in loads for copy in pair]:
        copy.start()
    for copy in small:
        copy.wait()
    gates = gates_low[...].astype(F32)
    pick, pick_gate = one_hot(ids[...], gates, row_blocks(experts, ids.shape[1]), experts)
    pick, pick_gate = pick.astype(BF16), pick_gate.astype(BF16)
    for step in range(steps):
        for copy in loads[step]:
            copy.wait()
        slot_x = jnp.dot(pick, x_ref[:, columns(step)], preferred_element_type=F32)
        slot_d = jnp.dot(pick_gate, d_ref[:, columns(step)], preferred_element_type=F32)
        for i in range(experts):
            slots[i, :, columns(step)] = jnp.concatenate(
                [slot_x[i * CAP:(i + 1) * CAP], slot_d[i * CAP:(i + 1) * CAP]], axis=0
            ).astype(BF16)
        stores[step].start()
    pick_out[...] = pick
    gates_out[...] = gates
    for copy in stores:
        copy.wait()


def pack(ids, gates, tokens, cotangent, experts):
    count, feat = tokens.shape
    block = column_block(feat)
    steps = feat // block
    rows = experts * CAP
    hbm = pl.BlockSpec(memory_space=pltpu.HBM)
    return pl.pallas_call(
        functools.partial(pack_kernel, experts, block),
        out_shape=[
            jax.ShapeDtypeStruct((experts, 2 * CAP, feat), BF16),
            jax.ShapeDtypeStruct((rows, count), BF16),
            jax.ShapeDtypeStruct((2, count), F32),
        ],
        in_specs=[hbm] * 4,
        out_specs=[hbm, VMEM, VMEM],
        scratch_shapes=[
            pltpu.VMEM((2, count), jnp.int32),
            pltpu.VMEM((2, count), BF16),
            pltpu.VMEM((count, feat), BF16),
            pltpu.VMEM((count, feat), BF16),
            pltpu.VMEM((experts, 2 * CAP, feat), BF16),
            pltpu.SemaphoreType.DMA((5, steps)),
        ],
        cost_estimate=pl.CostEstimate(flops=10**8, bytes_accessed=2 * 10**6, transcendentals=0),
        compiler_params=pltpu.CompilerParams(vmem_limit_bytes=2**23),
        name="pack",
    )(*[pltpu.with_memory_space_constraint(a, pltpu.HBM) for a in (ids, gates, tokens, cotangent)])


def load_kernel(count, *refs):
    sems = refs[-1]
    copies = [
        pltpu.make_async_copy(refs[i], refs[count + 1 + i], sems.at[i]) for i in range(count)
    ]
    for copy in copies:
        copy.start()
    for copy in copies:
        copy.wait()


def load(after, *arrays):
    count = len(arrays)
    total = sum(a.size * a.dtype.itemsize for a in arrays)
    return pl.pallas_call(
        functools.partial(load_kernel, count),
        out_shape=[pltpu.VMEM(a.shape, a.dtype) for a in arrays],
        in_specs=[pl.BlockSpec(memory_space=pltpu.HBM)] * count + [pl.BlockSpec(memory_space=pl.ANY)],
        out_specs=[VMEM] * count,
        scratch_shapes=[pltpu.SemaphoreType.DMA((count,))],
        cost_estimate=pl.CostEstimate(flops=0, bytes_accessed=total, transcendentals=0),
        compiler_params=pltpu.CompilerParams(vmem_limit_bytes=2**22),
        name="load",
    )(*[pltpu.with_memory_space_constraint(a, pltpu.HBM) for a in arrays], after)


def shard_at(me_ref, rel, feat):
    return pl.ds(pl.multiple_of((me_ref[0] ^ rel) * feat, feat), feat)


def products(rels, me_ref, x_refs, d_refs, gate_ref, up_ref, down_ref):
    feat = x_refs[0].shape[1]
    totals = None
    for rel, x_ref, d_ref in zip(rels, x_refs, d_refs):
        at = shard_at(me_ref, rel, feat)
        parts = (
            jnp.dot(x_ref[...], gate_ref[at, :], preferred_element_type=F32),
            jnp.dot(x_ref[...], up_ref[at, :], preferred_element_type=F32),
            lax.dot_general(
                d_ref[...], down_ref[:, at], (((1,), (1,)), ((), ())), preferred_element_type=F32
            ),
        )
        totals = parts if totals is None else tuple(a + b for a, b in zip(totals, parts))
    return totals


def early_kernel(rels, me_ref, *refs):
    count = len(rels)
    x_refs, d_refs, (gate_ref, up_ref, down_ref) = refs[:count], refs[count:2 * count], refs[2 * count:-3]
    totals = products(rels, me_ref, x_refs, d_refs, gate_ref, up_ref, down_ref)
    for out, value in zip(refs[-3:], totals):
        out[...] = value


def early(rels, me, x, d, weights):
    rows, units = x[0].shape[0], weights[0].shape[1]
    work = 6 * rows * units * x[0].shape[1] * len(rels)
    return pl.pallas_call(
        functools.partial(early_kernel, rels),
        out_shape=[jax.ShapeDtypeStruct((rows, units), F32)] * 3,
        in_specs=[SMEM] + [VMEM] * (2 * len(rels) + 3),
        out_specs=[VMEM] * 3,
        cost_estimate=pl.CostEstimate(flops=work, bytes_accessed=work // rows, transcendentals=0),
        compiler_params=pltpu.CompilerParams(vmem_limit_bytes=2**24),
        name="early",
    )(me, *[keep(a) for a in (*x, *d, *weights)])


def partial_x_kernel(rels, me_ref, after_ref, gate_ref, up_ref, down_ref, *refs):
    x_refs, outs = refs[:-2], refs[-2:]
    feat = x_refs[0].shape[1]
    for weight_ref, out in zip((gate_ref, up_ref), outs):
        total = None
        for rel, x_ref in zip(rels, x_refs):
            part = jnp.dot(
                x_ref[...], weight_ref[shard_at(me_ref, rel, feat), :], preferred_element_type=F32
            )
            total = part if total is None else total + part
        out[...] = total


def partial_d_kernel(rels, me_ref, after_ref, gate_ref, up_ref, down_ref, *refs):
    d_refs, out = refs[:-1], refs[-1]
    feat = d_refs[0].shape[1]
    total = None
    for rel, d_ref in zip(rels, d_refs):
        part = lax.dot_general(
            d_ref[...],
            down_ref[:, shard_at(me_ref, rel, feat)],
            (((1,), (1,)), ((), ())),
            preferred_element_type=F32,
        )
        total = part if total is None else total + part
    out[...] = total


def partial(kernel, count, rels, me, after, arrays, weights):
    rows, units = arrays[0].shape[0], weights[0].shape[1]
    work = 2 * count * rows * units * arrays[0].shape[1] * len(rels)
    return pl.pallas_call(
        functools.partial(kernel, rels),
        out_shape=[jax.ShapeDtypeStruct((rows, units), F32)] * count,
        in_specs=[SMEM, pl.BlockSpec(memory_space=pl.ANY)] + [VMEM] * (3 + len(rels)),
        out_specs=[VMEM] * count,
        cost_estimate=pl.CostEstimate(flops=work, bytes_accessed=work // rows, transcendentals=0),
        compiler_params=pltpu.CompilerParams(vmem_limit_bytes=2**24),
        name="partial",
    )(me, keep(after), *[keep(a) for a in (*weights, *arrays)])


def flip(index, rel):
    mask = 1
    while mask <= rel:
        if rel & mask:
            index = index + mask * (1 - 2 * ((index // mask) % 2))
        mask *= 2
    return index


def load_early_kernel(x0, d0, gate_in, up_in, down_in, gate, up, down, *refs):
    sums, sems = refs[:3], refs[3]
    feat = x0.shape[1]
    me = lax.axis_index("expert")
    shards = gate.shape[0] // feat

    def place(rel):
        return pl.ds(pl.multiple_of(flip(me, rel) * feat, feat), feat)

    def copies(rel):
        at = place(rel)
        return [
            pltpu.make_async_copy(src.at[where], dst.at[where], sems.at[i, rel])
            for i, (src, dst, where) in enumerate(
                ((gate_in, gate, at), (up_in, up, at), (down_in, down, (slice(None), at)))
            )
        ]

    first, *rest = [copies(rel) for rel in range(shards)]
    for copy in first:
        copy.start()
    for group in rest:
        for copy in group:
            copy.start()
    at = place(0)
    for i in range(3):
        first[i].wait()
        if i < 2:
            sums[i][...] = jnp.dot(x0[...], (gate, up)[i][at, :], preferred_element_type=F32)
        else:
            sums[i][...] = lax.dot_general(
                d0[...], down[:, at], (((1,), (1,)), ((), ())), preferred_element_type=F32
            )
    for group in rest:
        for copy in group:
            copy.wait()


def load_early(x, d, weights, after):
    rows = x.shape[0]
    units = weights[0].shape[1]
    shards = lax.axis_size("expert")
    out = pl.pallas_call(
        lambda after_ref, *refs: load_early_kernel(*refs),
        out_shape=[pltpu.VMEM(a.shape, a.dtype) for a in weights]
        + [jax.ShapeDtypeStruct((rows, units), F32)] * 3,
        in_specs=[pl.BlockSpec(memory_space=pl.ANY)]
        + [VMEM] * 2
        + [pl.BlockSpec(memory_space=pltpu.HBM)] * 3,
        out_specs=[VMEM] * 6,
        scratch_shapes=[pltpu.SemaphoreType.DMA((3, shards))],
        cost_estimate=pl.CostEstimate(
            flops=6 * rows * units * x.shape[1],
            bytes_accessed=sum(a.size * 2 for a in weights),
            transcendentals=0,
        ),
        compiler_params=pltpu.CompilerParams(vmem_limit_bytes=2**23),
        name="load_early",
    )(
        keep(after),
        keep(x),
        keep(d),
        *[pltpu.with_memory_space_constraint(a, pltpu.HBM) for a in weights],
    )
    return out[:3], out[3:]


def late_kernel(rels, feat, me_ref, *refs):
    count = len(rels)
    x_refs, d_refs, refs = refs[:count], refs[count:2 * count], refs[2 * count:]
    refs, outs = refs[:-4 - count], refs[-4 - count:]
    (gate_ref, up_ref, down_ref), sum_refs = refs[:3], refs[3:]
    hidden_out, d_gate_out, d_up_out, cols_out = outs[:4]
    totals = [ref[...] for ref in sum_refs[:3]]
    for i, ref in enumerate(sum_refs[3:]):
        totals[i % 3] += ref[...]
    if rels:
        parts = products(rels, me_ref, x_refs, d_refs, gate_ref, up_ref, down_ref)
        totals = [a + b for a, b in zip(totals, parts)]
    pre_gate, pre_up, dhid = totals
    sig = 1.0 / (1.0 + jnp.exp(-pre_gate))
    act = pre_gate * sig
    hidden = (act * pre_up).astype(BF16)
    d_gate = (dhid * pre_up * sig * (1.0 + pre_gate * (1.0 - sig))).astype(BF16)
    d_up = (dhid * act).astype(BF16)
    total = jnp.sum(dhid * hidden.astype(F32), axis=1, keepdims=True)
    cols = jnp.broadcast_to(total, cols_out.shape).astype(BF16)
    for rel, out in zip(rels, outs[4:]):
        out[:, :feat] = term_piece(me_ref, rel, 0, feat, feat, d_gate, d_up, gate_ref, up_ref)
        out[:, feat:] = cols
    hidden_out[...] = hidden
    d_gate_out[...] = d_gate
    d_up_out[...] = d_up
    cols_out[...] = cols


def late(rels, me, x, d, weights, sums, feat):
    rows, units = sums[0].shape
    work = 10 * rows * units * feat * max(1, len(rels))
    return pl.pallas_call(
        functools.partial(late_kernel, rels, feat),
        out_shape=[jax.ShapeDtypeStruct((rows, units), BF16)] * 3
        + [jax.ShapeDtypeStruct((rows, LANES), BF16)]
        + [jax.ShapeDtypeStruct((rows, feat + LANES), BF16)] * len(rels),
        in_specs=[SMEM] + [VMEM] * (2 * len(rels) + 3 + len(sums)),
        out_specs=[VMEM] * (4 + len(rels)),
        cost_estimate=pl.CostEstimate(
            flops=work, bytes_accessed=work // rows, transcendentals=rows * units
        ),
        compiler_params=pltpu.CompilerParams(vmem_limit_bytes=2**24),
        name="late",
    )(me, *[keep(a) for a in (*x, *d, *weights, *sums)])


def term_piece(me_ref, rel, low, high, feat, d_gate, d_up, gate_ref, up_ref):
    dims = (((1,), (1,)), ((), ()))
    start = (me_ref[0] ^ rel) * feat + low
    at = pl.ds(pl.multiple_of(start, math.gcd(feat, low)), high - low)
    term = lax.dot_general(d_gate, gate_ref[at, :], dims, preferred_element_type=F32)
    term += lax.dot_general(d_up, up_ref[at, :], dims, preferred_element_type=F32)
    return term.astype(BF16)


def term_kernel(pieces, feat, me_ref, after_ref, last_ref, d_gate_ref, d_up_ref, cols_ref, gate_ref, up_ref, *outs):
    for (rel, low, high), out in zip(pieces, outs):
        out[:, :high - low] = term_piece(
            me_ref, rel, low, high, feat, d_gate_ref[...], d_up_ref[...], gate_ref, up_ref
        )
        if high == feat:
            out[:, high - low:] = cols_ref[...]


def terms(pieces, me, after, d_gate, d_up, cols, gate_m, up_m, feat):
    rows = d_gate.shape[0]
    return pl.pallas_call(
        functools.partial(term_kernel, pieces, feat),
        out_shape=[
            jax.ShapeDtypeStruct((rows, high - low + (LANES if high == feat else 0)), BF16)
            for rel, low, high in pieces
        ],
        in_specs=[SMEM] + [pl.BlockSpec(memory_space=pl.ANY)] * 2 + [VMEM] * 5,
        out_specs=[VMEM] * len(pieces),
        cost_estimate=pl.CostEstimate(flops=1, bytes_accessed=1, transcendentals=0),
        compiler_params=pltpu.CompilerParams(vmem_limit_bytes=2**24),
        name="terms",
    )(me, *after, *[keep(a) for a in (d_gate, d_up, cols, gate_m, up_m)])


SLOTS = 4


def stream(steps, fill, copies, beside=()):
    beside = list(beside)
    for step in range(steps + SLOTS):
        if step >= SLOTS:
            for copy in copies(step - SLOTS, step % SLOTS):
                copy.wait()
        if step < steps:
            fill(step, step % SLOTS)
            for copy in copies(step, step % SLOTS):
                copy.start()
            if steps - step <= len(beside):
                beside[step - steps]()


def product(left, right, out):
    for j in range(0, right.shape[1], 256):
        part = right[:, j:j + 256]
        for i in range(0, left.shape[0], 128):
            out[i:i + 128, j:j + 256] = jnp.dot(
                left[i:i + 128], part, preferred_element_type=F32
            ).astype(BF16)


def places(feat, shards, block):
    me = lax.axis_index("expert") if shards > 1 else 0

    def place(step):
        rel, part = divmod(step, feat // block)
        start = flip(me, rel) * feat + part * block
        return pl.ds(pl.multiple_of(start, block) if shards > 1 else start, block)

    def source(step):
        rel, part = divmod(step, feat // block)
        return rel, slice(part * block, (part + 1) * block)

    return shards * feat // block, source, place


def outer_rows_kernel(block, shards, after_ref, *refs):
    stage, sems = refs[-2:]
    lefts, refs = refs[:shards], refs[shards:-2]
    half = len(refs) // 2
    rights, outs = refs[:half], refs[half:]
    steps, source, place = places(lefts[0].shape[1], shards, block)

    def fill(step, slot):
        rel, at = source(step)
        left = lefts[rel][:, at].astype(F32).T.astype(BF16)
        for i, right in enumerate(rights):
            product(left, right, stage.at[slot, i])

    def copies(step, slot):
        return [
            pltpu.make_async_copy(stage.at[slot, i], out.at[place(step)], sems.at[slot, i])
            for i, out in enumerate(outs)
        ]

    stream(steps, fill, copies)


def outer_rows(lefts, rights, after, block):
    rows, feat = lefts[0].shape
    tall = feat * len(lefts)
    narrow = rights[0].shape[1]
    count = len(rights)
    return pl.pallas_call(
        functools.partial(outer_rows_kernel, block, len(lefts)),
        out_shape=[jax.ShapeDtypeStruct((tall, narrow), BF16)] * count,
        in_specs=[pl.BlockSpec(memory_space=pl.ANY)] + [VMEM] * (len(lefts) + count),
        out_specs=[pl.BlockSpec(memory_space=pltpu.HBM)] * count,
        scratch_shapes=[
            pltpu.VMEM((SLOTS, count, block, narrow), BF16),
            pltpu.SemaphoreType.DMA((SLOTS, count)),
        ],
        cost_estimate=pl.CostEstimate(
            flops=2 * rows * tall * narrow * count,
            bytes_accessed=2 * tall * narrow * count,
            transcendentals=0,
        ),
        compiler_params=pltpu.CompilerParams(vmem_limit_bytes=2**24),
        name="outer_rows",
    )(pltpu.with_memory_space_constraint(after, pltpu.HBM), *[keep(a) for a in (*lefts, *rights)])


def middle_kernel(
    block, pieces, feat, me_ref, after_ref, left_ref, d_gate_ref, d_up_ref, cols_ref, gate_ref, up_ref, *refs
):
    outs, (turned, stage, sems) = refs[-4 - len(pieces):-3], refs[-3:]
    rights, out_ref, outs = refs[:-4 - len(pieces)], outs[0], outs[1:]
    turned[...] = left_ref[...].astype(F32).T.astype(BF16)
    steps, source, place = places(rights[0].shape[1], len(rights), block)

    def fill(step, slot):
        rel, at = source(step)
        product(turned, rights[rel].at[:, at], stage.at[slot])

    def copies(step, slot):
        return [pltpu.make_async_copy(stage.at[slot], out_ref.at[:, place(step)], sems.at[slot])]

    def term(piece, out):
        rel, low, high = piece
        out[:, :high - low] = term_piece(
            me_ref, rel, low, high, feat, d_gate_ref[...], d_up_ref[...], gate_ref, up_ref
        )
        if high == feat:
            out[:, high - low:] = cols_ref[...]

    stream(steps, fill, copies, [functools.partial(term, *pair) for pair in zip(pieces, outs)])


def middle(left, rights, after, block, pieces, me, d_gate, d_up, cols, gate_m, up_m, feat):
    rows = left.shape[0]
    wide = rights[0].shape[1] * len(rights)
    tall = left.shape[1]
    return pl.pallas_call(
        functools.partial(middle_kernel, block, pieces, feat),
        out_shape=[jax.ShapeDtypeStruct((tall, wide), BF16)]
        + [
            jax.ShapeDtypeStruct((rows, high - low + (LANES if high == feat else 0)), BF16)
            for rel, low, high in pieces
        ],
        in_specs=[SMEM, pl.BlockSpec(memory_space=pl.ANY)] + [VMEM] * (6 + len(rights)),
        out_specs=[pl.BlockSpec(memory_space=pltpu.HBM)] + [VMEM] * len(pieces),
        scratch_shapes=[
            pltpu.VMEM((tall, rows), BF16),
            pltpu.VMEM((SLOTS, tall, block), BF16),
            pltpu.SemaphoreType.DMA((SLOTS,)),
        ],
        cost_estimate=pl.CostEstimate(
            flops=4 * rows * wide * tall, bytes_accessed=2 * wide * tall, transcendentals=0
        ),
        compiler_params=pltpu.CompilerParams(vmem_limit_bytes=2**24),
        name="middle",
    )(me, keep(after), *[keep(a) for a in (left, d_gate, d_up, cols, gate_m, up_m, *rights)])


def settle_kernel(count, *refs):
    pieces, parts, out_ref = refs[:count], refs[count:-2], refs[-1]
    low = 0
    for piece in pieces:
        at = slice(low, low + piece.shape[1])
        total = piece[...].astype(F32)
        for ref in parts:
            total += ref[:, at].astype(F32)
        for i in range(out_ref.shape[0]):
            out_ref[i, :, at] = total[i * CAP:(i + 1) * CAP].astype(BF16)
        low += piece.shape[1]


def settle(pieces, parts, after):
    rows = pieces[0].shape[0]
    wide = sum(a.shape[1] for a in pieces)
    return pl.pallas_call(
        functools.partial(settle_kernel, len(pieces)),
        out_shape=jax.ShapeDtypeStruct((rows // CAP, CAP, wide), BF16),
        in_specs=[VMEM] * (len(pieces) + len(parts)) + [pl.BlockSpec(memory_space=pl.ANY)],
        out_specs=VMEM,
        cost_estimate=pl.CostEstimate(flops=0, bytes_accessed=10**6, transcendentals=0),
        name="settle",
    )(*[keep(a) for a in (*pieces, *parts)], pltpu.with_memory_space_constraint(after, pltpu.HBM))


def combine_kernel(feat, block, pick_ref, gates_ref, rows_ref, grad_ref, gate_ref):
    pick = pick_ref[...]
    at = pl.ds(pl.multiple_of(pl.program_id(0) * block, block), block) if block < feat else slice(0, feat)
    grad_ref[...] = lax.dot_general(
        pick, rows_ref[:, at], (((0,), (0,)), ((), ())), preferred_element_type=F32
    ).astype(BF16)

    @pl.when(pl.program_id(0) == 0)
    def _():
        half = pick.shape[0] // 2
        terms = pick.astype(F32) * rows_ref[:, feat:].astype(F32)
        gate_ref[0:1, :] = jnp.sum(terms[:half], axis=0, keepdims=True) / gates_ref[0:1, :]
        gate_ref[1:2, :] = jnp.sum(terms[half:], axis=0, keepdims=True) / gates_ref[1:2, :]


def combine(pick, gates, rows, feat):
    count = pick.shape[1]
    block = column_block(feat)
    return pl.pallas_call(
        functools.partial(combine_kernel, feat, block),
        grid=(feat // block,),
        out_shape=[
            jax.ShapeDtypeStruct((count, feat), BF16),
            jax.ShapeDtypeStruct((2, count), F32),
        ],
        in_specs=[VMEM] * 3,
        out_specs=[
            pl.BlockSpec((count, block), lambda i: (0, i)),
            pl.BlockSpec((2, count), lambda i: (0, 0)),
        ],
        cost_estimate=pl.CostEstimate(flops=10**8, bytes_accessed=10**6, transcendentals=0),
        name="combine",
    )(*[keep(a) for a in (pick, gates, rows)])


def per_device(tokens, cotangent, gates, expert_ids, w_gate, w_up, w_down):
    experts = lax.axis_size("dp")
    shards = lax.axis_size("expert")
    me = lax.axis_index("expert")
    rows = experts * CAP
    feat = tokens.shape[1]
    ids_t = expert_ids.T
    gates_t = gates.T
    me_ref = me.reshape(1)
    slots, pick, gates_f = pack(ids_t, gates_t, tokens, cotangent, experts)
    slots = lax.all_to_all(slots, "dp", split_axis=0, concat_axis=0, tiled=True)
    x = gather_far(slots[:, :CAP].reshape(rows, feat), "expert")
    d = gather_far(slots[:, CAP:].reshape(rows, feat), "expert")
    weights = [w_gate[0], w_up[0], w_down[0]]
    if feat % LANES or shards < 4:
        x, d = gather_near(x, "expert"), gather_near(d, "expert")
        x = [jnp.concatenate(reorder(x, me), axis=1)]
        d = [jnp.concatenate(reorder(d, me), axis=1)]
        weights = load(slots, *weights)
        sums = early([0], me_ref * 0, x, d, weights)
        odd = []
    else:
        x[1], d[1] = swap(x[0], "expert", 1), swap(d[0], "expert", 1)
        weights, sums = load_early(x[0], d[0], weights, slots)
        even = list(range(2, shards, 2))
        odd = list(range(3, shards, 2))
        rest, sums = lax.optimization_barrier(([x[i] for i in even], sums))
        for i, x_i in zip(even, rest):
            x[i], x[i + 1] = x_i, swap(x_i, "expert", 1)
        rels = [1] + even
        more = partial(partial_x_kernel, 2, rels, me_ref, sums[0], [x[1]] + rest, weights)
        rest, more = lax.optimization_barrier(([d[i] for i in even], more))
        for i, d_i in zip(even, rest):
            d[i], d[i + 1] = d_i, swap(d_i, "expert", 1)
        more = [*more, *partial(partial_d_kernel, 1, rels, me_ref, more[0], [d[1]] + rest, weights)]
        x, d = [x[i] for i in range(shards)], [d[i] for i in range(shards)]
        sums = [*sums, *more]
    hidden, d_gate, d_up, cols, *sent = late(
        odd, me_ref, [x[i] for i in odd], [d[i] for i in odd], weights, sums, feat
    )

    def term(pieces, after):
        return terms(pieces, me_ref, after, d_gate, d_up, cols, *weights[:2], feat) if pieces else []

    start = (keep(cols), keep(cols))
    if not odd:
        sent = term([(rel, 0, feat) for rel in range(3, shards, 2)], start)
    arrived = [swap(part, "expert", 1) for part in sent]
    even = list(range(2, shards, 2))
    kept = term([(rel, 0, feat) for rel in even], start)
    held = {rel: add(part, more) for rel, part, more in zip(even, kept, arrived)}
    last = held[max(held)] if held else cols
    wide = feat * shards
    other = sum_far(held, "expert")
    half = max(LANES, (feat - 2 * LANES) // LANES * LANES)
    pieces = ([(1, 0, feat)] if shards > 1 else []) + [(0, 0, half)]
    grad_down, *sent, first = middle(
        hidden, d, last, wide // 8, pieces, me_ref, d_gate, d_up, cols, *weights[:2], feat
    )
    down_done = pltpu.with_memory_space_constraint(grad_down, pltpu.HBM)
    parts = [swap(part, "expert", 1) for part in sent]
    parts += [] if other is None else [other]
    second, = term([(0, half, feat)], (keep(parts[-1] if parts else cols), down_done))
    total = settle([first, second], parts, grad_down)
    got = lax.all_to_all(total, "dp", split_axis=0, concat_axis=0, tiled=True)
    got = got.reshape(rows, feat + LANES)
    grad_gate, grad_up = outer_rows(x, (d_gate, d_up), total, wide // 16)
    grad_tokens, gate_grads = combine(pick, gates_f, got, feat)
    return (grad_tokens, gate_grads.T, grad_gate[None], grad_up[None], grad_down[None])


def solution(mesh):
    in_specs = (
        P("dp", "expert"),
        P("dp", "expert"),
        P("dp", None),
        P("dp", None),
        P("dp", None, "expert"),
        P("dp", None, "expert"),
        P("dp", "expert", None),
    )
    out_specs = (
        P("dp", "expert"),
        P("dp", None),
        P("dp", None, "expert"),
        P("dp", None, "expert"),
        P("dp", "expert", None),
    )
    return jax.shard_map(
        per_device, mesh=mesh, in_specs=in_specs, out_specs=out_specs, check_vma=False
    )
```

```python
import functools
import math

import jax
import jax.numpy as jnp
from jax import lax
from jax.experimental import pallas as pl
from jax.experimental.pallas import tpu as pltpu
from jax.sharding import PartitionSpec as P

CAP = 8
LANES = 128
F32 = jnp.float32
BF16 = jnp.bfloat16
VMEM = pl.BlockSpec(memory_space=pltpu.VMEM)
SMEM = pl.BlockSpec(memory_space=pltpu.SMEM)


def keep(array):
    return pltpu.with_memory_space_constraint(array, pltpu.VMEM)


def swap(value, axis, mask):
    size = lax.axis_size(axis)
    return lax.ppermute(value, axis, [(i, i ^ mask) for i in range(size)])


def reorder(shards, me):
    size = len(shards)
    mask = 1
    while mask < size:
        flip = (me & mask) != 0
        shards = [jnp.where(flip, shards[i ^ mask], shards[i]) for i in range(size)]
        mask *= 2
    return shards


def gather_far(own, axis):
    size = lax.axis_size(axis)
    held = {0: own}
    mask = size // 2
    while mask > 1:
        for rel in list(held):
            held[rel ^ mask] = swap(held[rel], axis, mask)
        mask //= 2
    return held


def gather_near(held, axis):
    size = lax.axis_size(axis)
    if size > 1:
        held = {**held, **{rel ^ 1: swap(held[rel], axis, 1) for rel in held}}
    return [held[i] for i in range(size)]


def gather_shards(own, axis):
    return gather_near(gather_far(own, axis), axis)


def add(held, arrived):
    return (held.astype(F32) + arrived.astype(F32)).astype(BF16)


def sum_far(held, axis):
    size = lax.axis_size(axis)
    total = None
    mask = 2
    while mask < size:
        arrived = {rel ^ mask: swap(held.pop(rel), axis, mask) for rel in list(held) if rel & mask}
        for rel, value in arrived.items():
            if rel:
                held[rel] = add(held[rel], value)
            else:
                total = value if total is None else add(total, value)
        mask *= 2
    return total


def one_hot(ids, gates, expert, experts):
    rows, tokens = expert.shape
    row = lax.broadcasted_iota(jnp.int32, (rows, tokens), 0)
    low = expert < experts // 2
    member = jnp.where(low, ids[0:1, :], ids[1:2, :]) == expert
    gate = jnp.where(low, gates[0:1, :], gates[1:2, :])
    earlier = lax.broadcasted_iota(jnp.int32, (tokens, tokens), 0) < lax.broadcasted_iota(
        jnp.int32, (tokens, tokens), 1
    )
    before = jnp.dot(
        member.astype(F32).astype(BF16), earlier.astype(F32).astype(BF16), preferred_element_type=F32
    )
    pick = jnp.logical_and(member, before == (row & (CAP - 1)).astype(F32))
    return jnp.where(pick, 1.0, 0.0), jnp.where(pick, gate, 0.0)


def owner_order(experts):
    places = experts // 2
    near = sorted(range(places), key=lambda place: abs(2 * place - places + 1))
    return [2 * place + last for place in near for last in range(2)]


def row_owners(experts, tokens):
    block = lax.broadcasted_iota(jnp.int32, (experts * CAP, tokens), 0) // CAP
    owner = jnp.zeros_like(block)
    for i, expert in enumerate(owner_order(experts)):
        owner = jnp.where(block == i, expert, owner)
    return owner


def exchange(blocks, axis):
    groups = [owner_order(lax.axis_size(axis))]
    return lax.all_to_all(
        blocks, axis, split_axis=0, concat_axis=0, axis_index_groups=groups, tiled=True
    )


def column_block(feat):
    return feat // 2 if feat % (2 * LANES) == 0 else feat


def pack_kernel(
    experts, block, ids_hbm, gates_hbm, x_hbm, d_hbm, slot_hbm, pick_out, gates_out, ids, gates_low, x_ref, d_ref, slots, sems
):
    feat = x_ref.shape[1]
    steps = feat // block

    def columns(step):
        return slice(step * block, (step + 1) * block)

    small = [
        pltpu.make_async_copy(ids_hbm, ids, sems.at[3, 0]),
        pltpu.make_async_copy(gates_hbm, gates_low, sems.at[4, 0]),
    ]
    loads = [
        [
            pltpu.make_async_copy(src.at[:, columns(step)], dst.at[:, columns(step)], sems.at[i, step])
            for i, (src, dst) in enumerate(((x_hbm, x_ref), (d_hbm, d_ref)))
        ]
        for step in range(steps)
    ]
    stores = [
        pltpu.make_async_copy(
            slots.at[:, :, columns(step)], slot_hbm.at[:, :, columns(step)], sems.at[2, step]
        )
        for step in range(steps)
    ]
    for copy in small + [copy for pair in loads for copy in pair]:
        copy.start()
    for copy in small:
        copy.wait()
    gates = gates_low[...].astype(F32)
    pick, pick_gate = one_hot(ids[...], gates, row_owners(experts, ids.shape[1]), experts)
    pick, pick_gate = pick.astype(BF16), pick_gate.astype(BF16)
    for step in range(steps):
        for copy in loads[step]:
            copy.wait()
        slot_x = jnp.dot(pick, x_ref[:, columns(step)], preferred_element_type=F32)
        slot_d = jnp.dot(pick_gate, d_ref[:, columns(step)], preferred_element_type=F32)
        for i in range(experts):
            slots[i, :, columns(step)] = jnp.concatenate(
                [slot_x[i * CAP:(i + 1) * CAP], slot_d[i * CAP:(i + 1) * CAP]], axis=0
            ).astype(BF16)
        stores[step].start()
    pick_out[...] = pick
    gates_out[...] = gates
    for copy in stores:
        copy.wait()


def pack(ids, gates, tokens, cotangent, experts):
    count, feat = tokens.shape
    block = column_block(feat)
    steps = feat // block
    rows = experts * CAP
    hbm = pl.BlockSpec(memory_space=pltpu.HBM)
    return pl.pallas_call(
        functools.partial(pack_kernel, experts, block),
        out_shape=[
            jax.ShapeDtypeStruct((experts, 2 * CAP, feat), BF16),
            jax.ShapeDtypeStruct((rows, count), BF16),
            jax.ShapeDtypeStruct((2, count), F32),
        ],
        in_specs=[hbm] * 4,
        out_specs=[hbm, VMEM, VMEM],
        scratch_shapes=[
            pltpu.VMEM((2, count), jnp.int32),
            pltpu.VMEM((2, count), BF16),
            pltpu.VMEM((count, feat), BF16),
            pltpu.VMEM((count, feat), BF16),
            pltpu.VMEM((experts, 2 * CAP, feat), BF16),
            pltpu.SemaphoreType.DMA((5, steps)),
        ],
        cost_estimate=pl.CostEstimate(flops=10**8, bytes_accessed=2 * 10**6, transcendentals=0),
        compiler_params=pltpu.CompilerParams(vmem_limit_bytes=2**23),
        name="pack",
    )(*[pltpu.with_memory_space_constraint(a, pltpu.HBM) for a in (ids, gates, tokens, cotangent)])


def load_kernel(count, *refs):
    sems = refs[-1]
    copies = [
        pltpu.make_async_copy(refs[i], refs[count + 1 + i], sems.at[i]) for i in range(count)
    ]
    for copy in copies:
        copy.start()
    for copy in copies:
        copy.wait()


def load(after, *arrays):
    count = len(arrays)
    total = sum(a.size * a.dtype.itemsize for a in arrays)
    return pl.pallas_call(
        functools.partial(load_kernel, count),
        out_shape=[pltpu.VMEM(a.shape, a.dtype) for a in arrays],
        in_specs=[pl.BlockSpec(memory_space=pltpu.HBM)] * count + [pl.BlockSpec(memory_space=pl.ANY)],
        out_specs=[VMEM] * count,
        scratch_shapes=[pltpu.SemaphoreType.DMA((count,))],
        cost_estimate=pl.CostEstimate(flops=0, bytes_accessed=total, transcendentals=0),
        compiler_params=pltpu.CompilerParams(vmem_limit_bytes=2**22),
        name="load",
    )(*[pltpu.with_memory_space_constraint(a, pltpu.HBM) for a in arrays], after)


def shard_at(me_ref, rel, feat):
    return pl.ds(pl.multiple_of((me_ref[0] ^ rel) * feat, feat), feat)


def products(rels, me_ref, x_refs, d_refs, gate_ref, up_ref, down_ref):
    feat = x_refs[0].shape[1]
    totals = None
    for rel, x_ref, d_ref in zip(rels, x_refs, d_refs):
        at = shard_at(me_ref, rel, feat)
        parts = (
            jnp.dot(x_ref[...], gate_ref[at, :], preferred_element_type=F32),
            jnp.dot(x_ref[...], up_ref[at, :], preferred_element_type=F32),
            lax.dot_general(
                d_ref[...], down_ref[:, at], (((1,), (1,)), ((), ())), preferred_element_type=F32
            ),
        )
        totals = parts if totals is None else tuple(a + b for a, b in zip(totals, parts))
    return totals


def early_kernel(rels, me_ref, *refs):
    count = len(rels)
    x_refs, d_refs, (gate_ref, up_ref, down_ref) = refs[:count], refs[count:2 * count], refs[2 * count:-3]
    totals = products(rels, me_ref, x_refs, d_refs, gate_ref, up_ref, down_ref)
    for out, value in zip(refs[-3:], totals):
        out[...] = value


def early(rels, me, x, d, weights):
    rows, units = x[0].shape[0], weights[0].shape[1]
    work = 6 * rows * units * x[0].shape[1] * len(rels)
    return pl.pallas_call(
        functools.partial(early_kernel, rels),
        out_shape=[jax.ShapeDtypeStruct((rows, units), F32)] * 3,
        in_specs=[SMEM] + [VMEM] * (2 * len(rels) + 3),
        out_specs=[VMEM] * 3,
        cost_estimate=pl.CostEstimate(flops=work, bytes_accessed=work // rows, transcendentals=0),
        compiler_params=pltpu.CompilerParams(vmem_limit_bytes=2**24),
        name="early",
    )(me, *[keep(a) for a in (*x, *d, *weights)])


def partial_x_kernel(rels, me_ref, after_ref, gate_ref, up_ref, down_ref, *refs):
    x_refs, outs = refs[:-2], refs[-2:]
    feat = x_refs[0].shape[1]
    for weight_ref, out in zip((gate_ref, up_ref), outs):
        total = None
        for rel, x_ref in zip(rels, x_refs):
            part = jnp.dot(
                x_ref[...], weight_ref[shard_at(me_ref, rel, feat), :], preferred_element_type=F32
            )
            total = part if total is None else total + part
        out[...] = total


def partial_d_kernel(rels, me_ref, after_ref, gate_ref, up_ref, down_ref, *refs):
    d_refs, out = refs[:-1], refs[-1]
    feat = d_refs[0].shape[1]
    total = None
    for rel, d_ref in zip(rels, d_refs):
        part = lax.dot_general(
            d_ref[...],
            down_ref[:, shard_at(me_ref, rel, feat)],
            (((1,), (1,)), ((), ())),
            preferred_element_type=F32,
        )
        total = part if total is None else total + part
    out[...] = total


def partial(kernel, count, rels, me, after, arrays, weights):
    rows, units = arrays[0].shape[0], weights[0].shape[1]
    work = 2 * count * rows * units * arrays[0].shape[1] * len(rels)
    return pl.pallas_call(
        functools.partial(kernel, rels),
        out_shape=[jax.ShapeDtypeStruct((rows, units), F32)] * count,
        in_specs=[SMEM, pl.BlockSpec(memory_space=pl.ANY)] + [VMEM] * (3 + len(rels)),
        out_specs=[VMEM] * count,
        cost_estimate=pl.CostEstimate(flops=work, bytes_accessed=work // rows, transcendentals=0),
        compiler_params=pltpu.CompilerParams(vmem_limit_bytes=2**24),
        name="partial",
    )(me, keep(after), *[keep(a) for a in (*weights, *arrays)])


def flip(index, rel):
    mask = 1
    while mask <= rel:
        if rel & mask:
            index = index + mask * (1 - 2 * ((index // mask) % 2))
        mask *= 2
    return index


def load_early_kernel(x0, d0, gate_in, up_in, down_in, gate, up, down, *refs):
    sums, sems = refs[:3], refs[3]
    feat = x0.shape[1]
    me = lax.axis_index("expert")
    shards = gate.shape[0] // feat

    def place(rel):
        return pl.ds(pl.multiple_of(flip(me, rel) * feat, feat), feat)

    def copies(rel):
        at = place(rel)
        return [
            pltpu.make_async_copy(src.at[where], dst.at[where], sems.at[i, rel])
            for i, (src, dst, where) in enumerate(
                ((gate_in, gate, at), (up_in, up, at), (down_in, down, (slice(None), at)))
            )
        ]

    first, *rest = [copies(rel) for rel in range(shards)]
    for copy in first:
        copy.start()
    for group in rest:
        for copy in group:
            copy.start()
    at = place(0)
    for i in range(3):
        first[i].wait()
        if i < 2:
            sums[i][...] = jnp.dot(x0[...], (gate, up)[i][at, :], preferred_element_type=F32)
        else:
            sums[i][...] = lax.dot_general(
                d0[...], down[:, at], (((1,), (1,)), ((), ())), preferred_element_type=F32
            )
    for group in rest:
        for copy in group:
            copy.wait()


def load_early(x, d, weights, after):
    rows = x.shape[0]
    units = weights[0].shape[1]
    shards = lax.axis_size("expert")
    out = pl.pallas_call(
        lambda after_ref, *refs: load_early_kernel(*refs),
        out_shape=[pltpu.VMEM(a.shape, a.dtype) for a in weights]
        + [jax.ShapeDtypeStruct((rows, units), F32)] * 3,
        in_specs=[pl.BlockSpec(memory_space=pl.ANY)]
        + [VMEM] * 2
        + [pl.BlockSpec(memory_space=pltpu.HBM)] * 3,
        out_specs=[VMEM] * 6,
        scratch_shapes=[pltpu.SemaphoreType.DMA((3, shards))],
        cost_estimate=pl.CostEstimate(
            flops=6 * rows * units * x.shape[1],
            bytes_accessed=sum(a.size * 2 for a in weights),
            transcendentals=0,
        ),
        compiler_params=pltpu.CompilerParams(vmem_limit_bytes=2**23),
        name="load_early",
    )(
        keep(after),
        keep(x),
        keep(d),
        *[pltpu.with_memory_space_constraint(a, pltpu.HBM) for a in weights],
    )
    return out[:3], out[3:]


def late_kernel(rels, feat, me_ref, *refs):
    count = len(rels)
    x_refs, d_refs, refs = refs[:count], refs[count:2 * count], refs[2 * count:]
    refs, outs = refs[:-4 - count], refs[-4 - count:]
    (gate_ref, up_ref, down_ref), sum_refs = refs[:3], refs[3:]
    hidden_out, d_gate_out, d_up_out, cols_out = outs[:4]
    totals = [ref[...] for ref in sum_refs[:3]]
    for i, ref in enumerate(sum_refs[3:]):
        totals[i % 3] += ref[...]
    if rels:
        parts = products(rels, me_ref, x_refs, d_refs, gate_ref, up_ref, down_ref)
        totals = [a + b for a, b in zip(totals, parts)]
    pre_gate, pre_up, dhid = totals
    sig = 1.0 / (1.0 + jnp.exp(-pre_gate))
    act = pre_gate * sig
    hidden = (act * pre_up).astype(BF16)
    d_gate = (dhid * pre_up * sig * (1.0 + pre_gate * (1.0 - sig))).astype(BF16)
    d_up = (dhid * act).astype(BF16)
    total = jnp.sum(dhid * hidden.astype(F32), axis=1, keepdims=True)
    cols = jnp.broadcast_to(total, cols_out.shape).astype(BF16)
    for rel, out in zip(rels, outs[4:]):
        out[:, :feat] = term_piece(me_ref, rel, 0, feat, feat, d_gate, d_up, gate_ref, up_ref)
        out[:, feat:] = cols
    hidden_out[...] = hidden
    d_gate_out[...] = d_gate
    d_up_out[...] = d_up
    cols_out[...] = cols


def late(rels, me, x, d, weights, sums, feat):
    rows, units = sums[0].shape
    work = 10 * rows * units * feat * max(1, len(rels))
    return pl.pallas_call(
        functools.partial(late_kernel, rels, feat),
        out_shape=[jax.ShapeDtypeStruct((rows, units), BF16)] * 3
        + [jax.ShapeDtypeStruct((rows, LANES), BF16)]
        + [jax.ShapeDtypeStruct((rows, feat + LANES), BF16)] * len(rels),
        in_specs=[SMEM] + [VMEM] * (2 * len(rels) + 3 + len(sums)),
        out_specs=[VMEM] * (4 + len(rels)),
        cost_estimate=pl.CostEstimate(
            flops=work, bytes_accessed=work // rows, transcendentals=rows * units
        ),
        compiler_params=pltpu.CompilerParams(vmem_limit_bytes=2**24),
        name="late",
    )(me, *[keep(a) for a in (*x, *d, *weights, *sums)])


def term_piece(me_ref, rel, low, high, feat, d_gate, d_up, gate_ref, up_ref):
    dims = (((1,), (1,)), ((), ()))
    start = (me_ref[0] ^ rel) * feat + low
    at = pl.ds(pl.multiple_of(start, math.gcd(feat, low)), high - low)
    term = lax.dot_general(d_gate, gate_ref[at, :], dims, preferred_element_type=F32)
    term += lax.dot_general(d_up, up_ref[at, :], dims, preferred_element_type=F32)
    return term.astype(BF16)


def term_kernel(pieces, feat, me_ref, after_ref, last_ref, d_gate_ref, d_up_ref, cols_ref, gate_ref, up_ref, *outs):
    for (rel, low, high), out in zip(pieces, outs):
        out[:, :high - low] = term_piece(
            me_ref, rel, low, high, feat, d_gate_ref[...], d_up_ref[...], gate_ref, up_ref
        )
        if high == feat:
            out[:, high - low:] = cols_ref[...]


def terms(pieces, me, after, d_gate, d_up, cols, gate_m, up_m, feat):
    rows = d_gate.shape[0]
    return pl.pallas_call(
        functools.partial(term_kernel, pieces, feat),
        out_shape=[
            jax.ShapeDtypeStruct((rows, high - low + (LANES if high == feat else 0)), BF16)
            for rel, low, high in pieces
        ],
        in_specs=[SMEM] + [pl.BlockSpec(memory_space=pl.ANY)] * 2 + [VMEM] * 5,
        out_specs=[VMEM] * len(pieces),
        cost_estimate=pl.CostEstimate(flops=1, bytes_accessed=1, transcendentals=0),
        compiler_params=pltpu.CompilerParams(vmem_limit_bytes=2**24),
        name="terms",
    )(me, *after, *[keep(a) for a in (d_gate, d_up, cols, gate_m, up_m)])


SLOTS = 4


def stream(steps, fill, copies, beside=()):
    beside = list(beside)
    for step in range(steps + SLOTS):
        if step >= SLOTS:
            for copy in copies(step - SLOTS, step % SLOTS):
                copy.wait()
        if step < steps:
            fill(step, step % SLOTS)
            for copy in copies(step, step % SLOTS):
                copy.start()
            if steps - step <= len(beside):
                beside[step - steps]()


def places(feat, shards, block):
    me = lax.axis_index("expert") if shards > 1 else 0

    def place(step):
        rel, part = divmod(step, feat // block)
        start = flip(me, rel) * feat + part * block
        return pl.ds(pl.multiple_of(start, block) if shards > 1 else start, block)

    def source(step):
        rel, part = divmod(step, feat // block)
        return rel, slice(part * block, (part + 1) * block)

    return shards * feat // block, source, place


def outer_rows_kernel(block, shards, after_ref, *refs):
    stage, sems = refs[-2:]
    lefts, refs = refs[:shards], refs[shards:-2]
    half = len(refs) // 2
    rights, outs = refs[:half], refs[half:]
    steps, source, place = places(lefts[0].shape[1], shards, block)

    def fill(step, slot):
        rel, at = source(step)
        left = lefts[rel][:, at].astype(F32).T.astype(BF16)
        for i, right in enumerate(rights):
            stage[slot, i] = jnp.dot(left, right[...], preferred_element_type=F32).astype(BF16)

    def copies(step, slot):
        return [
            pltpu.make_async_copy(stage.at[slot, i], out.at[place(step)], sems.at[slot, i])
            for i, out in enumerate(outs)
        ]

    stream(steps, fill, copies)


def outer_rows(lefts, rights, after, block):
    rows, feat = lefts[0].shape
    tall = feat * len(lefts)
    narrow = rights[0].shape[1]
    count = len(rights)
    return pl.pallas_call(
        functools.partial(outer_rows_kernel, block, len(lefts)),
        out_shape=[jax.ShapeDtypeStruct((tall, narrow), BF16)] * count,
        in_specs=[pl.BlockSpec(memory_space=pl.ANY)] + [VMEM] * (len(lefts) + count),
        out_specs=[pl.BlockSpec(memory_space=pltpu.HBM)] * count,
        scratch_shapes=[
            pltpu.VMEM((SLOTS, count, block, narrow), BF16),
            pltpu.SemaphoreType.DMA((SLOTS, count)),
        ],
        cost_estimate=pl.CostEstimate(
            flops=2 * rows * tall * narrow * count,
            bytes_accessed=2 * tall * narrow * count,
            transcendentals=0,
        ),
        compiler_params=pltpu.CompilerParams(vmem_limit_bytes=2**24),
        name="outer_rows",
    )(pltpu.with_memory_space_constraint(after, pltpu.HBM), *[keep(a) for a in (*lefts, *rights)])


def middle_kernel(
    block, pieces, feat, me_ref, after_ref, left_ref, d_gate_ref, d_up_ref, cols_ref, gate_ref, up_ref, *refs
):
    outs, (turned, stage, sems) = refs[-4 - len(pieces):-3], refs[-3:]
    rights, out_ref, outs = refs[:-4 - len(pieces)], outs[0], outs[1:]
    turned[...] = left_ref[...].astype(F32).T.astype(BF16)
    steps, source, place = places(rights[0].shape[1], len(rights), block)

    def fill(step, slot):
        rel, at = source(step)
        stage[slot] = jnp.dot(turned[...], rights[rel][:, at], preferred_element_type=F32).astype(BF16)

    def copies(step, slot):
        return [pltpu.make_async_copy(stage.at[slot], out_ref.at[:, place(step)], sems.at[slot])]

    def term(piece, out):
        rel, low, high = piece
        out[:, :high - low] = term_piece(
            me_ref, rel, low, high, feat, d_gate_ref[...], d_up_ref[...], gate_ref, up_ref
        )
        if high == feat:
            out[:, high - low:] = cols_ref[...]

    stream(steps, fill, copies, [functools.partial(term, *pair) for pair in zip(pieces, outs)])


def middle(left, rights, after, block, pieces, me, d_gate, d_up, cols, gate_m, up_m, feat):
    rows = left.shape[0]
    wide = rights[0].shape[1] * len(rights)
    tall = left.shape[1]
    return pl.pallas_call(
        functools.partial(middle_kernel, block, pieces, feat),
        out_shape=[jax.ShapeDtypeStruct((tall, wide), BF16)]
        + [
            jax.ShapeDtypeStruct((rows, high - low + (LANES if high == feat else 0)), BF16)
            for rel, low, high in pieces
        ],
        in_specs=[SMEM, pl.BlockSpec(memory_space=pl.ANY)] + [VMEM] * (6 + len(rights)),
        out_specs=[pl.BlockSpec(memory_space=pltpu.HBM)] + [VMEM] * len(pieces),
        scratch_shapes=[
            pltpu.VMEM((tall, rows), BF16),
            pltpu.VMEM((SLOTS, tall, block), BF16),
            pltpu.SemaphoreType.DMA((SLOTS,)),
        ],
        cost_estimate=pl.CostEstimate(
            flops=4 * rows * wide * tall, bytes_accessed=2 * wide * tall, transcendentals=0
        ),
        compiler_params=pltpu.CompilerParams(vmem_limit_bytes=2**24),
        name="middle",
    )(me, keep(after), *[keep(a) for a in (left, d_gate, d_up, cols, gate_m, up_m, *rights)])


def settle_kernel(count, *refs):
    pieces, parts, out_ref = refs[:count], refs[count:-2], refs[-1]
    low = 0
    for piece in pieces:
        at = slice(low, low + piece.shape[1])
        total = piece[...].astype(F32)
        for ref in parts:
            total += ref[:, at].astype(F32)
        for i in range(out_ref.shape[0]):
            out_ref[i, :, at] = total[i * CAP:(i + 1) * CAP].astype(BF16)
        low += piece.shape[1]


def settle(pieces, parts, after):
    rows = pieces[0].shape[0]
    wide = sum(a.shape[1] for a in pieces)
    return pl.pallas_call(
        functools.partial(settle_kernel, len(pieces)),
        out_shape=jax.ShapeDtypeStruct((rows // CAP, CAP, wide), BF16),
        in_specs=[VMEM] * (len(pieces) + len(parts)) + [pl.BlockSpec(memory_space=pl.ANY)],
        out_specs=VMEM,
        cost_estimate=pl.CostEstimate(flops=0, bytes_accessed=10**6, transcendentals=0),
        name="settle",
    )(*[keep(a) for a in (*pieces, *parts)], pltpu.with_memory_space_constraint(after, pltpu.HBM))


def combine_kernel(feat, block, pick_ref, gates_ref, rows_ref, grad_ref, gate_ref):
    pick = pick_ref[...]
    at = pl.ds(pl.multiple_of(pl.program_id(0) * block, block), block) if block < feat else slice(0, feat)
    grad_ref[...] = lax.dot_general(
        pick, rows_ref[:, at], (((0,), (0,)), ((), ())), preferred_element_type=F32
    ).astype(BF16)

    @pl.when(pl.program_id(0) == 0)
    def _():
        rows, count = pick.shape
        experts = rows // CAP
        terms = pick.astype(F32) * rows_ref[:, feat:].astype(F32)
        low = row_owners(experts, count) < experts // 2
        for i, part in enumerate((jnp.where(low, terms, 0.0), jnp.where(low, 0.0, terms))):
            gate_ref[i:i + 1, :] = jnp.sum(part, axis=0, keepdims=True) / gates_ref[i:i + 1, :]


def combine(pick, gates, rows, feat):
    count = pick.shape[1]
    block = column_block(feat)
    return pl.pallas_call(
        functools.partial(combine_kernel, feat, block),
        grid=(feat // block,),
        out_shape=[
            jax.ShapeDtypeStruct((count, feat), BF16),
            jax.ShapeDtypeStruct((2, count), F32),
        ],
        in_specs=[VMEM] * 3,
        out_specs=[
            pl.BlockSpec((count, block), lambda i: (0, i)),
            pl.BlockSpec((2, count), lambda i: (0, 0)),
        ],
        cost_estimate=pl.CostEstimate(flops=10**8, bytes_accessed=10**6, transcendentals=0),
        name="combine",
    )(*[keep(a) for a in (pick, gates, rows)])


def per_device(tokens, cotangent, gates, expert_ids, w_gate, w_up, w_down):
    experts = lax.axis_size("dp")
    shards = lax.axis_size("expert")
    me = lax.axis_index("expert")
    rows = experts * CAP
    feat = tokens.shape[1]
    ids_t = expert_ids.T
    gates_t = gates.T
    me_ref = me.reshape(1)
    slots, pick, gates_f = pack(ids_t, gates_t, tokens, cotangent, experts)
    slots = exchange(slots, "dp")
    x = gather_far(slots[:, :CAP].reshape(rows, feat), "expert")
    d = gather_far(slots[:, CAP:].reshape(rows, feat), "expert")
    weights = [w_gate[0], w_up[0], w_down[0]]
    if feat % LANES or shards < 4:
        x, d = gather_near(x, "expert"), gather_near(d, "expert")
        x = [jnp.concatenate(reorder(x, me), axis=1)]
        d = [jnp.concatenate(reorder(d, me), axis=1)]
        weights = load(slots, *weights)
        sums = early([0], me_ref * 0, x, d, weights)
        odd = []
    else:
        x[1], d[1] = swap(x[0], "expert", 1), swap(d[0], "expert", 1)
        weights, sums = load_early(x[0], d[0], weights, slots)
        even = list(range(2, shards, 2))
        odd = list(range(3, shards, 2))
        rest, sums = lax.optimization_barrier(([x[i] for i in even], sums))
        for i, x_i in zip(even, rest):
            x[i], x[i + 1] = x_i, swap(x_i, "expert", 1)
        rels = [1] + even
        more = partial(partial_x_kernel, 2, rels, me_ref, sums[0], [x[1]] + rest, weights)
        rest, more = lax.optimization_barrier(([d[i] for i in even], more))
        for i, d_i in zip(even, rest):
            d[i], d[i + 1] = d_i, swap(d_i, "expert", 1)
        more = [*more, *partial(partial_d_kernel, 1, rels, me_ref, more[0], [d[1]] + rest, weights)]
        x, d = [x[i] for i in range(shards)], [d[i] for i in range(shards)]
        sums = [*sums, *more]
    hidden, d_gate, d_up, cols, *sent = late(
        odd, me_ref, [x[i] for i in odd], [d[i] for i in odd], weights, sums, feat
    )

    def term(pieces, after):
        return terms(pieces, me_ref, after, d_gate, d_up, cols, *weights[:2], feat) if pieces else []

    start = (keep(cols), keep(cols))
    if not odd:
        sent = term([(rel, 0, feat) for rel in range(3, shards, 2)], start)
    arrived = [swap(part, "expert", 1) for part in sent]
    even = list(range(2, shards, 2))
    kept = term([(rel, 0, feat) for rel in even], start)
    held = {rel: add(part, more) for rel, part, more in zip(even, kept, arrived)}
    last = held[max(held)] if held else cols
    wide = feat * shards
    other = sum_far(held, "expert")
    half = max(LANES, (feat - 2 * LANES) // LANES * LANES)
    pieces = ([(1, 0, feat)] if shards > 1 else []) + [(0, 0, half)]
    grad_down, *sent, first = middle(
        hidden, d, last, wide // 8, pieces, me_ref, d_gate, d_up, cols, *weights[:2], feat
    )
    down_done = pltpu.with_memory_space_constraint(grad_down, pltpu.HBM)
    parts = [swap(part, "expert", 1) for part in sent]
    parts += [] if other is None else [other]
    second, = term([(0, half, feat)], (keep(parts[-1] if parts else cols), down_done))
    total = settle([first, second], parts, grad_down)
    got = exchange(total, "dp")
    got = got.reshape(rows, feat + LANES)
    grad_gate, grad_up = outer_rows(x, (d_gate, d_up), total, wide // 16)
    grad_tokens, gate_grads = combine(pick, gates_f, got, feat)
    return (grad_tokens, gate_grads.T, grad_gate[None], grad_up[None], grad_down[None])


def solution(mesh):
    in_specs = (
        P("dp", "expert"),
        P("dp", "expert"),
        P("dp", None),
        P("dp", None),
        P("dp", None, "expert"),
        P("dp", None, "expert"),
        P("dp", "expert", None),
    )
    out_specs = (
        P("dp", "expert"),
        P("dp", None),
        P("dp", None, "expert"),
        P("dp", None, "expert"),
        P("dp", "expert", None),
    )
    return jax.shard_map(
        per_device, mesh=mesh, in_specs=in_specs, out_specs=out_specs, check_vma=False
    )
```

```python
import functools
import math

import jax
import jax.numpy as jnp
from jax import lax
from jax.experimental import pallas as pl
from jax.experimental.pallas import tpu as pltpu
from jax.sharding import PartitionSpec as P

CAP = 8
LANES = 128
F32 = jnp.float32
BF16 = jnp.bfloat16
VMEM = pl.BlockSpec(memory_space=pltpu.VMEM)
SMEM = pl.BlockSpec(memory_space=pltpu.SMEM)


def keep(array):
    return pltpu.with_memory_space_constraint(array, pltpu.VMEM)


def swap(value, axis, mask):
    size = lax.axis_size(axis)
    return lax.ppermute(value, axis, [(i, i ^ mask) for i in range(size)])


def reorder(shards, me):
    size = len(shards)
    mask = 1
    while mask < size:
        flip = (me & mask) != 0
        shards = [jnp.where(flip, shards[i ^ mask], shards[i]) for i in range(size)]
        mask *= 2
    return shards


def gather_far(own, axis):
    size = lax.axis_size(axis)
    held = {0: own}
    mask = size // 2
    while mask > 1:
        for rel in list(held):
            held[rel ^ mask] = swap(held[rel], axis, mask)
        mask //= 2
    return held


def gather_near(held, axis):
    size = lax.axis_size(axis)
    if size > 1:
        held = {**held, **{rel ^ 1: swap(held[rel], axis, 1) for rel in held}}
    return [held[i] for i in range(size)]


def gather_shards(own, axis):
    return gather_near(gather_far(own, axis), axis)


def add(held, arrived):
    return (held.astype(F32) + arrived.astype(F32)).astype(BF16)


def sum_far(held, axis):
    size = lax.axis_size(axis)
    total = None
    mask = 2
    while mask < size:
        arrived = {rel ^ mask: swap(held.pop(rel), axis, mask) for rel in list(held) if rel & mask}
        for rel, value in arrived.items():
            if rel:
                held[rel] = add(held[rel], value)
            else:
                total = value if total is None else add(total, value)
        mask *= 2
    return total


def one_hot(ids, gates, expert, experts):
    rows, tokens = expert.shape
    row = lax.broadcasted_iota(jnp.int32, (rows, tokens), 0)
    low = expert < experts // 2
    member = jnp.where(low, ids[0:1, :], ids[1:2, :]) == expert
    gate = jnp.where(low, gates[0:1, :], gates[1:2, :])
    earlier = lax.broadcasted_iota(jnp.int32, (tokens, tokens), 0) < lax.broadcasted_iota(
        jnp.int32, (tokens, tokens), 1
    )
    before = jnp.dot(
        member.astype(F32).astype(BF16), earlier.astype(F32).astype(BF16), preferred_element_type=F32
    )
    pick = jnp.logical_and(member, before == (row & (CAP - 1)).astype(F32))
    return jnp.where(pick, 1.0, 0.0), jnp.where(pick, gate, 0.0)


def owner_order(experts):
    places = experts // 2
    near = sorted(range(places), key=lambda place: (abs(2 * place - places + 1), -place))
    return [2 * place + last for place in near for last in (1, 0)]


def row_owners(experts, tokens):
    block = lax.broadcasted_iota(jnp.int32, (experts * CAP, tokens), 0) // CAP
    owner = jnp.zeros_like(block)
    for i, expert in enumerate(owner_order(experts)):
        owner = jnp.where(block == i, expert, owner)
    return owner


def exchange(blocks, axis):
    groups = [owner_order(lax.axis_size(axis))]
    return lax.all_to_all(
        blocks, axis, split_axis=0, concat_axis=0, axis_index_groups=groups, tiled=True
    )


def column_block(feat):
    return feat // 2 if feat % (2 * LANES) == 0 else feat


def pack_kernel(
    experts, block, ids_hbm, gates_hbm, x_hbm, d_hbm, slot_hbm, pick_out, gates_out, ids, gates_low, x_ref, d_ref, slots, sems
):
    feat = x_ref.shape[1]
    steps = feat // block

    def columns(step):
        return slice(step * block, (step + 1) * block)

    small = [
        pltpu.make_async_copy(ids_hbm, ids, sems.at[3, 0]),
        pltpu.make_async_copy(gates_hbm, gates_low, sems.at[4, 0]),
    ]
    loads = [
        [
            pltpu.make_async_copy(src.at[:, columns(step)], dst.at[:, columns(step)], sems.at[i, step])
            for i, (src, dst) in enumerate(((x_hbm, x_ref), (d_hbm, d_ref)))
        ]
        for step in range(steps)
    ]
    stores = [
        pltpu.make_async_copy(
            slots.at[:, :, columns(step)], slot_hbm.at[:, :, columns(step)], sems.at[2, step]
        )
        for step in range(steps)
    ]
    for copy in small + [copy for pair in loads for copy in pair]:
        copy.start()
    for copy in small:
        copy.wait()
    gates = gates_low[...].astype(F32)
    pick, pick_gate = one_hot(ids[...], gates, row_owners(experts, ids.shape[1]), experts)
    pick, pick_gate = pick.astype(BF16), pick_gate.astype(BF16)
    for step in range(steps):
        for copy in loads[step]:
            copy.wait()
        slot_x = jnp.dot(pick, x_ref[:, columns(step)], preferred_element_type=F32)
        slot_d = jnp.dot(pick_gate, d_ref[:, columns(step)], preferred_element_type=F32)
        for i in range(experts):
            slots[i, :, columns(step)] = jnp.concatenate(
                [slot_x[i * CAP:(i + 1) * CAP], slot_d[i * CAP:(i + 1) * CAP]], axis=0
            ).astype(BF16)
        stores[step].start()
    pick_out[...] = pick
    gates_out[...] = gates
    for copy in stores:
        copy.wait()


def pack(ids, gates, tokens, cotangent, experts):
    count, feat = tokens.shape
    block = column_block(feat)
    steps = feat // block
    rows = experts * CAP
    hbm = pl.BlockSpec(memory_space=pltpu.HBM)
    return pl.pallas_call(
        functools.partial(pack_kernel, experts, block),
        out_shape=[
            jax.ShapeDtypeStruct((experts, 2 * CAP, feat), BF16),
            jax.ShapeDtypeStruct((rows, count), BF16),
            jax.ShapeDtypeStruct((2, count), F32),
        ],
        in_specs=[hbm] * 4,
        out_specs=[hbm, VMEM, VMEM],
        scratch_shapes=[
            pltpu.VMEM((2, count), jnp.int32),
            pltpu.VMEM((2, count), BF16),
            pltpu.VMEM((count, feat), BF16),
            pltpu.VMEM((count, feat), BF16),
            pltpu.VMEM((experts, 2 * CAP, feat), BF16),
            pltpu.SemaphoreType.DMA((5, steps)),
        ],
        cost_estimate=pl.CostEstimate(flops=10**8, bytes_accessed=2 * 10**6, transcendentals=0),
        compiler_params=pltpu.CompilerParams(vmem_limit_bytes=2**23),
        name="pack",
    )(*[pltpu.with_memory_space_constraint(a, pltpu.HBM) for a in (ids, gates, tokens, cotangent)])


def load_kernel(count, *refs):
    sems = refs[-1]
    copies = [
        pltpu.make_async_copy(refs[i], refs[count + 1 + i], sems.at[i]) for i in range(count)
    ]
    for copy in copies:
        copy.start()
    for copy in copies:
        copy.wait()


def load(after, *arrays):
    count = len(arrays)
    total = sum(a.size * a.dtype.itemsize for a in arrays)
    return pl.pallas_call(
        functools.partial(load_kernel, count),
        out_shape=[pltpu.VMEM(a.shape, a.dtype) for a in arrays],
        in_specs=[pl.BlockSpec(memory_space=pltpu.HBM)] * count + [pl.BlockSpec(memory_space=pl.ANY)],
        out_specs=[VMEM] * count,
        scratch_shapes=[pltpu.SemaphoreType.DMA((count,))],
        cost_estimate=pl.CostEstimate(flops=0, bytes_accessed=total, transcendentals=0),
        compiler_params=pltpu.CompilerParams(vmem_limit_bytes=2**22),
        name="load",
    )(*[pltpu.with_memory_space_constraint(a, pltpu.HBM) for a in arrays], after)


def shard_at(me_ref, rel, feat):
    return pl.ds(pl.multiple_of((me_ref[0] ^ rel) * feat, feat), feat)


def products(rels, me_ref, x_refs, d_refs, gate_ref, up_ref, down_ref):
    feat = x_refs[0].shape[1]
    totals = None
    for rel, x_ref, d_ref in zip(rels, x_refs, d_refs):
        at = shard_at(me_ref, rel, feat)
        parts = (
            jnp.dot(x_ref[...], gate_ref[at, :], preferred_element_type=F32),
            jnp.dot(x_ref[...], up_ref[at, :], preferred_element_type=F32),
            lax.dot_general(
                d_ref[...], down_ref[:, at], (((1,), (1,)), ((), ())), preferred_element_type=F32
            ),
        )
        totals = parts if totals is None else tuple(a + b for a, b in zip(totals, parts))
    return totals


def early_kernel(rels, me_ref, *refs):
    count = len(rels)
    x_refs, d_refs, (gate_ref, up_ref, down_ref) = refs[:count], refs[count:2 * count], refs[2 * count:-3]
    totals = products(rels, me_ref, x_refs, d_refs, gate_ref, up_ref, down_ref)
    for out, value in zip(refs[-3:], totals):
        out[...] = value


def early(rels, me, x, d, weights):
    rows, units = x[0].shape[0], weights[0].shape[1]
    work = 6 * rows * units * x[0].shape[1] * len(rels)
    return pl.pallas_call(
        functools.partial(early_kernel, rels),
        out_shape=[jax.ShapeDtypeStruct((rows, units), F32)] * 3,
        in_specs=[SMEM] + [VMEM] * (2 * len(rels) + 3),
        out_specs=[VMEM] * 3,
        cost_estimate=pl.CostEstimate(flops=work, bytes_accessed=work // rows, transcendentals=0),
        compiler_params=pltpu.CompilerParams(vmem_limit_bytes=2**24),
        name="early",
    )(me, *[keep(a) for a in (*x, *d, *weights)])


def partial_x_kernel(rels, me_ref, after_ref, gate_ref, up_ref, down_ref, *refs):
    x_refs, outs = refs[:-2], refs[-2:]
    feat = x_refs[0].shape[1]
    for weight_ref, out in zip((gate_ref, up_ref), outs):
        total = None
        for rel, x_ref in zip(rels, x_refs):
            part = jnp.dot(
                x_ref[...], weight_ref[shard_at(me_ref, rel, feat), :], preferred_element_type=F32
            )
            total = part if total is None else total + part
        out[...] = total


def partial_d_kernel(rels, me_ref, after_ref, gate_ref, up_ref, down_ref, *refs):
    d_refs, out = refs[:-1], refs[-1]
    feat = d_refs[0].shape[1]
    total = None
    for rel, d_ref in zip(rels, d_refs):
        part = lax.dot_general(
            d_ref[...],
            down_ref[:, shard_at(me_ref, rel, feat)],
            (((1,), (1,)), ((), ())),
            preferred_element_type=F32,
        )
        total = part if total is None else total + part
    out[...] = total


def partial(kernel, count, rels, me, after, arrays, weights):
    rows, units = arrays[0].shape[0], weights[0].shape[1]
    work = 2 * count * rows * units * arrays[0].shape[1] * len(rels)
    return pl.pallas_call(
        functools.partial(kernel, rels),
        out_shape=[jax.ShapeDtypeStruct((rows, units), F32)] * count,
        in_specs=[SMEM, pl.BlockSpec(memory_space=pl.ANY)] + [VMEM] * (3 + len(rels)),
        out_specs=[VMEM] * count,
        cost_estimate=pl.CostEstimate(flops=work, bytes_accessed=work // rows, transcendentals=0),
        compiler_params=pltpu.CompilerParams(vmem_limit_bytes=2**24),
        name="partial",
    )(me, keep(after), *[keep(a) for a in (*weights, *arrays)])


def flip(index, rel):
    mask = 1
    while mask <= rel:
        if rel & mask:
            index = index + mask * (1 - 2 * ((index // mask) % 2))
        mask *= 2
    return index


def load_early_kernel(x0, d0, gate_in, up_in, down_in, gate, up, down, *refs):
    sums, sems = refs[:3], refs[3]
    feat = x0.shape[1]
    me = lax.axis_index("expert")
    shards = gate.shape[0] // feat

    def place(rel):
        return pl.ds(pl.multiple_of(flip(me, rel) * feat, feat), feat)

    def copies(rel):
        at = place(rel)
        return [
            pltpu.make_async_copy(src.at[where], dst.at[where], sems.at[i, rel])
            for i, (src, dst, where) in enumerate(
                ((gate_in, gate, at), (up_in, up, at), (down_in, down, (slice(None), at)))
            )
        ]

    first, *rest = [copies(rel) for rel in range(shards)]
    for copy in first:
        copy.start()
    for group in rest:
        for copy in group:
            copy.start()
    at = place(0)
    for i in range(3):
        first[i].wait()
        if i < 2:
            sums[i][...] = jnp.dot(x0[...], (gate, up)[i][at, :], preferred_element_type=F32)
        else:
            sums[i][...] = lax.dot_general(
                d0[...], down[:, at], (((1,), (1,)), ((), ())), preferred_element_type=F32
            )
    for group in rest:
        for copy in group:
            copy.wait()


def load_early(x, d, weights, after):
    rows = x.shape[0]
    units = weights[0].shape[1]
    shards = lax.axis_size("expert")
    out = pl.pallas_call(
        lambda after_ref, *refs: load_early_kernel(*refs),
        out_shape=[pltpu.VMEM(a.shape, a.dtype) for a in weights]
        + [jax.ShapeDtypeStruct((rows, units), F32)] * 3,
        in_specs=[pl.BlockSpec(memory_space=pl.ANY)]
        + [VMEM] * 2
        + [pl.BlockSpec(memory_space=pltpu.HBM)] * 3,
        out_specs=[VMEM] * 6,
        scratch_shapes=[pltpu.SemaphoreType.DMA((3, shards))],
        cost_estimate=pl.CostEstimate(
            flops=6 * rows * units * x.shape[1],
            bytes_accessed=sum(a.size * 2 for a in weights),
            transcendentals=0,
        ),
        compiler_params=pltpu.CompilerParams(vmem_limit_bytes=2**23),
        name="load_early",
    )(
        keep(after),
        keep(x),
        keep(d),
        *[pltpu.with_memory_space_constraint(a, pltpu.HBM) for a in weights],
    )
    return out[:3], out[3:]


def late_kernel(rels, feat, me_ref, *refs):
    count = len(rels)
    x_refs, d_refs, refs = refs[:count], refs[count:2 * count], refs[2 * count:]
    refs, outs = refs[:-4 - count], refs[-4 - count:]
    (gate_ref, up_ref, down_ref), sum_refs = refs[:3], refs[3:]
    hidden_out, d_gate_out, d_up_out, cols_out = outs[:4]
    totals = [ref[...] for ref in sum_refs[:3]]
    for i, ref in enumerate(sum_refs[3:]):
        totals[i % 3] += ref[...]
    if rels:
        parts = products(rels, me_ref, x_refs, d_refs, gate_ref, up_ref, down_ref)
        totals = [a + b for a, b in zip(totals, parts)]
    pre_gate, pre_up, dhid = totals
    sig = 1.0 / (1.0 + jnp.exp(-pre_gate))
    act = pre_gate * sig
    hidden = (act * pre_up).astype(BF16)
    d_gate = (dhid * pre_up * sig * (1.0 + pre_gate * (1.0 - sig))).astype(BF16)
    d_up = (dhid * act).astype(BF16)
    total = jnp.sum(dhid * hidden.astype(F32), axis=1, keepdims=True)
    cols = jnp.broadcast_to(total, cols_out.shape).astype(BF16)
    for rel, out in zip(rels, outs[4:]):
        out[:, :feat] = term_piece(me_ref, rel, 0, feat, feat, d_gate, d_up, gate_ref, up_ref)
        out[:, feat:] = cols
    hidden_out[...] = hidden
    d_gate_out[...] = d_gate
    d_up_out[...] = d_up
    cols_out[...] = cols


def late(rels, me, x, d, weights, sums, feat):
    rows, units = sums[0].shape
    work = 10 * rows * units * feat * max(1, len(rels))
    return pl.pallas_call(
        functools.partial(late_kernel, rels, feat),
        out_shape=[jax.ShapeDtypeStruct((rows, units), BF16)] * 3
        + [jax.ShapeDtypeStruct((rows, LANES), BF16)]
        + [jax.ShapeDtypeStruct((rows, feat + LANES), BF16)] * len(rels),
        in_specs=[SMEM] + [VMEM] * (2 * len(rels) + 3 + len(sums)),
        out_specs=[VMEM] * (4 + len(rels)),
        cost_estimate=pl.CostEstimate(
            flops=work, bytes_accessed=work // rows, transcendentals=rows * units
        ),
        compiler_params=pltpu.CompilerParams(vmem_limit_bytes=2**24),
        name="late",
    )(me, *[keep(a) for a in (*x, *d, *weights, *sums)])


def term_piece(me_ref, rel, low, high, feat, d_gate, d_up, gate_ref, up_ref):
    dims = (((1,), (1,)), ((), ()))
    start = (me_ref[0] ^ rel) * feat + low
    at = pl.ds(pl.multiple_of(start, math.gcd(feat, low)), high - low)
    term = lax.dot_general(d_gate, gate_ref[at, :], dims, preferred_element_type=F32)
    term += lax.dot_general(d_up, up_ref[at, :], dims, preferred_element_type=F32)
    return term.astype(BF16)


def term_kernel(pieces, feat, me_ref, after_ref, last_ref, d_gate_ref, d_up_ref, cols_ref, gate_ref, up_ref, *outs):
    for (rel, low, high), out in zip(pieces, outs):
        out[:, :high - low] = term_piece(
            me_ref, rel, low, high, feat, d_gate_ref[...], d_up_ref[...], gate_ref, up_ref
        )
        if high == feat:
            out[:, high - low:] = cols_ref[...]


def terms(pieces, me, after, d_gate, d_up, cols, gate_m, up_m, feat):
    rows = d_gate.shape[0]
    return pl.pallas_call(
        functools.partial(term_kernel, pieces, feat),
        out_shape=[
            jax.ShapeDtypeStruct((rows, high - low + (LANES if high == feat else 0)), BF16)
            for rel, low, high in pieces
        ],
        in_specs=[SMEM] + [pl.BlockSpec(memory_space=pl.ANY)] * 2 + [VMEM] * 5,
        out_specs=[VMEM] * len(pieces),
        cost_estimate=pl.CostEstimate(flops=1, bytes_accessed=1, transcendentals=0),
        compiler_params=pltpu.CompilerParams(vmem_limit_bytes=2**24),
        name="terms",
    )(me, *after, *[keep(a) for a in (d_gate, d_up, cols, gate_m, up_m)])


SLOTS = 4


def stream(steps, fill, copies, beside=()):
    beside = list(beside)
    for step in range(steps + SLOTS):
        if step >= SLOTS:
            for copy in copies(step - SLOTS, step % SLOTS):
                copy.wait()
        if step < steps:
            fill(step, step % SLOTS)
            for copy in copies(step, step % SLOTS):
                copy.start()
            if steps - step <= len(beside):
                beside[step - steps]()


def places(feat, shards, block):
    me = lax.axis_index("expert") if shards > 1 else 0

    def place(step):
        rel, part = divmod(step, feat // block)
        start = flip(me, rel) * feat + part * block
        return pl.ds(pl.multiple_of(start, block) if shards > 1 else start, block)

    def source(step):
        rel, part = divmod(step, feat // block)
        return rel, slice(part * block, (part + 1) * block)

    return shards * feat // block, source, place


def outer_rows_kernel(block, shards, after_ref, *refs):
    stage, sems = refs[-2:]
    lefts, refs = refs[:shards], refs[shards:-2]
    half = len(refs) // 2
    rights, outs = refs[:half], refs[half:]
    steps, source, place = places(lefts[0].shape[1], shards, block)

    def fill(step, slot):
        rel, at = source(step)
        left = lefts[rel][:, at].astype(F32).T.astype(BF16)
        for i, right in enumerate(rights):
            stage[slot, i] = jnp.dot(left, right[...], preferred_element_type=F32).astype(BF16)

    def copies(step, slot):
        return [
            pltpu.make_async_copy(stage.at[slot, i], out.at[place(step)], sems.at[slot, i])
            for i, out in enumerate(outs)
        ]

    stream(steps, fill, copies)


def outer_rows(lefts, rights, after, block):
    rows, feat = lefts[0].shape
    tall = feat * len(lefts)
    narrow = rights[0].shape[1]
    count = len(rights)
    return pl.pallas_call(
        functools.partial(outer_rows_kernel, block, len(lefts)),
        out_shape=[jax.ShapeDtypeStruct((tall, narrow), BF16)] * count,
        in_specs=[pl.BlockSpec(memory_space=pl.ANY)] + [VMEM] * (len(lefts) + count),
        out_specs=[pl.BlockSpec(memory_space=pltpu.HBM)] * count,
        scratch_shapes=[
            pltpu.VMEM((SLOTS, count, block, narrow), BF16),
            pltpu.SemaphoreType.DMA((SLOTS, count)),
        ],
        cost_estimate=pl.CostEstimate(
            flops=2 * rows * tall * narrow * count,
            bytes_accessed=2 * tall * narrow * count,
            transcendentals=0,
        ),
        compiler_params=pltpu.CompilerParams(vmem_limit_bytes=2**24),
        name="outer_rows",
    )(pltpu.with_memory_space_constraint(after, pltpu.HBM), *[keep(a) for a in (*lefts, *rights)])


def middle_kernel(
    block, pieces, feat, me_ref, after_ref, left_ref, d_gate_ref, d_up_ref, cols_ref, gate_ref, up_ref, *refs
):
    outs, (turned, stage, sems) = refs[-4 - len(pieces):-3], refs[-3:]
    rights, out_ref, outs = refs[:-4 - len(pieces)], outs[0], outs[1:]
    turned[...] = left_ref[...].astype(F32).T.astype(BF16)
    steps, source, place = places(rights[0].shape[1], len(rights), block)

    def fill(step, slot):
        rel, at = source(step)
        stage[slot] = jnp.dot(turned[...], rights[rel][:, at], preferred_element_type=F32).astype(BF16)

    def copies(step, slot):
        return [pltpu.make_async_copy(stage.at[slot], out_ref.at[:, place(step)], sems.at[slot])]

    def term(piece, out):
        rel, low, high = piece
        out[:, :high - low] = term_piece(
            me_ref, rel, low, high, feat, d_gate_ref[...], d_up_ref[...], gate_ref, up_ref
        )
        if high == feat:
            out[:, high - low:] = cols_ref[...]

    stream(steps, fill, copies, [functools.partial(term, *pair) for pair in zip(pieces, outs)])


def middle(left, rights, after, block, pieces, me, d_gate, d_up, cols, gate_m, up_m, feat):
    rows = left.shape[0]
    wide = rights[0].shape[1] * len(rights)
    tall = left.shape[1]
    return pl.pallas_call(
        functools.partial(middle_kernel, block, pieces, feat),
        out_shape=[jax.ShapeDtypeStruct((tall, wide), BF16)]
        + [
            jax.ShapeDtypeStruct((rows, high - low + (LANES if high == feat else 0)), BF16)
            for rel, low, high in pieces
        ],
        in_specs=[SMEM, pl.BlockSpec(memory_space=pl.ANY)] + [VMEM] * (6 + len(rights)),
        out_specs=[pl.BlockSpec(memory_space=pltpu.HBM)] + [VMEM] * len(pieces),
        scratch_shapes=[
            pltpu.VMEM((tall, rows), BF16),
            pltpu.VMEM((SLOTS, tall, block), BF16),
            pltpu.SemaphoreType.DMA((SLOTS,)),
        ],
        cost_estimate=pl.CostEstimate(
            flops=4 * rows * wide * tall, bytes_accessed=2 * wide * tall, transcendentals=0
        ),
        compiler_params=pltpu.CompilerParams(vmem_limit_bytes=2**24),
        name="middle",
    )(me, keep(after), *[keep(a) for a in (left, d_gate, d_up, cols, gate_m, up_m, *rights)])


def settle_kernel(count, *refs):
    pieces, parts, out_ref = refs[:count], refs[count:-2], refs[-1]
    low = 0
    for piece in pieces:
        at = slice(low, low + piece.shape[1])
        total = piece[...].astype(F32)
        for ref in parts:
            total += ref[:, at].astype(F32)
        for i in range(out_ref.shape[0]):
            out_ref[i, :, at] = total[i * CAP:(i + 1) * CAP].astype(BF16)
        low += piece.shape[1]


def settle(pieces, parts, after):
    rows = pieces[0].shape[0]
    wide = sum(a.shape[1] for a in pieces)
    return pl.pallas_call(
        functools.partial(settle_kernel, len(pieces)),
        out_shape=jax.ShapeDtypeStruct((rows // CAP, CAP, wide), BF16),
        in_specs=[VMEM] * (len(pieces) + len(parts)) + [pl.BlockSpec(memory_space=pl.ANY)],
        out_specs=VMEM,
        cost_estimate=pl.CostEstimate(flops=0, bytes_accessed=10**6, transcendentals=0),
        name="settle",
    )(*[keep(a) for a in (*pieces, *parts)], pltpu.with_memory_space_constraint(after, pltpu.HBM))


def combine_kernel(feat, block, pick_ref, gates_ref, rows_ref, grad_ref, gate_ref):
    pick = pick_ref[...]
    at = pl.ds(pl.multiple_of(pl.program_id(0) * block, block), block) if block < feat else slice(0, feat)
    grad_ref[...] = lax.dot_general(
        pick, rows_ref[:, at], (((0,), (0,)), ((), ())), preferred_element_type=F32
    ).astype(BF16)

    @pl.when(pl.program_id(0) == 0)
    def _():
        rows, count = pick.shape
        experts = rows // CAP
        terms = pick.astype(F32) * rows_ref[:, feat:].astype(F32)
        low = row_owners(experts, count) < experts // 2
        for i, part in enumerate((jnp.where(low, terms, 0.0), jnp.where(low, 0.0, terms))):
            gate_ref[i:i + 1, :] = jnp.sum(part, axis=0, keepdims=True) / gates_ref[i:i + 1, :]


def combine(pick, gates, rows, feat):
    count = pick.shape[1]
    block = column_block(feat)
    return pl.pallas_call(
        functools.partial(combine_kernel, feat, block),
        grid=(feat // block,),
        out_shape=[
            jax.ShapeDtypeStruct((count, feat), BF16),
            jax.ShapeDtypeStruct((2, count), F32),
        ],
        in_specs=[VMEM] * 3,
        out_specs=[
            pl.BlockSpec((count, block), lambda i: (0, i)),
            pl.BlockSpec((2, count), lambda i: (0, 0)),
        ],
        cost_estimate=pl.CostEstimate(flops=10**8, bytes_accessed=10**6, transcendentals=0),
        name="combine",
    )(*[keep(a) for a in (pick, gates, rows)])


def per_device(tokens, cotangent, gates, expert_ids, w_gate, w_up, w_down):
    experts = lax.axis_size("dp")
    shards = lax.axis_size("expert")
    me = lax.axis_index("expert")
    rows = experts * CAP
    feat = tokens.shape[1]
    ids_t = expert_ids.T
    gates_t = gates.T
    me_ref = me.reshape(1)
    slots, pick, gates_f = pack(ids_t, gates_t, tokens, cotangent, experts)
    slots = exchange(slots, "dp")
    x = gather_far(slots[:, :CAP].reshape(rows, feat), "expert")
    d = gather_far(slots[:, CAP:].reshape(rows, feat), "expert")
    weights = [w_gate[0], w_up[0], w_down[0]]
    if feat % LANES or shards < 4:
        x, d = gather_near(x, "expert"), gather_near(d, "expert")
        x = [jnp.concatenate(reorder(x, me), axis=1)]
        d = [jnp.concatenate(reorder(d, me), axis=1)]
        weights = load(slots, *weights)
        sums = early([0], me_ref * 0, x, d, weights)
        odd = []
    else:
        x[1], d[1] = swap(x[0], "expert", 1), swap(d[0], "expert", 1)
        weights, sums = load_early(x[0], d[0], weights, slots)
        even = list(range(2, shards, 2))
        odd = list(range(3, shards, 2))
        rest, sums = lax.optimization_barrier(([x[i] for i in even], sums))
        for i, x_i in zip(even, rest):
            x[i], x[i + 1] = x_i, swap(x_i, "expert", 1)
        rels = [1] + even
        more = partial(partial_x_kernel, 2, rels, me_ref, sums[0], [x[1]] + rest, weights)
        rest, more = lax.optimization_barrier(([d[i] for i in even], more))
        for i, d_i in zip(even, rest):
            d[i], d[i + 1] = d_i, swap(d_i, "expert", 1)
        more = [*more, *partial(partial_d_kernel, 1, rels, me_ref, more[0], [d[1]] + rest, weights)]
        x, d = [x[i] for i in range(shards)], [d[i] for i in range(shards)]
        sums = [*sums, *more]
    hidden, d_gate, d_up, cols, *sent = late(
        odd, me_ref, [x[i] for i in odd], [d[i] for i in odd], weights, sums, feat
    )

    def term(pieces, after):
        return terms(pieces, me_ref, after, d_gate, d_up, cols, *weights[:2], feat) if pieces else []

    start = (keep(cols), keep(cols))
    if not odd:
        sent = term([(rel, 0, feat) for rel in range(3, shards, 2)], start)
    arrived = [swap(part, "expert", 1) for part in sent]
    even = list(range(2, shards, 2))
    kept = term([(rel, 0, feat) for rel in even], start)
    held = {rel: add(part, more) for rel, part, more in zip(even, kept, arrived)}
    last = held[max(held)] if held else cols
    wide = feat * shards
    other = sum_far(held, "expert")
    half = max(LANES, (feat - 2 * LANES) // LANES * LANES)
    pieces = ([(1, 0, feat)] if shards > 1 else []) + [(0, 0, half)]
    grad_down, *sent, first = middle(
        hidden, d, last, wide // 8, pieces, me_ref, d_gate, d_up, cols, *weights[:2], feat
    )
    down_done = pltpu.with_memory_space_constraint(grad_down, pltpu.HBM)
    parts = [swap(part, "expert", 1) for part in sent]
    parts += [] if other is None else [other]
    second, = term([(0, half, feat)], (keep(parts[-1] if parts else cols), down_done))
    total = settle([first, second], parts, grad_down)
    got = exchange(total, "dp")
    got = got.reshape(rows, feat + LANES)
    grad_gate, grad_up = outer_rows(x, (d_gate, d_up), total, wide // 16)
    grad_tokens, gate_grads = combine(pick, gates_f, got, feat)
    return (grad_tokens, gate_grads.T, grad_gate[None], grad_up[None], grad_down[None])


def solution(mesh):
    in_specs = (
        P("dp", "expert"),
        P("dp", "expert"),
        P("dp", None),
        P("dp", None),
        P("dp", None, "expert"),
        P("dp", None, "expert"),
        P("dp", "expert", None),
    )
    out_specs = (
        P("dp", "expert"),
        P("dp", None),
        P("dp", None, "expert"),
        P("dp", None, "expert"),
        P("dp", "expert", None),
    )
    return jax.shard_map(
        per_device, mesh=mesh, in_specs=in_specs, out_specs=out_specs, check_vma=False
    )
```

```python
import functools
import math

import jax
import jax.numpy as jnp
from jax import lax
from jax.experimental import pallas as pl
from jax.experimental.pallas import tpu as pltpu
from jax.sharding import PartitionSpec as P

CAP = 8
LANES = 128
F32 = jnp.float32
BF16 = jnp.bfloat16
VMEM = pl.BlockSpec(memory_space=pltpu.VMEM)
SMEM = pl.BlockSpec(memory_space=pltpu.SMEM)


def keep(array):
    return pltpu.with_memory_space_constraint(array, pltpu.VMEM)


def swap(value, axis, mask):
    size = lax.axis_size(axis)
    return lax.ppermute(value, axis, [(i, i ^ mask) for i in range(size)])


def reorder(shards, me):
    size = len(shards)
    mask = 1
    while mask < size:
        flip = (me & mask) != 0
        shards = [jnp.where(flip, shards[i ^ mask], shards[i]) for i in range(size)]
        mask *= 2
    return shards


def gather_far(own, axis):
    size = lax.axis_size(axis)
    held = {0: own}
    mask = size // 2
    while mask > 1:
        for rel in list(held):
            held[rel ^ mask] = swap(held[rel], axis, mask)
        mask //= 2
    return held


def gather_near(held, axis):
    size = lax.axis_size(axis)
    if size > 1:
        held = {**held, **{rel ^ 1: swap(held[rel], axis, 1) for rel in held}}
    return [held[i] for i in range(size)]


def gather_shards(own, axis):
    return gather_near(gather_far(own, axis), axis)


def add(held, arrived):
    return (held.astype(F32) + arrived.astype(F32)).astype(BF16)


def sum_far(held, axis):
    size = lax.axis_size(axis)
    total = None
    mask = 2
    while mask < size:
        arrived = {rel ^ mask: swap(held.pop(rel), axis, mask) for rel in list(held) if rel & mask}
        for rel, value in arrived.items():
            if rel:
                held[rel] = add(held[rel], value)
            else:
                total = value if total is None else add(total, value)
        mask *= 2
    return total


def one_hot(ids, gates, expert, experts):
    rows, tokens = expert.shape
    row = lax.broadcasted_iota(jnp.int32, (rows, tokens), 0)
    low = expert < experts // 2
    member = jnp.where(low, ids[0:1, :], ids[1:2, :]) == expert
    gate = jnp.where(low, gates[0:1, :], gates[1:2, :])
    earlier = lax.broadcasted_iota(jnp.int32, (tokens, tokens), 0) < lax.broadcasted_iota(
        jnp.int32, (tokens, tokens), 1
    )
    before = jnp.dot(
        member.astype(F32).astype(BF16), earlier.astype(F32).astype(BF16), preferred_element_type=F32
    )
    pick = jnp.logical_and(member, before == (row & (CAP - 1)).astype(F32))
    return jnp.where(pick, 1.0, 0.0), jnp.where(pick, gate, 0.0)


def owner_order(experts):
    places = experts // 2
    near = sorted(range(places), key=lambda place: abs(2 * place - places + 1))
    return [
        2 * place + last for i in range(0, places, 2) for last in range(2) for place in near[i:i + 2]
    ]


def row_owners(experts, tokens):
    block = lax.broadcasted_iota(jnp.int32, (experts * CAP, tokens), 0) // CAP
    owner = jnp.zeros_like(block)
    for i, expert in enumerate(owner_order(experts)):
        owner = jnp.where(block == i, expert, owner)
    return owner


def exchange(blocks, axis):
    groups = [owner_order(lax.axis_size(axis))]
    return lax.all_to_all(
        blocks, axis, split_axis=0, concat_axis=0, axis_index_groups=groups, tiled=True
    )


def column_block(feat):
    return feat // 2 if feat % (2 * LANES) == 0 else feat


def pack_kernel(
    experts, block, ids_hbm, gates_hbm, x_hbm, d_hbm, slot_hbm, pick_out, gates_out, ids, gates_low, x_ref, d_ref, slots, sems
):
    feat = x_ref.shape[1]
    steps = feat // block

    def columns(step):
        return slice(step * block, (step + 1) * block)

    small = [
        pltpu.make_async_copy(ids_hbm, ids, sems.at[3, 0]),
        pltpu.make_async_copy(gates_hbm, gates_low, sems.at[4, 0]),
    ]
    loads = [
        [
            pltpu.make_async_copy(src.at[:, columns(step)], dst.at[:, columns(step)], sems.at[i, step])
            for i, (src, dst) in enumerate(((x_hbm, x_ref), (d_hbm, d_ref)))
        ]
        for step in range(steps)
    ]
    stores = [
        pltpu.make_async_copy(
            slots.at[:, :, columns(step)], slot_hbm.at[:, :, columns(step)], sems.at[2, step]
        )
        for step in range(steps)
    ]
    for copy in small + [copy for pair in loads for copy in pair]:
        copy.start()
    for copy in small:
        copy.wait()
    gates = gates_low[...].astype(F32)
    pick, pick_gate = one_hot(ids[...], gates, row_owners(experts, ids.shape[1]), experts)
    pick, pick_gate = pick.astype(BF16), pick_gate.astype(BF16)
    for step in range(steps):
        for copy in loads[step]:
            copy.wait()
        slot_x = jnp.dot(pick, x_ref[:, columns(step)], preferred_element_type=F32)
        slot_d = jnp.dot(pick_gate, d_ref[:, columns(step)], preferred_element_type=F32)
        for i in range(experts):
            slots[i, :, columns(step)] = jnp.concatenate(
                [slot_x[i * CAP:(i + 1) * CAP], slot_d[i * CAP:(i + 1) * CAP]], axis=0
            ).astype(BF16)
        stores[step].start()
    pick_out[...] = pick
    gates_out[...] = gates
    for copy in stores:
        copy.wait()


def pack(ids, gates, tokens, cotangent, experts):
    count, feat = tokens.shape
    block = column_block(feat)
    steps = feat // block
    rows = experts * CAP
    hbm = pl.BlockSpec(memory_space=pltpu.HBM)
    return pl.pallas_call(
        functools.partial(pack_kernel, experts, block),
        out_shape=[
            jax.ShapeDtypeStruct((experts, 2 * CAP, feat), BF16),
            jax.ShapeDtypeStruct((rows, count), BF16),
            jax.ShapeDtypeStruct((2, count), F32),
        ],
        in_specs=[hbm] * 4,
        out_specs=[hbm, VMEM, VMEM],
        scratch_shapes=[
            pltpu.VMEM((2, count), jnp.int32),
            pltpu.VMEM((2, count), BF16),
            pltpu.VMEM((count, feat), BF16),
            pltpu.VMEM((count, feat), BF16),
            pltpu.VMEM((experts, 2 * CAP, feat), BF16),
            pltpu.SemaphoreType.DMA((5, steps)),
        ],
        cost_estimate=pl.CostEstimate(flops=10**8, bytes_accessed=2 * 10**6, transcendentals=0),
        compiler_params=pltpu.CompilerParams(vmem_limit_bytes=2**23),
        name="pack",
    )(*[pltpu.with_memory_space_constraint(a, pltpu.HBM) for a in (ids, gates, tokens, cotangent)])


def load_kernel(count, *refs):
    sems = refs[-1]
    copies = [
        pltpu.make_async_copy(refs[i], refs[count + 1 + i], sems.at[i]) for i in range(count)
    ]
    for copy in copies:
        copy.start()
    for copy in copies:
        copy.wait()


def load(after, *arrays):
    count = len(arrays)
    total = sum(a.size * a.dtype.itemsize for a in arrays)
    return pl.pallas_call(
        functools.partial(load_kernel, count),
        out_shape=[pltpu.VMEM(a.shape, a.dtype) for a in arrays],
        in_specs=[pl.BlockSpec(memory_space=pltpu.HBM)] * count + [pl.BlockSpec(memory_space=pl.ANY)],
        out_specs=[VMEM] * count,
        scratch_shapes=[pltpu.SemaphoreType.DMA((count,))],
        cost_estimate=pl.CostEstimate(flops=0, bytes_accessed=total, transcendentals=0),
        compiler_params=pltpu.CompilerParams(vmem_limit_bytes=2**22),
        name="load",
    )(*[pltpu.with_memory_space_constraint(a, pltpu.HBM) for a in arrays], after)


def shard_at(me_ref, rel, feat):
    return pl.ds(pl.multiple_of((me_ref[0] ^ rel) * feat, feat), feat)


def products(rels, me_ref, x_refs, d_refs, gate_ref, up_ref, down_ref):
    feat = x_refs[0].shape[1]
    totals = None
    for rel, x_ref, d_ref in zip(rels, x_refs, d_refs):
        at = shard_at(me_ref, rel, feat)
        parts = (
            jnp.dot(x_ref[...], gate_ref[at, :], preferred_element_type=F32),
            jnp.dot(x_ref[...], up_ref[at, :], preferred_element_type=F32),
            lax.dot_general(
                d_ref[...], down_ref[:, at], (((1,), (1,)), ((), ())), preferred_element_type=F32
            ),
        )
        totals = parts if totals is None else tuple(a + b for a, b in zip(totals, parts))
    return totals


def early_kernel(rels, me_ref, *refs):
    count = len(rels)
    x_refs, d_refs, (gate_ref, up_ref, down_ref) = refs[:count], refs[count:2 * count], refs[2 * count:-3]
    totals = products(rels, me_ref, x_refs, d_refs, gate_ref, up_ref, down_ref)
    for out, value in zip(refs[-3:], totals):
        out[...] = value


def early(rels, me, x, d, weights):
    rows, units = x[0].shape[0], weights[0].shape[1]
    work = 6 * rows * units * x[0].shape[1] * len(rels)
    return pl.pallas_call(
        functools.partial(early_kernel, rels),
        out_shape=[jax.ShapeDtypeStruct((rows, units), F32)] * 3,
        in_specs=[SMEM] + [VMEM] * (2 * len(rels) + 3),
        out_specs=[VMEM] * 3,
        cost_estimate=pl.CostEstimate(flops=work, bytes_accessed=work // rows, transcendentals=0),
        compiler_params=pltpu.CompilerParams(vmem_limit_bytes=2**24),
        name="early",
    )(me, *[keep(a) for a in (*x, *d, *weights)])


def partial_x_kernel(rels, me_ref, after_ref, gate_ref, up_ref, down_ref, *refs):
    x_refs, outs = refs[:-2], refs[-2:]
    feat = x_refs[0].shape[1]
    for weight_ref, out in zip((gate_ref, up_ref), outs):
        total = None
        for rel, x_ref in zip(rels, x_refs):
            part = jnp.dot(
                x_ref[...], weight_ref[shard_at(me_ref, rel, feat), :], preferred_element_type=F32
            )
            total = part if total is None else total + part
        out[...] = total


def partial_d_kernel(rels, me_ref, after_ref, gate_ref, up_ref, down_ref, *refs):
    d_refs, out = refs[:-1], refs[-1]
    feat = d_refs[0].shape[1]
    total = None
    for rel, d_ref in zip(rels, d_refs):
        part = lax.dot_general(
            d_ref[...],
            down_ref[:, shard_at(me_ref, rel, feat)],
            (((1,), (1,)), ((), ())),
            preferred_element_type=F32,
        )
        total = part if total is None else total + part
    out[...] = total


def partial(kernel, count, rels, me, after, arrays, weights):
    rows, units = arrays[0].shape[0], weights[0].shape[1]
    work = 2 * count * rows * units * arrays[0].shape[1] * len(rels)
    return pl.pallas_call(
        functools.partial(kernel, rels),
        out_shape=[jax.ShapeDtypeStruct((rows, units), F32)] * count,
        in_specs=[SMEM, pl.BlockSpec(memory_space=pl.ANY)] + [VMEM] * (3 + len(rels)),
        out_specs=[VMEM] * count,
        cost_estimate=pl.CostEstimate(flops=work, bytes_accessed=work // rows, transcendentals=0),
        compiler_params=pltpu.CompilerParams(vmem_limit_bytes=2**24),
        name="partial",
    )(me, keep(after), *[keep(a) for a in (*weights, *arrays)])


def flip(index, rel):
    mask = 1
    while mask <= rel:
        if rel & mask:
            index = index + mask * (1 - 2 * ((index // mask) % 2))
        mask *= 2
    return index


def load_early_kernel(x0, d0, gate_in, up_in, down_in, gate, up, down, *refs):
    sums, sems = refs[:3], refs[3]
    feat = x0.shape[1]
    me = lax.axis_index("expert")
    shards = gate.shape[0] // feat

    def place(rel):
        return pl.ds(pl.multiple_of(flip(me, rel) * feat, feat), feat)

    def copies(rel):
        at = place(rel)
        return [
            pltpu.make_async_copy(src.at[where], dst.at[where], sems.at[i, rel])
            for i, (src, dst, where) in enumerate(
                ((gate_in, gate, at), (up_in, up, at), (down_in, down, (slice(None), at)))
            )
        ]

    first, *rest = [copies(rel) for rel in range(shards)]
    for copy in first:
        copy.start()
    for group in rest:
        for copy in group:
            copy.start()
    at = place(0)
    for i in range(3):
        first[i].wait()
        if i < 2:
            sums[i][...] = jnp.dot(x0[...], (gate, up)[i][at, :], preferred_element_type=F32)
        else:
            sums[i][...] = lax.dot_general(
                d0[...], down[:, at], (((1,), (1,)), ((), ())), preferred_element_type=F32
            )
    for group in rest:
        for copy in group:
            copy.wait()


def load_early(x, d, weights, after):
    rows = x.shape[0]
    units = weights[0].shape[1]
    shards = lax.axis_size("expert")
    out = pl.pallas_call(
        lambda after_ref, *refs: load_early_kernel(*refs),
        out_shape=[pltpu.VMEM(a.shape, a.dtype) for a in weights]
        + [jax.ShapeDtypeStruct((rows, units), F32)] * 3,
        in_specs=[pl.BlockSpec(memory_space=pl.ANY)]
        + [VMEM] * 2
        + [pl.BlockSpec(memory_space=pltpu.HBM)] * 3,
        out_specs=[VMEM] * 6,
        scratch_shapes=[pltpu.SemaphoreType.DMA((3, shards))],
        cost_estimate=pl.CostEstimate(
            flops=6 * rows * units * x.shape[1],
            bytes_accessed=sum(a.size * 2 for a in weights),
            transcendentals=0,
        ),
        compiler_params=pltpu.CompilerParams(vmem_limit_bytes=2**23),
        name="load_early",
    )(
        keep(after),
        keep(x),
        keep(d),
        *[pltpu.with_memory_space_constraint(a, pltpu.HBM) for a in weights],
    )
    return out[:3], out[3:]


def late_kernel(rels, feat, me_ref, *refs):
    count = len(rels)
    x_refs, d_refs, refs = refs[:count], refs[count:2 * count], refs[2 * count:]
    refs, outs = refs[:-4 - count], refs[-4 - count:]
    (gate_ref, up_ref, down_ref), sum_refs = refs[:3], refs[3:]
    hidden_out, d_gate_out, d_up_out, cols_out = outs[:4]
    totals = [ref[...] for ref in sum_refs[:3]]
    for i, ref in enumerate(sum_refs[3:]):
        totals[i % 3] += ref[...]
    if rels:
        parts = products(rels, me_ref, x_refs, d_refs, gate_ref, up_ref, down_ref)
        totals = [a + b for a, b in zip(totals, parts)]
    pre_gate, pre_up, dhid = totals
    sig = 1.0 / (1.0 + jnp.exp(-pre_gate))
    act = pre_gate * sig
    hidden = (act * pre_up).astype(BF16)
    d_gate = (dhid * pre_up * sig * (1.0 + pre_gate * (1.0 - sig))).astype(BF16)
    d_up = (dhid * act).astype(BF16)
    total = jnp.sum(dhid * hidden.astype(F32), axis=1, keepdims=True)
    cols = jnp.broadcast_to(total, cols_out.shape).astype(BF16)
    for rel, out in zip(rels, outs[4:]):
        out[:, :feat] = term_piece(me_ref, rel, 0, feat, feat, d_gate, d_up, gate_ref, up_ref)
        out[:, feat:] = cols
    hidden_out[...] = hidden
    d_gate_out[...] = d_gate
    d_up_out[...] = d_up
    cols_out[...] = cols


def late(rels, me, x, d, weights, sums, feat):
    rows, units = sums[0].shape
    work = 10 * rows * units * feat * max(1, len(rels))
    return pl.pallas_call(
        functools.partial(late_kernel, rels, feat),
        out_shape=[jax.ShapeDtypeStruct((rows, units), BF16)] * 3
        + [jax.ShapeDtypeStruct((rows, LANES), BF16)]
        + [jax.ShapeDtypeStruct((rows, feat + LANES), BF16)] * len(rels),
        in_specs=[SMEM] + [VMEM] * (2 * len(rels) + 3 + len(sums)),
        out_specs=[VMEM] * (4 + len(rels)),
        cost_estimate=pl.CostEstimate(
            flops=work, bytes_accessed=work // rows, transcendentals=rows * units
        ),
        compiler_params=pltpu.CompilerParams(vmem_limit_bytes=2**24),
        name="late",
    )(me, *[keep(a) for a in (*x, *d, *weights, *sums)])


def term_piece(me_ref, rel, low, high, feat, d_gate, d_up, gate_ref, up_ref):
    dims = (((1,), (1,)), ((), ()))
    start = (me_ref[0] ^ rel) * feat + low
    at = pl.ds(pl.multiple_of(start, math.gcd(feat, low)), high - low)
    term = lax.dot_general(d_gate, gate_ref[at, :], dims, preferred_element_type=F32)
    term += lax.dot_general(d_up, up_ref[at, :], dims, preferred_element_type=F32)
    return term.astype(BF16)


def term_kernel(pieces, feat, me_ref, after_ref, last_ref, d_gate_ref, d_up_ref, cols_ref, gate_ref, up_ref, *outs):
    for (rel, low, high), out in zip(pieces, outs):
        out[:, :high - low] = term_piece(
            me_ref, rel, low, high, feat, d_gate_ref[...], d_up_ref[...], gate_ref, up_ref
        )
        if high == feat:
            out[:, high - low:] = cols_ref[...]


def terms(pieces, me, after, d_gate, d_up, cols, gate_m, up_m, feat):
    rows = d_gate.shape[0]
    return pl.pallas_call(
        functools.partial(term_kernel, pieces, feat),
        out_shape=[
            jax.ShapeDtypeStruct((rows, high - low + (LANES if high == feat else 0)), BF16)
            for rel, low, high in pieces
        ],
        in_specs=[SMEM] + [pl.BlockSpec(memory_space=pl.ANY)] * 2 + [VMEM] * 5,
        out_specs=[VMEM] * len(pieces),
        cost_estimate=pl.CostEstimate(flops=1, bytes_accessed=1, transcendentals=0),
        compiler_params=pltpu.CompilerParams(vmem_limit_bytes=2**24),
        name="terms",
    )(me, *after, *[keep(a) for a in (d_gate, d_up, cols, gate_m, up_m)])


SLOTS = 4


def stream(steps, fill, copies, beside=()):
    beside = list(beside)
    for step in range(steps + SLOTS):
        if step >= SLOTS:
            for copy in copies(step - SLOTS, step % SLOTS):
                copy.wait()
        if step < steps:
            fill(step, step % SLOTS)
            for copy in copies(step, step % SLOTS):
                copy.start()
            if steps - step <= len(beside):
                beside[step - steps]()


def places(feat, shards, block):
    me = lax.axis_index("expert") if shards > 1 else 0

    def place(step):
        rel, part = divmod(step, feat // block)
        start = flip(me, rel) * feat + part * block
        return pl.ds(pl.multiple_of(start, block) if shards > 1 else start, block)

    def source(step):
        rel, part = divmod(step, feat // block)
        return rel, slice(part * block, (part + 1) * block)

    return shards * feat // block, source, place


def outer_rows_kernel(block, shards, after_ref, *refs):
    stage, sems = refs[-2:]
    lefts, refs = refs[:shards], refs[shards:-2]
    half = len(refs) // 2
    rights, outs = refs[:half], refs[half:]
    steps, source, place = places(lefts[0].shape[1], shards, block)

    def fill(step, slot):
        rel, at = source(step)
        left = lefts[rel][:, at].astype(F32).T.astype(BF16)
        for i, right in enumerate(rights):
            stage[slot, i] = jnp.dot(left, right[...], preferred_element_type=F32).astype(BF16)

    def copies(step, slot):
        return [
            pltpu.make_async_copy(stage.at[slot, i], out.at[place(step)], sems.at[slot, i])
            for i, out in enumerate(outs)
        ]

    stream(steps, fill, copies)


def outer_rows(lefts, rights, after, block):
    rows, feat = lefts[0].shape
    tall = feat * len(lefts)
    narrow = rights[0].shape[1]
    count = len(rights)
    return pl.pallas_call(
        functools.partial(outer_rows_kernel, block, len(lefts)),
        out_shape=[jax.ShapeDtypeStruct((tall, narrow), BF16)] * count,
        in_specs=[pl.BlockSpec(memory_space=pl.ANY)] + [VMEM] * (len(lefts) + count),
        out_specs=[pl.BlockSpec(memory_space=pltpu.HBM)] * count,
        scratch_shapes=[
            pltpu.VMEM((SLOTS, count, block, narrow), BF16),
            pltpu.SemaphoreType.DMA((SLOTS, count)),
        ],
        cost_estimate=pl.CostEstimate(
            flops=2 * rows * tall * narrow * count,
            bytes_accessed=2 * tall * narrow * count,
            transcendentals=0,
        ),
        compiler_params=pltpu.CompilerParams(vmem_limit_bytes=2**24),
        name="outer_rows",
    )(pltpu.with_memory_space_constraint(after, pltpu.HBM), *[keep(a) for a in (*lefts, *rights)])


def middle_kernel(
    block, pieces, feat, me_ref, after_ref, left_ref, d_gate_ref, d_up_ref, cols_ref, gate_ref, up_ref, *refs
):
    outs, (turned, stage, sems) = refs[-4 - len(pieces):-3], refs[-3:]
    rights, out_ref, outs = refs[:-4 - len(pieces)], outs[0], outs[1:]
    turned[...] = left_ref[...].astype(F32).T.astype(BF16)
    steps, source, place = places(rights[0].shape[1], len(rights), block)

    def fill(step, slot):
        rel, at = source(step)
        stage[slot] = jnp.dot(turned[...], rights[rel][:, at], preferred_element_type=F32).astype(BF16)

    def copies(step, slot):
        return [pltpu.make_async_copy(stage.at[slot], out_ref.at[:, place(step)], sems.at[slot])]

    def term(piece, out):
        rel, low, high = piece
        out[:, :high - low] = term_piece(
            me_ref, rel, low, high, feat, d_gate_ref[...], d_up_ref[...], gate_ref, up_ref
        )
        if high == feat:
            out[:, high - low:] = cols_ref[...]

    stream(steps, fill, copies, [functools.partial(term, *pair) for pair in zip(pieces, outs)])


def middle(left, rights, after, block, pieces, me, d_gate, d_up, cols, gate_m, up_m, feat):
    rows = left.shape[0]
    wide = rights[0].shape[1] * len(rights)
    tall = left.shape[1]
    return pl.pallas_call(
        functools.partial(middle_kernel, block, pieces, feat),
        out_shape=[jax.ShapeDtypeStruct((tall, wide), BF16)]
        + [
            jax.ShapeDtypeStruct((rows, high - low + (LANES if high == feat else 0)), BF16)
            for rel, low, high in pieces
        ],
        in_specs=[SMEM, pl.BlockSpec(memory_space=pl.ANY)] + [VMEM] * (6 + len(rights)),
        out_specs=[pl.BlockSpec(memory_space=pltpu.HBM)] + [VMEM] * len(pieces),
        scratch_shapes=[
            pltpu.VMEM((tall, rows), BF16),
            pltpu.VMEM((SLOTS, tall, block), BF16),
            pltpu.SemaphoreType.DMA((SLOTS,)),
        ],
        cost_estimate=pl.CostEstimate(
            flops=4 * rows * wide * tall, bytes_accessed=2 * wide * tall, transcendentals=0
        ),
        compiler_params=pltpu.CompilerParams(vmem_limit_bytes=2**24),
        name="middle",
    )(me, keep(after), *[keep(a) for a in (left, d_gate, d_up, cols, gate_m, up_m, *rights)])


def settle_kernel(count, *refs):
    pieces, parts, out_ref = refs[:count], refs[count:-2], refs[-1]
    low = 0
    for piece in pieces:
        at = slice(low, low + piece.shape[1])
        total = piece[...].astype(F32)
        for ref in parts:
            total += ref[:, at].astype(F32)
        for i in range(out_ref.shape[0]):
            out_ref[i, :, at] = total[i * CAP:(i + 1) * CAP].astype(BF16)
        low += piece.shape[1]


def settle(pieces, parts, after):
    rows = pieces[0].shape[0]
    wide = sum(a.shape[1] for a in pieces)
    return pl.pallas_call(
        functools.partial(settle_kernel, len(pieces)),
        out_shape=jax.ShapeDtypeStruct((rows // CAP, CAP, wide), BF16),
        in_specs=[VMEM] * (len(pieces) + len(parts)) + [pl.BlockSpec(memory_space=pl.ANY)],
        out_specs=VMEM,
        cost_estimate=pl.CostEstimate(flops=0, bytes_accessed=10**6, transcendentals=0),
        name="settle",
    )(*[keep(a) for a in (*pieces, *parts)], pltpu.with_memory_space_constraint(after, pltpu.HBM))


def combine_kernel(feat, block, pick_ref, gates_ref, rows_ref, grad_ref, gate_ref):
    pick = pick_ref[...]
    at = pl.ds(pl.multiple_of(pl.program_id(0) * block, block), block) if block < feat else slice(0, feat)
    grad_ref[...] = lax.dot_general(
        pick, rows_ref[:, at], (((0,), (0,)), ((), ())), preferred_element_type=F32
    ).astype(BF16)

    @pl.when(pl.program_id(0) == 0)
    def _():
        rows, count = pick.shape
        experts = rows // CAP
        terms = pick.astype(F32) * rows_ref[:, feat:].astype(F32)
        low = row_owners(experts, count) < experts // 2
        for i, part in enumerate((jnp.where(low, terms, 0.0), jnp.where(low, 0.0, terms))):
            gate_ref[i:i + 1, :] = jnp.sum(part, axis=0, keepdims=True) / gates_ref[i:i + 1, :]


def combine(pick, gates, rows, feat):
    count = pick.shape[1]
    block = column_block(feat)
    return pl.pallas_call(
        functools.partial(combine_kernel, feat, block),
        grid=(feat // block,),
        out_shape=[
            jax.ShapeDtypeStruct((count, feat), BF16),
            jax.ShapeDtypeStruct((2, count), F32),
        ],
        in_specs=[VMEM] * 3,
        out_specs=[
            pl.BlockSpec((count, block), lambda i: (0, i)),
            pl.BlockSpec((2, count), lambda i: (0, 0)),
        ],
        cost_estimate=pl.CostEstimate(flops=10**8, bytes_accessed=10**6, transcendentals=0),
        name="combine",
    )(*[keep(a) for a in (pick, gates, rows)])


def per_device(tokens, cotangent, gates, expert_ids, w_gate, w_up, w_down):
    experts = lax.axis_size("dp")
    shards = lax.axis_size("expert")
    me = lax.axis_index("expert")
    rows = experts * CAP
    feat = tokens.shape[1]
    ids_t = expert_ids.T
    gates_t = gates.T
    me_ref = me.reshape(1)
    slots, pick, gates_f = pack(ids_t, gates_t, tokens, cotangent, experts)
    slots = exchange(slots, "dp")
    x = gather_far(slots[:, :CAP].reshape(rows, feat), "expert")
    d = gather_far(slots[:, CAP:].reshape(rows, feat), "expert")
    weights = [w_gate[0], w_up[0], w_down[0]]
    if feat % LANES or shards < 4:
        x, d = gather_near(x, "expert"), gather_near(d, "expert")
        x = [jnp.concatenate(reorder(x, me), axis=1)]
        d = [jnp.concatenate(reorder(d, me), axis=1)]
        weights = load(slots, *weights)
        sums = early([0], me_ref * 0, x, d, weights)
        odd = []
    else:
        x[1], d[1] = swap(x[0], "expert", 1), swap(d[0], "expert", 1)
        weights, sums = load_early(x[0], d[0], weights, slots)
        even = list(range(2, shards, 2))
        odd = list(range(3, shards, 2))
        rest, sums = lax.optimization_barrier(([x[i] for i in even], sums))
        for i, x_i in zip(even, rest):
            x[i], x[i + 1] = x_i, swap(x_i, "expert", 1)
        rels = [1] + even
        more = partial(partial_x_kernel, 2, rels, me_ref, sums[0], [x[1]] + rest, weights)
        rest, more = lax.optimization_barrier(([d[i] for i in even], more))
        for i, d_i in zip(even, rest):
            d[i], d[i + 1] = d_i, swap(d_i, "expert", 1)
        more = [*more, *partial(partial_d_kernel, 1, rels, me_ref, more[0], [d[1]] + rest, weights)]
        x, d = [x[i] for i in range(shards)], [d[i] for i in range(shards)]
        sums = [*sums, *more]
    hidden, d_gate, d_up, cols, *sent = late(
        odd, me_ref, [x[i] for i in odd], [d[i] for i in odd], weights, sums, feat
    )

    def term(pieces, after):
        return terms(pieces, me_ref, after, d_gate, d_up, cols, *weights[:2], feat) if pieces else []

    start = (keep(cols), keep(cols))
    if not odd:
        sent = term([(rel, 0, feat) for rel in range(3, shards, 2)], start)
    arrived = [swap(part, "expert", 1) for part in sent]
    even = list(range(2, shards, 2))
    kept = term([(rel, 0, feat) for rel in even], start)
    held = {rel: add(part, more) for rel, part, more in zip(even, kept, arrived)}
    last = held[max(held)] if held else cols
    wide = feat * shards
    other = sum_far(held, "expert")
    half = max(LANES, (feat - 2 * LANES) // LANES * LANES)
    pieces = ([(1, 0, feat)] if shards > 1 else []) + [(0, 0, half)]
    grad_down, *sent, first = middle(
        hidden, d, last, wide // 8, pieces, me_ref, d_gate, d_up, cols, *weights[:2], feat
    )
    down_done = pltpu.with_memory_space_constraint(grad_down, pltpu.HBM)
    parts = [swap(part, "expert", 1) for part in sent]
    parts += [] if other is None else [other]
    second, = term([(0, half, feat)], (keep(parts[-1] if parts else cols), down_done))
    total = settle([first, second], parts, grad_down)
    got = exchange(total, "dp")
    got = got.reshape(rows, feat + LANES)
    grad_gate, grad_up = outer_rows(x, (d_gate, d_up), total, wide // 16)
    grad_tokens, gate_grads = combine(pick, gates_f, got, feat)
    return (grad_tokens, gate_grads.T, grad_gate[None], grad_up[None], grad_down[None])


def solution(mesh):
    in_specs = (
        P("dp", "expert"),
        P("dp", "expert"),
        P("dp", None),
        P("dp", None),
        P("dp", None, "expert"),
        P("dp", None, "expert"),
        P("dp", "expert", None),
    )
    out_specs = (
        P("dp", "expert"),
        P("dp", None),
        P("dp", None, "expert"),
        P("dp", None, "expert"),
        P("dp", "expert", None),
    )
    return jax.shard_map(
        per_device, mesh=mesh, in_specs=in_specs, out_specs=out_specs, check_vma=False
    )
```

```python
import functools
import math

import jax
import jax.numpy as jnp
from jax import lax
from jax.experimental import pallas as pl
from jax.experimental.pallas import tpu as pltpu
from jax.sharding import PartitionSpec as P

CAP = 8
LANES = 128
F32 = jnp.float32
BF16 = jnp.bfloat16
VMEM = pl.BlockSpec(memory_space=pltpu.VMEM)
SMEM = pl.BlockSpec(memory_space=pltpu.SMEM)


def keep(array):
    return pltpu.with_memory_space_constraint(array, pltpu.VMEM)


def swap(value, axis, mask):
    size = lax.axis_size(axis)
    return lax.ppermute(value, axis, [(i, i ^ mask) for i in range(size)])


def reorder(shards, me):
    size = len(shards)
    mask = 1
    while mask < size:
        flip = (me & mask) != 0
        shards = [jnp.where(flip, shards[i ^ mask], shards[i]) for i in range(size)]
        mask *= 2
    return shards


def gather_far(own, axis):
    size = lax.axis_size(axis)
    held = {0: own}
    mask = size // 2
    while mask > 1:
        for rel in list(held):
            held[rel ^ mask] = swap(held[rel], axis, mask)
        mask //= 2
    return held


def gather_near(held, axis):
    size = lax.axis_size(axis)
    if size > 1:
        held = {**held, **{rel ^ 1: swap(held[rel], axis, 1) for rel in held}}
    return [held[i] for i in range(size)]


def gather_shards(own, axis):
    return gather_near(gather_far(own, axis), axis)


def add(held, arrived):
    return (held.astype(F32) + arrived.astype(F32)).astype(BF16)


def sum_far(held, axis):
    size = lax.axis_size(axis)
    total = None
    mask = 2
    while mask < size:
        arrived = {rel ^ mask: swap(held.pop(rel), axis, mask) for rel in list(held) if rel & mask}
        for rel, value in arrived.items():
            if rel:
                held[rel] = add(held[rel], value)
            else:
                total = value if total is None else add(total, value)
        mask *= 2
    return total


def one_hot(ids, gates, expert, experts):
    rows, tokens = expert.shape
    row = lax.broadcasted_iota(jnp.int32, (rows, tokens), 0)
    low = expert < experts // 2
    member = jnp.where(low, ids[0:1, :], ids[1:2, :]) == expert
    gate = jnp.where(low, gates[0:1, :], gates[1:2, :])
    earlier = lax.broadcasted_iota(jnp.int32, (tokens, tokens), 0) < lax.broadcasted_iota(
        jnp.int32, (tokens, tokens), 1
    )
    before = jnp.dot(
        member.astype(F32).astype(BF16), earlier.astype(F32).astype(BF16), preferred_element_type=F32
    )
    pick = jnp.logical_and(member, before == (row & (CAP - 1)).astype(F32))
    return jnp.where(pick, 1.0, 0.0), jnp.where(pick, gate, 0.0)


def owner_order(experts):
    places = experts // 2
    near = sorted(range(places), key=lambda place: (abs(2 * place - places + 1), -place))
    return [2 * place + last for place in near for last in (1, 0)]


def row_owners(experts, tokens):
    block = lax.broadcasted_iota(jnp.int32, (experts * CAP, tokens), 0) // CAP
    owner = jnp.zeros_like(block)
    for i, expert in enumerate(owner_order(experts)):
        owner = jnp.where(block == i, expert, owner)
    return owner


def exchange(blocks, axis):
    groups = [owner_order(lax.axis_size(axis))]
    return lax.all_to_all(
        blocks, axis, split_axis=0, concat_axis=0, axis_index_groups=groups, tiled=True
    )


def column_block(feat):
    return feat // 2 if feat % (2 * LANES) == 0 else feat


def pack_kernel(
    experts, block, ids_hbm, gates_hbm, x_hbm, d_hbm, slot_hbm, pick_out, gates_out, ids, gates_low, x_ref, d_ref, slots, sems
):
    feat = x_ref.shape[1]
    steps = feat // block

    def columns(step):
        return slice(step * block, (step + 1) * block)

    small = [
        pltpu.make_async_copy(ids_hbm, ids, sems.at[3, 0]),
        pltpu.make_async_copy(gates_hbm, gates_low, sems.at[4, 0]),
    ]
    loads = [
        [
            pltpu.make_async_copy(src.at[:, columns(step)], dst.at[:, columns(step)], sems.at[i, step])
            for i, (src, dst) in enumerate(((x_hbm, x_ref), (d_hbm, d_ref)))
        ]
        for step in range(steps)
    ]
    stores = [
        pltpu.make_async_copy(
            slots.at[:, :, columns(step)], slot_hbm.at[:, :, columns(step)], sems.at[2, step]
        )
        for step in range(steps)
    ]
    for copy in small + [copy for pair in loads for copy in pair]:
        copy.start()
    for copy in small:
        copy.wait()
    gates = gates_low[...].astype(F32)
    pick, pick_gate = one_hot(ids[...], gates, row_owners(experts, ids.shape[1]), experts)
    pick, pick_gate = pick.astype(BF16), pick_gate.astype(BF16)
    for step in range(steps):
        for copy in loads[step]:
            copy.wait()
        slot_x = jnp.dot(pick, x_ref[:, columns(step)], preferred_element_type=F32)
        slot_d = jnp.dot(pick_gate, d_ref[:, columns(step)], preferred_element_type=F32)
        for i in range(experts):
            slots[i, :, columns(step)] = jnp.concatenate(
                [slot_x[i * CAP:(i + 1) * CAP], slot_d[i * CAP:(i + 1) * CAP]], axis=0
            ).astype(BF16)
        stores[step].start()
    pick_out[...] = pick
    gates_out[...] = gates
    for copy in stores:
        copy.wait()


def pack(ids, gates, tokens, cotangent, experts):
    count, feat = tokens.shape
    block = column_block(feat)
    steps = feat // block
    rows = experts * CAP
    hbm = pl.BlockSpec(memory_space=pltpu.HBM)
    return pl.pallas_call(
        functools.partial(pack_kernel, experts, block),
        out_shape=[
            jax.ShapeDtypeStruct((experts, 2 * CAP, feat), BF16),
            jax.ShapeDtypeStruct((rows, count), BF16),
            jax.ShapeDtypeStruct((2, count), F32),
        ],
        in_specs=[hbm] * 4,
        out_specs=[hbm, VMEM, VMEM],
        scratch_shapes=[
            pltpu.VMEM((2, count), jnp.int32),
            pltpu.VMEM((2, count), BF16),
            pltpu.VMEM((count, feat), BF16),
            pltpu.VMEM((count, feat), BF16),
            pltpu.VMEM((experts, 2 * CAP, feat), BF16),
            pltpu.SemaphoreType.DMA((5, steps)),
        ],
        cost_estimate=pl.CostEstimate(flops=10**8, bytes_accessed=2 * 10**6, transcendentals=0),
        compiler_params=pltpu.CompilerParams(vmem_limit_bytes=2**23),
        name="pack",
    )(*[pltpu.with_memory_space_constraint(a, pltpu.HBM) for a in (ids, gates, tokens, cotangent)])


def load_kernel(count, *refs):
    sems = refs[-1]
    copies = [
        pltpu.make_async_copy(refs[i], refs[count + 1 + i], sems.at[i]) for i in range(count)
    ]
    for copy in copies:
        copy.start()
    for copy in copies:
        copy.wait()


def load(after, *arrays):
    count = len(arrays)
    total = sum(a.size * a.dtype.itemsize for a in arrays)
    return pl.pallas_call(
        functools.partial(load_kernel, count),
        out_shape=[pltpu.VMEM(a.shape, a.dtype) for a in arrays],
        in_specs=[pl.BlockSpec(memory_space=pltpu.HBM)] * count + [pl.BlockSpec(memory_space=pl.ANY)],
        out_specs=[VMEM] * count,
        scratch_shapes=[pltpu.SemaphoreType.DMA((count,))],
        cost_estimate=pl.CostEstimate(flops=0, bytes_accessed=total, transcendentals=0),
        compiler_params=pltpu.CompilerParams(vmem_limit_bytes=2**22),
        name="load",
    )(*[pltpu.with_memory_space_constraint(a, pltpu.HBM) for a in arrays], after)


def shard_at(me_ref, rel, feat):
    return pl.ds(pl.multiple_of((me_ref[0] ^ rel) * feat, feat), feat)


def products(rels, me_ref, x_refs, d_refs, gate_ref, up_ref, down_ref):
    feat = x_refs[0].shape[1]
    totals = None
    for rel, x_ref, d_ref in zip(rels, x_refs, d_refs):
        at = shard_at(me_ref, rel, feat)
        parts = (
            jnp.dot(x_ref[...], gate_ref[at, :], preferred_element_type=F32),
            jnp.dot(x_ref[...], up_ref[at, :], preferred_element_type=F32),
            lax.dot_general(
                d_ref[...], down_ref[:, at], (((1,), (1,)), ((), ())), preferred_element_type=F32
            ),
        )
        totals = parts if totals is None else tuple(a + b for a, b in zip(totals, parts))
    return totals


def early_kernel(rels, me_ref, *refs):
    count = len(rels)
    x_refs, d_refs, (gate_ref, up_ref, down_ref) = refs[:count], refs[count:2 * count], refs[2 * count:-3]
    totals = products(rels, me_ref, x_refs, d_refs, gate_ref, up_ref, down_ref)
    for out, value in zip(refs[-3:], totals):
        out[...] = value


def early(rels, me, x, d, weights):
    rows, units = x[0].shape[0], weights[0].shape[1]
    work = 6 * rows * units * x[0].shape[1] * len(rels)
    return pl.pallas_call(
        functools.partial(early_kernel, rels),
        out_shape=[jax.ShapeDtypeStruct((rows, units), F32)] * 3,
        in_specs=[SMEM] + [VMEM] * (2 * len(rels) + 3),
        out_specs=[VMEM] * 3,
        cost_estimate=pl.CostEstimate(flops=work, bytes_accessed=work // rows, transcendentals=0),
        compiler_params=pltpu.CompilerParams(vmem_limit_bytes=2**24),
        name="early",
    )(me, *[keep(a) for a in (*x, *d, *weights)])


def partial_x_kernel(rels, me_ref, after_ref, gate_ref, up_ref, down_ref, *refs):
    x_refs, outs = refs[:-2], refs[-2:]
    feat = x_refs[0].shape[1]
    for weight_ref, out in zip((gate_ref, up_ref), outs):
        total = None
        for rel, x_ref in zip(rels, x_refs):
            part = jnp.dot(
                x_ref[...], weight_ref[shard_at(me_ref, rel, feat), :], preferred_element_type=F32
            )
            total = part if total is None else total + part
        out[...] = total


def partial_d_kernel(rels, me_ref, after_ref, gate_ref, up_ref, down_ref, *refs):
    d_refs, out = refs[:-1], refs[-1]
    feat = d_refs[0].shape[1]
    total = None
    for rel, d_ref in zip(rels, d_refs):
        part = lax.dot_general(
            d_ref[...],
            down_ref[:, shard_at(me_ref, rel, feat)],
            (((1,), (1,)), ((), ())),
            preferred_element_type=F32,
        )
        total = part if total is None else total + part
    out[...] = total


def partial(kernel, count, rels, me, after, arrays, weights):
    rows, units = arrays[0].shape[0], weights[0].shape[1]
    work = 2 * count * rows * units * arrays[0].shape[1] * len(rels)
    return pl.pallas_call(
        functools.partial(kernel, rels),
        out_shape=[jax.ShapeDtypeStruct((rows, units), F32)] * count,
        in_specs=[SMEM, pl.BlockSpec(memory_space=pl.ANY)] + [VMEM] * (3 + len(rels)),
        out_specs=[VMEM] * count,
        cost_estimate=pl.CostEstimate(flops=work, bytes_accessed=work // rows, transcendentals=0),
        compiler_params=pltpu.CompilerParams(vmem_limit_bytes=2**24),
        name="partial",
    )(me, keep(after), *[keep(a) for a in (*weights, *arrays)])


def flip(index, rel):
    mask = 1
    while mask <= rel:
        if rel & mask:
            index = index + mask * (1 - 2 * ((index // mask) % 2))
        mask *= 2
    return index


def load_early_kernel(x0, d0, gate_in, up_in, down_in, gate, up, down, *refs):
    sums, sems = refs[:3], refs[3]
    feat = x0.shape[1]
    me = lax.axis_index("expert")
    shards = gate.shape[0] // feat

    def place(rel):
        return pl.ds(pl.multiple_of(flip(me, rel) * feat, feat), feat)

    def copies(rel):
        at = place(rel)
        return [
            pltpu.make_async_copy(src.at[where], dst.at[where], sems.at[i, rel])
            for i, (src, dst, where) in enumerate(
                ((gate_in, gate, at), (up_in, up, at), (down_in, down, (slice(None), at)))
            )
        ]

    first, *rest = [copies(rel) for rel in range(shards)]
    for copy in first:
        copy.start()
    for group in rest:
        for copy in group:
            copy.start()
    at = place(0)
    for i in range(3):
        first[i].wait()
        if i < 2:
            sums[i][...] = jnp.dot(x0[...], (gate, up)[i][at, :], preferred_element_type=F32)
        else:
            sums[i][...] = lax.dot_general(
                d0[...], down[:, at], (((1,), (1,)), ((), ())), preferred_element_type=F32
            )
    for group in rest:
        for copy in group:
            copy.wait()


def load_early(x, d, weights, after):
    rows = x.shape[0]
    units = weights[0].shape[1]
    shards = lax.axis_size("expert")
    out = pl.pallas_call(
        lambda after_ref, *refs: load_early_kernel(*refs),
        out_shape=[pltpu.VMEM(a.shape, a.dtype) for a in weights]
        + [jax.ShapeDtypeStruct((rows, units), F32)] * 3,
        in_specs=[pl.BlockSpec(memory_space=pl.ANY)]
        + [VMEM] * 2
        + [pl.BlockSpec(memory_space=pltpu.HBM)] * 3,
        out_specs=[VMEM] * 6,
        scratch_shapes=[pltpu.SemaphoreType.DMA((3, shards))],
        cost_estimate=pl.CostEstimate(
            flops=6 * rows * units * x.shape[1],
            bytes_accessed=sum(a.size * 2 for a in weights),
            transcendentals=0,
        ),
        compiler_params=pltpu.CompilerParams(vmem_limit_bytes=2**23),
        name="load_early",
    )(
        keep(after),
        keep(x),
        keep(d),
        *[pltpu.with_memory_space_constraint(a, pltpu.HBM) for a in weights],
    )
    return out[:3], out[3:]


def late_kernel(rels, feat, me_ref, *refs):
    count = len(rels)
    x_refs, d_refs, refs = refs[:count], refs[count:2 * count], refs[2 * count:]
    refs, outs = refs[:-4 - count], refs[-4 - count:]
    (gate_ref, up_ref, down_ref), sum_refs = refs[:3], refs[3:]
    hidden_out, d_gate_out, d_up_out, cols_out = outs[:4]
    totals = [ref[...] for ref in sum_refs[:3]]
    for i, ref in enumerate(sum_refs[3:]):
        totals[i % 3] += ref[...]
    if rels:
        parts = products(rels, me_ref, x_refs, d_refs, gate_ref, up_ref, down_ref)
        totals = [a + b for a, b in zip(totals, parts)]
    pre_gate, pre_up, dhid = totals
    sig = 1.0 / (1.0 + jnp.exp(-pre_gate))
    act = pre_gate * sig
    hidden = (act * pre_up).astype(BF16)
    d_gate = (dhid * pre_up * sig * (1.0 + pre_gate * (1.0 - sig))).astype(BF16)
    d_up = (dhid * act).astype(BF16)
    total = jnp.sum(dhid * hidden.astype(F32), axis=1, keepdims=True)
    cols = jnp.broadcast_to(total, cols_out.shape).astype(BF16)
    for rel, out in zip(rels, outs[4:]):
        out[:, :feat] = term_piece(me_ref, rel, 0, feat, feat, d_gate, d_up, gate_ref, up_ref)
        out[:, feat:] = cols
    hidden_out[...] = hidden
    d_gate_out[...] = d_gate
    d_up_out[...] = d_up
    cols_out[...] = cols


def late(rels, me, x, d, weights, sums, feat):
    rows, units = sums[0].shape
    work = 10 * rows * units * feat * max(1, len(rels))
    return pl.pallas_call(
        functools.partial(late_kernel, rels, feat),
        out_shape=[jax.ShapeDtypeStruct((rows, units), BF16)] * 3
        + [jax.ShapeDtypeStruct((rows, LANES), BF16)]
        + [jax.ShapeDtypeStruct((rows, feat + LANES), BF16)] * len(rels),
        in_specs=[SMEM] + [VMEM] * (2 * len(rels) + 3 + len(sums)),
        out_specs=[VMEM] * (4 + len(rels)),
        cost_estimate=pl.CostEstimate(
            flops=work, bytes_accessed=work // rows, transcendentals=rows * units
        ),
        compiler_params=pltpu.CompilerParams(vmem_limit_bytes=2**24),
        name="late",
    )(me, *[keep(a) for a in (*x, *d, *weights, *sums)])


def term_piece(me_ref, rel, low, high, feat, d_gate, d_up, gate_ref, up_ref):
    dims = (((1,), (1,)), ((), ()))
    start = (me_ref[0] ^ rel) * feat + low
    at = pl.ds(pl.multiple_of(start, math.gcd(feat, low)), high - low)
    term = lax.dot_general(d_gate, gate_ref[at, :], dims, preferred_element_type=F32)
    term += lax.dot_general(d_up, up_ref[at, :], dims, preferred_element_type=F32)
    return term.astype(BF16)


def term_kernel(pieces, feat, me_ref, after_ref, last_ref, d_gate_ref, d_up_ref, cols_ref, gate_ref, up_ref, *outs):
    for (rel, low, high), out in zip(pieces, outs):
        out[:, :high - low] = term_piece(
            me_ref, rel, low, high, feat, d_gate_ref[...], d_up_ref[...], gate_ref, up_ref
        )
        if high == feat:
            out[:, high - low:] = cols_ref[...]


def terms(pieces, me, after, d_gate, d_up, cols, gate_m, up_m, feat):
    rows = d_gate.shape[0]
    return pl.pallas_call(
        functools.partial(term_kernel, pieces, feat),
        out_shape=[
            jax.ShapeDtypeStruct((rows, high - low + (LANES if high == feat else 0)), BF16)
            for rel, low, high in pieces
        ],
        in_specs=[SMEM] + [pl.BlockSpec(memory_space=pl.ANY)] * 2 + [VMEM] * 5,
        out_specs=[VMEM] * len(pieces),
        cost_estimate=pl.CostEstimate(flops=1, bytes_accessed=1, transcendentals=0),
        compiler_params=pltpu.CompilerParams(vmem_limit_bytes=2**24),
        name="terms",
    )(me, *after, *[keep(a) for a in (d_gate, d_up, cols, gate_m, up_m)])


SLOTS = 4


def stream(steps, fill, copies, beside=()):
    beside = list(beside)
    for step in range(steps + SLOTS):
        if step >= SLOTS:
            for copy in copies(step - SLOTS, step % SLOTS):
                copy.wait()
        if step < steps:
            fill(step, step % SLOTS)
            for copy in copies(step, step % SLOTS):
                copy.start()
            if steps - step <= len(beside):
                beside[step - steps]()


def places(feat, shards, block):
    me = lax.axis_index("expert") if shards > 1 else 0

    def place(step):
        rel, part = divmod(step, feat // block)
        start = flip(me, rel) * feat + part * block
        return pl.ds(pl.multiple_of(start, block) if shards > 1 else start, block)

    def source(step):
        rel, part = divmod(step, feat // block)
        return rel, slice(part * block, (part + 1) * block)

    return shards * feat // block, source, place


def outer_rows_kernel(block, shards, after_ref, *refs):
    stage, sems = refs[-2:]
    lefts, refs = refs[:shards], refs[shards:-2]
    half = len(refs) // 2
    rights, outs = refs[:half], refs[half:]
    steps, source, place = places(lefts[0].shape[1], shards, block)

    def fill(step, slot):
        rel, at = source(step)
        left = lefts[rel][:, at].astype(F32).T.astype(BF16)
        for i, right in enumerate(rights):
            stage[slot, i] = jnp.dot(left, right[...], preferred_element_type=F32).astype(BF16)

    def copies(step, slot):
        return [
            pltpu.make_async_copy(stage.at[slot, i], out.at[place(step)], sems.at[slot, i])
            for i, out in enumerate(outs)
        ]

    stream(steps, fill, copies)


def outer_rows(lefts, rights, after, block):
    rows, feat = lefts[0].shape
    tall = feat * len(lefts)
    narrow = rights[0].shape[1]
    count = len(rights)
    return pl.pallas_call(
        functools.partial(outer_rows_kernel, block, len(lefts)),
        out_shape=[jax.ShapeDtypeStruct((tall, narrow), BF16)] * count,
        in_specs=[pl.BlockSpec(memory_space=pl.ANY)] + [VMEM] * (len(lefts) + count),
        out_specs=[pl.BlockSpec(memory_space=pltpu.HBM)] * count,
        scratch_shapes=[
            pltpu.VMEM((SLOTS, count, block, narrow), BF16),
            pltpu.SemaphoreType.DMA((SLOTS, count)),
        ],
        cost_estimate=pl.CostEstimate(
            flops=2 * rows * tall * narrow * count,
            bytes_accessed=2 * tall * narrow * count,
            transcendentals=0,
        ),
        compiler_params=pltpu.CompilerParams(vmem_limit_bytes=2**24),
        name="outer_rows",
    )(pltpu.with_memory_space_constraint(after, pltpu.HBM), *[keep(a) for a in (*lefts, *rights)])


def middle_kernel(
    block, pieces, feat, me_ref, after_ref, left_ref, d_gate_ref, d_up_ref, cols_ref, gate_ref, up_ref, *refs
):
    outs, (turned, stage, sems) = refs[-4 - len(pieces):-3], refs[-3:]
    rights, out_ref, outs = refs[:-4 - len(pieces)], outs[0], outs[1:]
    turned[...] = left_ref[...].astype(F32).T.astype(BF16)
    steps, source, place = places(rights[0].shape[1], len(rights), block)

    def fill(step, slot):
        rel, at = source(step)
        stage[slot] = jnp.dot(turned[...], rights[rel][:, at], preferred_element_type=F32).astype(BF16)

    def copies(step, slot):
        return [pltpu.make_async_copy(stage.at[slot], out_ref.at[:, place(step)], sems.at[slot])]

    def term(piece, out):
        rel, low, high = piece
        out[:, :high - low] = term_piece(
            me_ref, rel, low, high, feat, d_gate_ref[...], d_up_ref[...], gate_ref, up_ref
        )
        if high == feat:
            out[:, high - low:] = cols_ref[...]

    stream(steps, fill, copies, [functools.partial(term, *pair) for pair in zip(pieces, outs)])


def middle(left, rights, after, block, pieces, me, d_gate, d_up, cols, gate_m, up_m, feat):
    rows = left.shape[0]
    wide = rights[0].shape[1] * len(rights)
    tall = left.shape[1]
    return pl.pallas_call(
        functools.partial(middle_kernel, block, pieces, feat),
        out_shape=[jax.ShapeDtypeStruct((tall, wide), BF16)]
        + [
            jax.ShapeDtypeStruct((rows, high - low + (LANES if high == feat else 0)), BF16)
            for rel, low, high in pieces
        ],
        in_specs=[SMEM, pl.BlockSpec(memory_space=pl.ANY)] + [VMEM] * (6 + len(rights)),
        out_specs=[pl.BlockSpec(memory_space=pltpu.HBM)] + [VMEM] * len(pieces),
        scratch_shapes=[
            pltpu.VMEM((tall, rows), BF16),
            pltpu.VMEM((SLOTS, tall, block), BF16),
            pltpu.SemaphoreType.DMA((SLOTS,)),
        ],
        cost_estimate=pl.CostEstimate(
            flops=4 * rows * wide * tall, bytes_accessed=2 * wide * tall, transcendentals=0
        ),
        compiler_params=pltpu.CompilerParams(vmem_limit_bytes=2**24),
        name="middle",
    )(me, keep(after), *[keep(a) for a in (left, d_gate, d_up, cols, gate_m, up_m, *rights)])


def settle_kernel(count, *refs):
    pieces, parts, out_ref = refs[:count], refs[count:-2], refs[-1]
    low = 0
    for piece in pieces:
        at = slice(low, low + piece.shape[1])
        total = piece[...].astype(F32)
        for ref in parts:
            total += ref[:, at].astype(F32)
        for i in range(out_ref.shape[0]):
            out_ref[i, :, at] = total[i * CAP:(i + 1) * CAP].astype(BF16)
        low += piece.shape[1]


def settle(pieces, parts, after):
    rows = pieces[0].shape[0]
    wide = sum(a.shape[1] for a in pieces)
    return pl.pallas_call(
        functools.partial(settle_kernel, len(pieces)),
        out_shape=jax.ShapeDtypeStruct((rows // CAP, CAP, wide), BF16),
        in_specs=[VMEM] * (len(pieces) + len(parts)) + [pl.BlockSpec(memory_space=pl.ANY)],
        out_specs=VMEM,
        cost_estimate=pl.CostEstimate(flops=0, bytes_accessed=10**6, transcendentals=0),
        name="settle",
    )(*[keep(a) for a in (*pieces, *parts)], pltpu.with_memory_space_constraint(after, pltpu.HBM))


def combine_kernel(feat, block, pick_ref, gates_ref, rows_ref, grad_hbm, gate_ref, stage, sems):
    pick = pick_ref[...]
    turned = pick.astype(F32).T.astype(BF16)
    copies = []
    for i, low in enumerate(range(0, feat, block)):
        at = slice(low, low + block)
        stage[:, at] = jnp.dot(turned, rows_ref[:, at], preferred_element_type=F32).astype(BF16)
        copies.append(pltpu.make_async_copy(stage.at[:, at], grad_hbm.at[:, at], sems.at[i]))
        copies[-1].start()
    rows, count = pick.shape
    experts = rows // CAP
    terms = pick.astype(F32) * rows_ref[:, feat:].astype(F32)
    low = row_owners(experts, count) < experts // 2
    for i, part in enumerate((jnp.where(low, terms, 0.0), jnp.where(low, 0.0, terms))):
        gate_ref[i:i + 1, :] = jnp.sum(part, axis=0, keepdims=True) / gates_ref[i:i + 1, :]
    for copy in copies:
        copy.wait()


def combine(pick, gates, rows, feat):
    count = pick.shape[1]
    block = 2 * LANES if feat % (2 * LANES) == 0 else feat
    return pl.pallas_call(
        functools.partial(combine_kernel, feat, block),
        out_shape=[
            jax.ShapeDtypeStruct((count, feat), BF16),
            jax.ShapeDtypeStruct((2, count), F32),
        ],
        in_specs=[VMEM] * 3,
        out_specs=[pl.BlockSpec(memory_space=pltpu.HBM), VMEM],
        scratch_shapes=[
            pltpu.VMEM((count, feat), BF16),
            pltpu.SemaphoreType.DMA((feat // block,)),
        ],
        cost_estimate=pl.CostEstimate(flops=10**8, bytes_accessed=10**6, transcendentals=0),
        compiler_params=pltpu.CompilerParams(vmem_limit_bytes=2**23),
        name="combine",
    )(*[keep(a) for a in (pick, gates, rows)])


def per_device(tokens, cotangent, gates, expert_ids, w_gate, w_up, w_down):
    experts = lax.axis_size("dp")
    shards = lax.axis_size("expert")
    me = lax.axis_index("expert")
    rows = experts * CAP
    feat = tokens.shape[1]
    ids_t = expert_ids.T
    gates_t = gates.T
    me_ref = me.reshape(1)
    slots, pick, gates_f = pack(ids_t, gates_t, tokens, cotangent, experts)
    slots = exchange(slots, "dp")
    x = gather_far(slots[:, :CAP].reshape(rows, feat), "expert")
    d = gather_far(slots[:, CAP:].reshape(rows, feat), "expert")
    weights = [w_gate[0], w_up[0], w_down[0]]
    if feat % LANES or shards < 4:
        x, d = gather_near(x, "expert"), gather_near(d, "expert")
        x = [jnp.concatenate(reorder(x, me), axis=1)]
        d = [jnp.concatenate(reorder(d, me), axis=1)]
        weights = load(slots, *weights)
        sums = early([0], me_ref * 0, x, d, weights)
        odd = []
    else:
        x[1], d[1] = swap(x[0], "expert", 1), swap(d[0], "expert", 1)
        weights, sums = load_early(x[0], d[0], weights, slots)
        even = list(range(2, shards, 2))
        odd = list(range(3, shards, 2))
        rest, sums = lax.optimization_barrier(([x[i] for i in even], sums))
        for i, x_i in zip(even, rest):
            x[i], x[i + 1] = x_i, swap(x_i, "expert", 1)
        rels = [1] + even
        more = partial(partial_x_kernel, 2, rels, me_ref, sums[0], [x[1]] + rest, weights)
        rest, more = lax.optimization_barrier(([d[i] for i in even], more))
        for i, d_i in zip(even, rest):
            d[i], d[i + 1] = d_i, swap(d_i, "expert", 1)
        more = [*more, *partial(partial_d_kernel, 1, rels, me_ref, more[0], [d[1]] + rest, weights)]
        x, d = [x[i] for i in range(shards)], [d[i] for i in range(shards)]
        sums = [*sums, *more]
    hidden, d_gate, d_up, cols, *sent = late(
        odd, me_ref, [x[i] for i in odd], [d[i] for i in odd], weights, sums, feat
    )

    def term(pieces, after):
        return terms(pieces, me_ref, after, d_gate, d_up, cols, *weights[:2], feat) if pieces else []

    start = (keep(cols), keep(cols))
    if not odd:
        sent = term([(rel, 0, feat) for rel in range(3, shards, 2)], start)
    arrived = [swap(part, "expert", 1) for part in sent]
    even = list(range(2, shards, 2))
    kept = term([(rel, 0, feat) for rel in even], start)
    held = {rel: add(part, more) for rel, part, more in zip(even, kept, arrived)}
    last = held[max(held)] if held else cols
    wide = feat * shards
    other = sum_far(held, "expert")
    half = max(LANES, (feat - LANES) // LANES * LANES)
    pieces = ([(1, 0, feat)] if shards > 1 else []) + [(0, 0, half)]
    grad_down, *sent, first = middle(
        hidden, d, last, wide // 8, pieces, me_ref, d_gate, d_up, cols, *weights[:2], feat
    )
    down_done = pltpu.with_memory_space_constraint(grad_down, pltpu.HBM)
    parts = [swap(part, "expert", 1) for part in sent]
    parts += [] if other is None else [other]
    second, = term([(0, half, feat)], (keep(parts[-1] if parts else cols), down_done))
    total = settle([first, second], parts, grad_down)
    got = exchange(total, "dp")
    got = got.reshape(rows, feat + LANES)
    grad_gate, grad_up = outer_rows(x, (d_gate, d_up), total, wide // 16)
    grad_tokens, gate_grads = combine(pick, gates_f, got, feat)
    return (grad_tokens, gate_grads.T, grad_gate[None], grad_up[None], grad_down[None])


def solution(mesh):
    in_specs = (
        P("dp", "expert"),
        P("dp", "expert"),
        P("dp", None),
        P("dp", None),
        P("dp", None, "expert"),
        P("dp", None, "expert"),
        P("dp", "expert", None),
    )
    out_specs = (
        P("dp", "expert"),
        P("dp", None),
        P("dp", None, "expert"),
        P("dp", None, "expert"),
        P("dp", "expert", None),
    )
    return jax.shard_map(
        per_device, mesh=mesh, in_specs=in_specs, out_specs=out_specs, check_vma=False
    )
```

```python
import functools
import math

import jax
import jax.numpy as jnp
from jax import lax
from jax.experimental import pallas as pl
from jax.experimental.pallas import tpu as pltpu
from jax.sharding import PartitionSpec as P

CAP = 8
LANES = 128
F32 = jnp.float32
BF16 = jnp.bfloat16
VMEM = pl.BlockSpec(memory_space=pltpu.VMEM)
SMEM = pl.BlockSpec(memory_space=pltpu.SMEM)


def keep(array):
    return pltpu.with_memory_space_constraint(array, pltpu.VMEM)


def swap(value, axis, mask):
    size = lax.axis_size(axis)
    return lax.ppermute(value, axis, [(i, i ^ mask) for i in range(size)])


def reorder(shards, me):
    size = len(shards)
    mask = 1
    while mask < size:
        flip = (me & mask) != 0
        shards = [jnp.where(flip, shards[i ^ mask], shards[i]) for i in range(size)]
        mask *= 2
    return shards


def gather_far(own, axis):
    size = lax.axis_size(axis)
    held = {0: own}
    mask = size // 2
    while mask > 1:
        for rel in list(held):
            held[rel ^ mask] = swap(held[rel], axis, mask)
        mask //= 2
    return held


def gather_near(held, axis):
    size = lax.axis_size(axis)
    if size > 1:
        held = {**held, **{rel ^ 1: swap(held[rel], axis, 1) for rel in held}}
    return [held[i] for i in range(size)]


def gather_shards(own, axis):
    return gather_near(gather_far(own, axis), axis)


def add(held, arrived):
    return (held.astype(F32) + arrived.astype(F32)).astype(BF16)


def sum_far(held, axis):
    size = lax.axis_size(axis)
    total = None
    mask = 2
    while mask < size:
        arrived = {rel ^ mask: swap(held.pop(rel), axis, mask) for rel in list(held) if rel & mask}
        for rel, value in arrived.items():
            if rel:
                held[rel] = add(held[rel], value)
            else:
                total = value if total is None else add(total, value)
        mask *= 2
    return total


def one_hot(ids, gates, expert, experts):
    rows, tokens = expert.shape
    row = lax.broadcasted_iota(jnp.int32, (rows, tokens), 0)
    low = expert < experts // 2
    member = jnp.where(low, ids[0:1, :], ids[1:2, :]) == expert
    gate = jnp.where(low, gates[0:1, :], gates[1:2, :])
    earlier = lax.broadcasted_iota(jnp.int32, (tokens, tokens), 0) < lax.broadcasted_iota(
        jnp.int32, (tokens, tokens), 1
    )
    before = jnp.dot(
        member.astype(F32).astype(BF16), earlier.astype(F32).astype(BF16), preferred_element_type=F32
    )
    pick = jnp.logical_and(member, before == (row & (CAP - 1)).astype(F32))
    return jnp.where(pick, 1.0, 0.0), jnp.where(pick, gate, 0.0)


def owner_order(experts):
    places = experts // 2
    near = sorted(range(places), key=lambda place: (abs(2 * place - places + 1), -place))
    return [2 * place + last for place in near for last in (1, 0)]


def row_owners(experts, tokens):
    block = lax.broadcasted_iota(jnp.int32, (experts * CAP, tokens), 0) // CAP
    owner = jnp.zeros_like(block)
    for i, expert in enumerate(owner_order(experts)):
        owner = jnp.where(block == i, expert, owner)
    return owner


def exchange(blocks, axis):
    groups = [owner_order(lax.axis_size(axis))]
    return lax.all_to_all(
        blocks, axis, split_axis=0, concat_axis=0, axis_index_groups=groups, tiled=True
    )


def column_block(feat):
    return feat // 2 if feat % (2 * LANES) == 0 else feat


def pack_kernel(
    experts, block, ids_hbm, gates_hbm, x_hbm, d_hbm, slot_hbm, pick_out, gates_out, ids, gates_low, x_ref, d_ref, slots, sems
):
    feat = x_ref.shape[1]
    steps = feat // block

    def columns(step):
        return slice(step * block, (step + 1) * block)

    small = [
        pltpu.make_async_copy(ids_hbm, ids, sems.at[3, 0]),
        pltpu.make_async_copy(gates_hbm, gates_low, sems.at[4, 0]),
    ]
    loads = [
        [
            pltpu.make_async_copy(src.at[:, columns(step)], dst.at[:, columns(step)], sems.at[i, step])
            for i, (src, dst) in enumerate(((x_hbm, x_ref), (d_hbm, d_ref)))
        ]
        for step in range(steps)
    ]
    stores = [
        pltpu.make_async_copy(
            slots.at[:, :, columns(step)], slot_hbm.at[:, :, columns(step)], sems.at[2, step]
        )
        for step in range(steps)
    ]
    for copy in small + [copy for pair in loads for copy in pair]:
        copy.start()
    for copy in small:
        copy.wait()
    gates = gates_low[...].astype(F32)
    pick, pick_gate = one_hot(ids[...], gates, row_owners(experts, ids.shape[1]), experts)
    pick, pick_gate = pick.astype(BF16), pick_gate.astype(BF16)
    for step in range(steps):
        for copy in loads[step]:
            copy.wait()
        slot_x = jnp.dot(pick, x_ref[:, columns(step)], preferred_element_type=F32)
        slot_d = jnp.dot(pick_gate, d_ref[:, columns(step)], preferred_element_type=F32)
        for i in range(experts):
            slots[i, :, columns(step)] = jnp.concatenate(
                [slot_x[i * CAP:(i + 1) * CAP], slot_d[i * CAP:(i + 1) * CAP]], axis=0
            ).astype(BF16)
        stores[step].start()
    pick_out[...] = pick
    gates_out[...] = gates
    for copy in stores:
        copy.wait()


def pack(ids, gates, tokens, cotangent, experts):
    count, feat = tokens.shape
    block = column_block(feat)
    steps = feat // block
    rows = experts * CAP
    hbm = pl.BlockSpec(memory_space=pltpu.HBM)
    return pl.pallas_call(
        functools.partial(pack_kernel, experts, block),
        out_shape=[
            jax.ShapeDtypeStruct((experts, 2 * CAP, feat), BF16),
            jax.ShapeDtypeStruct((rows, count), BF16),
            jax.ShapeDtypeStruct((2, count), F32),
        ],
        in_specs=[hbm] * 4,
        out_specs=[hbm, VMEM, VMEM],
        scratch_shapes=[
            pltpu.VMEM((2, count), jnp.int32),
            pltpu.VMEM((2, count), BF16),
            pltpu.VMEM((count, feat), BF16),
            pltpu.VMEM((count, feat), BF16),
            pltpu.VMEM((experts, 2 * CAP, feat), BF16),
            pltpu.SemaphoreType.DMA((5, steps)),
        ],
        cost_estimate=pl.CostEstimate(flops=10**8, bytes_accessed=2 * 10**6, transcendentals=0),
        compiler_params=pltpu.CompilerParams(vmem_limit_bytes=2**23),
        name="pack",
    )(*[pltpu.with_memory_space_constraint(a, pltpu.HBM) for a in (ids, gates, tokens, cotangent)])


def load_kernel(count, *refs):
    sems = refs[-1]
    copies = [
        pltpu.make_async_copy(refs[i], refs[count + 1 + i], sems.at[i]) for i in range(count)
    ]
    for copy in copies:
        copy.start()
    for copy in copies:
        copy.wait()


def load(after, *arrays):
    count = len(arrays)
    total = sum(a.size * a.dtype.itemsize for a in arrays)
    return pl.pallas_call(
        functools.partial(load_kernel, count),
        out_shape=[pltpu.VMEM(a.shape, a.dtype) for a in arrays],
        in_specs=[pl.BlockSpec(memory_space=pltpu.HBM)] * count + [pl.BlockSpec(memory_space=pl.ANY)],
        out_specs=[VMEM] * count,
        scratch_shapes=[pltpu.SemaphoreType.DMA((count,))],
        cost_estimate=pl.CostEstimate(flops=0, bytes_accessed=total, transcendentals=0),
        compiler_params=pltpu.CompilerParams(vmem_limit_bytes=2**22),
        name="load",
    )(*[pltpu.with_memory_space_constraint(a, pltpu.HBM) for a in arrays], after)


def shard_at(me_ref, rel, feat):
    return pl.ds(pl.multiple_of((me_ref[0] ^ rel) * feat, feat), feat)


def products(rels, me_ref, x_refs, d_refs, gate_ref, up_ref, down_ref):
    feat = x_refs[0].shape[1]
    totals = None
    for rel, x_ref, d_ref in zip(rels, x_refs, d_refs):
        at = shard_at(me_ref, rel, feat)
        parts = (
            jnp.dot(x_ref[...], gate_ref[at, :], preferred_element_type=F32),
            jnp.dot(x_ref[...], up_ref[at, :], preferred_element_type=F32),
            lax.dot_general(
                d_ref[...], down_ref[:, at], (((1,), (1,)), ((), ())), preferred_element_type=F32
            ),
        )
        totals = parts if totals is None else tuple(a + b for a, b in zip(totals, parts))
    return totals


def early_kernel(rels, me_ref, *refs):
    count = len(rels)
    x_refs, d_refs, (gate_ref, up_ref, down_ref) = refs[:count], refs[count:2 * count], refs[2 * count:-3]
    totals = products(rels, me_ref, x_refs, d_refs, gate_ref, up_ref, down_ref)
    for out, value in zip(refs[-3:], totals):
        out[...] = value


def early(rels, me, x, d, weights):
    rows, units = x[0].shape[0], weights[0].shape[1]
    work = 6 * rows * units * x[0].shape[1] * len(rels)
    return pl.pallas_call(
        functools.partial(early_kernel, rels),
        out_shape=[jax.ShapeDtypeStruct((rows, units), F32)] * 3,
        in_specs=[SMEM] + [VMEM] * (2 * len(rels) + 3),
        out_specs=[VMEM] * 3,
        cost_estimate=pl.CostEstimate(flops=work, bytes_accessed=work // rows, transcendentals=0),
        compiler_params=pltpu.CompilerParams(vmem_limit_bytes=2**24),
        name="early",
    )(me, *[keep(a) for a in (*x, *d, *weights)])


def partial_x_kernel(rels, me_ref, after_ref, gate_ref, up_ref, down_ref, *refs):
    x_refs, outs = refs[:-2], refs[-2:]
    feat = x_refs[0].shape[1]
    for weight_ref, out in zip((gate_ref, up_ref), outs):
        total = None
        for rel, x_ref in zip(rels, x_refs):
            part = jnp.dot(
                x_ref[...], weight_ref[shard_at(me_ref, rel, feat), :], preferred_element_type=F32
            )
            total = part if total is None else total + part
        out[...] = total


def partial_d_kernel(rels, me_ref, after_ref, gate_ref, up_ref, down_ref, *refs):
    d_refs, out = refs[:-1], refs[-1]
    feat = d_refs[0].shape[1]
    total = None
    for rel, d_ref in zip(rels, d_refs):
        part = lax.dot_general(
            d_ref[...],
            down_ref[:, shard_at(me_ref, rel, feat)],
            (((1,), (1,)), ((), ())),
            preferred_element_type=F32,
        )
        total = part if total is None else total + part
    out[...] = total


def partial(kernel, count, rels, me, after, arrays, weights):
    rows, units = arrays[0].shape[0], weights[0].shape[1]
    work = 2 * count * rows * units * arrays[0].shape[1] * len(rels)
    return pl.pallas_call(
        functools.partial(kernel, rels),
        out_shape=[jax.ShapeDtypeStruct((rows, units), F32)] * count,
        in_specs=[SMEM, pl.BlockSpec(memory_space=pl.ANY)] + [VMEM] * (3 + len(rels)),
        out_specs=[VMEM] * count,
        cost_estimate=pl.CostEstimate(flops=work, bytes_accessed=work // rows, transcendentals=0),
        compiler_params=pltpu.CompilerParams(vmem_limit_bytes=2**24),
        name="partial",
    )(me, keep(after), *[keep(a) for a in (*weights, *arrays)])


def flip(index, rel):
    mask = 1
    while mask <= rel:
        if rel & mask:
            index = index + mask * (1 - 2 * ((index // mask) % 2))
        mask *= 2
    return index


def load_early_kernel(x0, d0, gate_in, up_in, down_in, gate, up, down, *refs):
    sums, sems = refs[:3], refs[3]
    feat = x0.shape[1]
    me = lax.axis_index("expert")
    shards = gate.shape[0] // feat

    def place(rel):
        return pl.ds(pl.multiple_of(flip(me, rel) * feat, feat), feat)

    def copies(rel):
        at = place(rel)
        return [
            pltpu.make_async_copy(src.at[at], dst.at[at], sems.at[i, rel])
            for i, (src, dst) in enumerate(((gate_in, gate), (up_in, up)))
        ]

    height = down.shape[0] // shards
    downs = [
        pltpu.make_async_copy(
            down_in.at[i * height:(i + 1) * height], down.at[i * height:(i + 1) * height], sems.at[2, i]
        )
        for i in range(shards)
    ]
    first, *rest = [copies(rel) for rel in range(shards)]
    for group in [first, downs] + rest:
        for copy in group:
            copy.start()
    at = place(0)
    for copy, weight, out in zip(first, (gate, up), sums[:2]):
        copy.wait()
        out[...] = jnp.dot(x0[...], weight[at, :], preferred_element_type=F32)
    for copy in downs:
        copy.wait()
    sums[2][...] = lax.dot_general(
        d0[...], down[:, at], (((1,), (1,)), ((), ())), preferred_element_type=F32
    )
    for group in rest:
        for copy in group:
            copy.wait()


def load_early(x, d, weights, after):
    rows = x.shape[0]
    units = weights[0].shape[1]
    shards = lax.axis_size("expert")
    out = pl.pallas_call(
        lambda after_ref, *refs: load_early_kernel(*refs),
        out_shape=[pltpu.VMEM(a.shape, a.dtype) for a in weights]
        + [jax.ShapeDtypeStruct((rows, units), F32)] * 3,
        in_specs=[pl.BlockSpec(memory_space=pl.ANY)]
        + [VMEM] * 2
        + [pl.BlockSpec(memory_space=pltpu.HBM)] * 3,
        out_specs=[VMEM] * 6,
        scratch_shapes=[pltpu.SemaphoreType.DMA((3, shards))],
        cost_estimate=pl.CostEstimate(
            flops=6 * rows * units * x.shape[1],
            bytes_accessed=sum(a.size * 2 for a in weights),
            transcendentals=0,
        ),
        compiler_params=pltpu.CompilerParams(vmem_limit_bytes=2**23),
        name="load_early",
    )(
        keep(after),
        keep(x),
        keep(d),
        *[pltpu.with_memory_space_constraint(a, pltpu.HBM) for a in weights],
    )
    return out[:3], out[3:]


def late_kernel(rels, feat, me_ref, *refs):
    count = len(rels)
    x_refs, d_refs, refs = refs[:count], refs[count:2 * count], refs[2 * count:]
    refs, outs = refs[:-4 - count], refs[-4 - count:]
    (gate_ref, up_ref, down_ref), sum_refs = refs[:3], refs[3:]
    hidden_out, d_gate_out, d_up_out, cols_out = outs[:4]
    totals = [ref[...] for ref in sum_refs[:3]]
    for i, ref in enumerate(sum_refs[3:]):
        totals[i % 3] += ref[...]
    if rels:
        parts = products(rels, me_ref, x_refs, d_refs, gate_ref, up_ref, down_ref)
        totals = [a + b for a, b in zip(totals, parts)]
    pre_gate, pre_up, dhid = totals
    sig = 1.0 / (1.0 + jnp.exp(-pre_gate))
    act = pre_gate * sig
    hidden = (act * pre_up).astype(BF16)
    d_gate = (dhid * pre_up * sig * (1.0 + pre_gate * (1.0 - sig))).astype(BF16)
    d_up = (dhid * act).astype(BF16)
    total = jnp.sum(dhid * hidden.astype(F32), axis=1, keepdims=True)
    cols = jnp.broadcast_to(total, cols_out.shape).astype(BF16)
    for rel, out in zip(rels, outs[4:]):
        out[:, :feat] = term_piece(me_ref, rel, 0, feat, feat, d_gate, d_up, gate_ref, up_ref)
        out[:, feat:] = cols
    hidden_out[...] = hidden
    d_gate_out[...] = d_gate
    d_up_out[...] = d_up
    cols_out[...] = cols


def late(rels, me, x, d, weights, sums, feat):
    rows, units = sums[0].shape
    work = 10 * rows * units * feat * max(1, len(rels))
    return pl.pallas_call(
        functools.partial(late_kernel, rels, feat),
        out_shape=[jax.ShapeDtypeStruct((rows, units), BF16)] * 3
        + [jax.ShapeDtypeStruct((rows, LANES), BF16)]
        + [jax.ShapeDtypeStruct((rows, feat + LANES), BF16)] * len(rels),
        in_specs=[SMEM] + [VMEM] * (2 * len(rels) + 3 + len(sums)),
        out_specs=[VMEM] * (4 + len(rels)),
        cost_estimate=pl.CostEstimate(
            flops=work, bytes_accessed=work // rows, transcendentals=rows * units
        ),
        compiler_params=pltpu.CompilerParams(vmem_limit_bytes=2**24),
        name="late",
    )(me, *[keep(a) for a in (*x, *d, *weights, *sums)])


def term_piece(me_ref, rel, low, high, feat, d_gate, d_up, gate_ref, up_ref):
    dims = (((1,), (1,)), ((), ()))
    start = (me_ref[0] ^ rel) * feat + low
    at = pl.ds(pl.multiple_of(start, math.gcd(feat, low)), high - low)
    term = lax.dot_general(d_gate, gate_ref[at, :], dims, preferred_element_type=F32)
    term += lax.dot_general(d_up, up_ref[at, :], dims, preferred_element_type=F32)
    return term.astype(BF16)


def term_kernel(pieces, feat, me_ref, after_ref, last_ref, d_gate_ref, d_up_ref, cols_ref, gate_ref, up_ref, *outs):
    for (rel, low, high), out in zip(pieces, outs):
        out[:, :high - low] = term_piece(
            me_ref, rel, low, high, feat, d_gate_ref[...], d_up_ref[...], gate_ref, up_ref
        )
        if high == feat:
            out[:, high - low:] = cols_ref[...]


def terms(pieces, me, after, d_gate, d_up, cols, gate_m, up_m, feat):
    rows = d_gate.shape[0]
    return pl.pallas_call(
        functools.partial(term_kernel, pieces, feat),
        out_shape=[
            jax.ShapeDtypeStruct((rows, high - low + (LANES if high == feat else 0)), BF16)
            for rel, low, high in pieces
        ],
        in_specs=[SMEM] + [pl.BlockSpec(memory_space=pl.ANY)] * 2 + [VMEM] * 5,
        out_specs=[VMEM] * len(pieces),
        cost_estimate=pl.CostEstimate(flops=1, bytes_accessed=1, transcendentals=0),
        compiler_params=pltpu.CompilerParams(vmem_limit_bytes=2**24),
        name="terms",
    )(me, *after, *[keep(a) for a in (d_gate, d_up, cols, gate_m, up_m)])


SLOTS = 4


def stream(steps, fill, copies, beside=()):
    beside = list(beside)
    for step in range(steps + SLOTS):
        if step >= SLOTS:
            for copy in copies(step - SLOTS, step % SLOTS):
                copy.wait()
        if step < steps:
            fill(step, step % SLOTS)
            for copy in copies(step, step % SLOTS):
                copy.start()
            if steps - step <= len(beside):
                beside[step - steps]()


def places(feat, shards, block):
    me = lax.axis_index("expert") if shards > 1 else 0

    def place(step):
        rel, part = divmod(step, feat // block)
        start = flip(me, rel) * feat + part * block
        return pl.ds(pl.multiple_of(start, block) if shards > 1 else start, block)

    def source(step):
        rel, part = divmod(step, feat // block)
        return rel, slice(part * block, (part + 1) * block)

    return shards * feat // block, source, place


def outer_rows_kernel(block, shards, after_ref, *refs):
    stage, sems = refs[-2:]
    lefts, refs = refs[:shards], refs[shards:-2]
    half = len(refs) // 2
    rights, outs = refs[:half], refs[half:]
    steps, source, place = places(lefts[0].shape[1], shards, block)

    def fill(step, slot):
        rel, at = source(step)
        left = lefts[rel][:, at].astype(F32).T.astype(BF16)
        for i, right in enumerate(rights):
            stage[slot, i] = jnp.dot(left, right[...], preferred_element_type=F32).astype(BF16)

    def copies(step, slot):
        return [
            pltpu.make_async_copy(stage.at[slot, i], out.at[place(step)], sems.at[slot, i])
            for i, out in enumerate(outs)
        ]

    stream(steps, fill, copies)


def outer_rows(lefts, rights, after, block):
    rows, feat = lefts[0].shape
    tall = feat * len(lefts)
    narrow = rights[0].shape[1]
    count = len(rights)
    return pl.pallas_call(
        functools.partial(outer_rows_kernel, block, len(lefts)),
        out_shape=[jax.ShapeDtypeStruct((tall, narrow), BF16)] * count,
        in_specs=[pl.BlockSpec(memory_space=pl.ANY)] + [VMEM] * (len(lefts) + count),
        out_specs=[pl.BlockSpec(memory_space=pltpu.HBM)] * count,
        scratch_shapes=[
            pltpu.VMEM((SLOTS, count, block, narrow), BF16),
            pltpu.SemaphoreType.DMA((SLOTS, count)),
        ],
        cost_estimate=pl.CostEstimate(
            flops=2 * rows * tall * narrow * count,
            bytes_accessed=2 * tall * narrow * count,
            transcendentals=0,
        ),
        compiler_params=pltpu.CompilerParams(vmem_limit_bytes=2**24),
        name="outer_rows",
    )(pltpu.with_memory_space_constraint(after, pltpu.HBM), *[keep(a) for a in (*lefts, *rights)])


def middle_kernel(
    block, pieces, feat, me_ref, after_ref, left_ref, d_gate_ref, d_up_ref, cols_ref, gate_ref, up_ref, *refs
):
    outs, (turned, stage, sems) = refs[-4 - len(pieces):-3], refs[-3:]
    rights, out_ref, outs = refs[:-4 - len(pieces)], outs[0], outs[1:]
    turned[...] = left_ref[...].astype(F32).T.astype(BF16)
    steps, source, place = places(rights[0].shape[1], len(rights), block)

    def fill(step, slot):
        rel, at = source(step)
        stage[slot] = jnp.dot(turned[...], rights[rel][:, at], preferred_element_type=F32).astype(BF16)

    def copies(step, slot):
        return [pltpu.make_async_copy(stage.at[slot], out_ref.at[:, place(step)], sems.at[slot])]

    def term(piece, out):
        rel, low, high = piece
        out[:, :high - low] = term_piece(
            me_ref, rel, low, high, feat, d_gate_ref[...], d_up_ref[...], gate_ref, up_ref
        )
        if high == feat:
            out[:, high - low:] = cols_ref[...]

    stream(steps, fill, copies, [functools.partial(term, *pair) for pair in zip(pieces, outs)])


def middle(left, rights, after, block, pieces, me, d_gate, d_up, cols, gate_m, up_m, feat):
    rows = left.shape[0]
    wide = rights[0].shape[1] * len(rights)
    tall = left.shape[1]
    return pl.pallas_call(
        functools.partial(middle_kernel, block, pieces, feat),
        out_shape=[jax.ShapeDtypeStruct((tall, wide), BF16)]
        + [
            jax.ShapeDtypeStruct((rows, high - low + (LANES if high == feat else 0)), BF16)
            for rel, low, high in pieces
        ],
        in_specs=[SMEM, pl.BlockSpec(memory_space=pl.ANY)] + [VMEM] * (6 + len(rights)),
        out_specs=[pl.BlockSpec(memory_space=pltpu.HBM)] + [VMEM] * len(pieces),
        scratch_shapes=[
            pltpu.VMEM((tall, rows), BF16),
            pltpu.VMEM((SLOTS, tall, block), BF16),
            pltpu.SemaphoreType.DMA((SLOTS,)),
        ],
        cost_estimate=pl.CostEstimate(
            flops=4 * rows * wide * tall, bytes_accessed=2 * wide * tall, transcendentals=0
        ),
        compiler_params=pltpu.CompilerParams(vmem_limit_bytes=2**24),
        name="middle",
    )(me, keep(after), *[keep(a) for a in (left, d_gate, d_up, cols, gate_m, up_m, *rights)])


def settle_kernel(count, *refs):
    pieces, parts, out_ref = refs[:count], refs[count:-2], refs[-1]
    low = 0
    for piece in pieces:
        at = slice(low, low + piece.shape[1])
        total = piece[...].astype(F32)
        for ref in parts:
            total += ref[:, at].astype(F32)
        for i in range(out_ref.shape[0]):
            out_ref[i, :, at] = total[i * CAP:(i + 1) * CAP].astype(BF16)
        low += piece.shape[1]


def settle(pieces, parts, after):
    rows = pieces[0].shape[0]
    wide = sum(a.shape[1] for a in pieces)
    return pl.pallas_call(
        functools.partial(settle_kernel, len(pieces)),
        out_shape=jax.ShapeDtypeStruct((rows // CAP, CAP, wide), BF16),
        in_specs=[VMEM] * (len(pieces) + len(parts)) + [pl.BlockSpec(memory_space=pl.ANY)],
        out_specs=VMEM,
        cost_estimate=pl.CostEstimate(flops=0, bytes_accessed=10**6, transcendentals=0),
        name="settle",
    )(*[keep(a) for a in (*pieces, *parts)], pltpu.with_memory_space_constraint(after, pltpu.HBM))


def combine_kernel(feat, block, pick_ref, gates_ref, rows_ref, grad_ref, gate_ref):
    pick = pick_ref[...]
    at = pl.ds(pl.multiple_of(pl.program_id(0) * block, block), block) if block < feat else slice(0, feat)
    grad_ref[...] = lax.dot_general(
        pick, rows_ref[:, at], (((0,), (0,)), ((), ())), preferred_element_type=F32
    ).astype(BF16)

    @pl.when(pl.program_id(0) == 0)
    def _():
        rows, count = pick.shape
        experts = rows // CAP
        terms = pick.astype(F32) * rows_ref[:, feat:].astype(F32)
        low = row_owners(experts, count) < experts // 2
        for i, part in enumerate((jnp.where(low, terms, 0.0), jnp.where(low, 0.0, terms))):
            gate_ref[i:i + 1, :] = jnp.sum(part, axis=0, keepdims=True) / gates_ref[i:i + 1, :]


def combine(pick, gates, rows, feat):
    count = pick.shape[1]
    block = column_block(feat)
    return pl.pallas_call(
        functools.partial(combine_kernel, feat, block),
        grid=(feat // block,),
        out_shape=[
            jax.ShapeDtypeStruct((count, feat), BF16),
            jax.ShapeDtypeStruct((2, count), F32),
        ],
        in_specs=[VMEM] * 3,
        out_specs=[
            pl.BlockSpec((count, block), lambda i: (0, i)),
            pl.BlockSpec((2, count), lambda i: (0, 0)),
        ],
        cost_estimate=pl.CostEstimate(flops=10**8, bytes_accessed=10**6, transcendentals=0),
        name="combine",
    )(*[keep(a) for a in (pick, gates, rows)])


def per_device(tokens, cotangent, gates, expert_ids, w_gate, w_up, w_down):
    experts = lax.axis_size("dp")
    shards = lax.axis_size("expert")
    me = lax.axis_index("expert")
    rows = experts * CAP
    feat = tokens.shape[1]
    ids_t = expert_ids.T
    gates_t = gates.T
    me_ref = me.reshape(1)
    slots, pick, gates_f = pack(ids_t, gates_t, tokens, cotangent, experts)
    slots = exchange(slots, "dp")
    x = gather_far(slots[:, :CAP].reshape(rows, feat), "expert")
    d = gather_far(slots[:, CAP:].reshape(rows, feat), "expert")
    weights = [w_gate[0], w_up[0], w_down[0]]
    if feat % LANES or shards < 4:
        x, d = gather_near(x, "expert"), gather_near(d, "expert")
        x = [jnp.concatenate(reorder(x, me), axis=1)]
        d = [jnp.concatenate(reorder(d, me), axis=1)]
        weights = load(slots, *weights)
        sums = early([0], me_ref * 0, x, d, weights)
        odd = []
    else:
        x[1], d[1] = swap(x[0], "expert", 1), swap(d[0], "expert", 1)
        weights, sums = load_early(x[0], d[0], weights, slots)
        even = list(range(2, shards, 2))
        odd = list(range(3, shards, 2))
        rest, sums = lax.optimization_barrier(([x[i] for i in even], sums))
        for i, x_i in zip(even, rest):
            x[i], x[i + 1] = x_i, swap(x_i, "expert", 1)
        rels = [1] + even
        more = partial(partial_x_kernel, 2, rels, me_ref, sums[0], [x[1]] + rest, weights)
        rest, more = lax.optimization_barrier(([d[i] for i in even], more))
        for i, d_i in zip(even, rest):
            d[i], d[i + 1] = d_i, swap(d_i, "expert", 1)
        more = [*more, *partial(partial_d_kernel, 1, rels, me_ref, more[0], [d[1]] + rest, weights)]
        x, d = [x[i] for i in range(shards)], [d[i] for i in range(shards)]
        sums = [*sums, *more]
    hidden, d_gate, d_up, cols, *sent = late(
        odd, me_ref, [x[i] for i in odd], [d[i] for i in odd], weights, sums, feat
    )

    def term(pieces, after):
        return terms(pieces, me_ref, after, d_gate, d_up, cols, *weights[:2], feat) if pieces else []

    start = (keep(cols), keep(cols))
    if not odd:
        sent = term([(rel, 0, feat) for rel in range(3, shards, 2)], start)
    arrived = [swap(part, "expert", 1) for part in sent]
    even = list(range(2, shards, 2))
    kept = term([(rel, 0, feat) for rel in even], start)
    held = {rel: add(part, more) for rel, part, more in zip(even, kept, arrived)}
    last = held[max(held)] if held else cols
    wide = feat * shards
    other = sum_far(held, "expert")
    half = max(LANES, (feat - 2 * LANES) // LANES * LANES)
    pieces = ([(1, 0, feat)] if shards > 1 else []) + [(0, 0, half)]
    grad_down, *sent, first = middle(
        hidden, d, last, wide // 8, pieces, me_ref, d_gate, d_up, cols, *weights[:2], feat
    )
    down_done = pltpu.with_memory_space_constraint(grad_down, pltpu.HBM)
    parts = [swap(part, "expert", 1) for part in sent]
    parts += [] if other is None else [other]
    second, = term([(0, half, feat)], (keep(parts[-1] if parts else cols), down_done))
    total = settle([first, second], parts, grad_down)
    got = exchange(total, "dp")
    got = got.reshape(rows, feat + LANES)
    grad_gate, grad_up = outer_rows(x, (d_gate, d_up), total, wide // 16)
    grad_tokens, gate_grads = combine(pick, gates_f, got, feat)
    return (grad_tokens, gate_grads.T, grad_gate[None], grad_up[None], grad_down[None])


def solution(mesh):
    in_specs = (
        P("dp", "expert"),
        P("dp", "expert"),
        P("dp", None),
        P("dp", None),
        P("dp", None, "expert"),
        P("dp", None, "expert"),
        P("dp", "expert", None),
    )
    out_specs = (
        P("dp", "expert"),
        P("dp", None),
        P("dp", None, "expert"),
        P("dp", None, "expert"),
        P("dp", "expert", None),
    )
    return jax.shard_map(
        per_device, mesh=mesh, in_specs=in_specs, out_specs=out_specs, check_vma=False
    )
```
